32 devices in a mesh: dp: 8 (over z, x), tensor: 4 (over y, core).
Axes of the slice: x: 2, y: 2, z: 4, core: 2. Of those that a mesh axis runs over, the one named last changes fastest.
Arguments:
- hidden_in: bfloat16 [8192, 2048], P('dp'), may hold values from -6 to 6
- out_cotangent: bfloat16 [8192, 2048], P('dp'), may hold values from -6 to 6
- episode_lengths: int32 [8, 8], P('dp'), may hold values from 1 to 512, 1024 in all within a row
- self_generated: int32 [8192], P('dp'), may hold values 0 or 1
- loss_numerator: int32 [8192], P('dp'), may hold values from 1 to 8
- attend_weights: float32 [2048, 3, 2048], P('dp', None, 'tensor'), may hold values from -0.125 to 0.125
- attend_first: float32 [2048, 3, 2048], P('dp', None, 'tensor'), may hold values from -512 to 512
- attend_second: float32 [2048, 3, 2048], P('dp', None, 'tensor'), may hold values from 4096 to 65536
- attend_average: float32 [2048, 3, 2048], P('dp', None, 'tensor'), may hold values from -0.125 to 0.125
- combine_weights: float32 [2048, 2048], P('tensor', 'dp'), may hold values from -1 to 1
- combine_first: float32 [2048, 2048], P('tensor', 'dp'), may hold values from -80 to 80
- combine_second: float32 [2048, 2048], P('tensor', 'dp'), may hold values from 96 to 1600
- combine_average: float32 [2048, 2048], P('tensor', 'dp'), may hold values from -1 to 1
- expand_weights: float32 [2048, 8192], P('dp', 'tensor'), may hold values from -0.125 to 0.125
- expand_first: float32 [2048, 8192], P('dp', 'tensor'), may hold values from -128 to 128
- expand_second: float32 [2048, 8192], P('dp', 'tensor'), may hold values from 245.76 to 4096
- expand_average: float32 [2048, 8192], P('dp', 'tensor'), may hold values from -0.125 to 0.125
- shrink_weights: float32 [8192, 2048], P('tensor', 'dp'), may hold values from -0.0625 to 0.0625
- shrink_first: float32 [8192, 2048], P('tensor', 'dp'), may hold values from -256 to 256
- shrink_second: float32 [8192, 2048], P('tensor', 'dp'), may hold values from 983.04 to 16384
- shrink_average: float32 [8192, 2048], P('tensor', 'dp'), may hold values from -0.0625 to 0.0625
- layernorm_params: float32 [4, 2048], P(None, 'dp'), may hold values from -1 to 1.3, as said below
- layernorm_first: float32 [4, 2048], P(None, 'dp'), may hold values from -384 to 384
- layernorm_second: float32 [4, 2048], P(None, 'dp'), may hold values from 2048 to 32768
- layernorm_average: float32 [4, 2048], P(None, 'dp'), may hold values from -1 to 1.3, as said below
Outputs:
- layer_output: bfloat16 [8192, 2048], P('dp')
- input_gradient: float32 [8192, 2048], P('dp')
- attend_master: float32 [2048, 3, 2048], P('dp', None, 'tensor')
- attend_moment: float32 [2048, 3, 2048], P('dp', None, 'tensor')
- attend_square: float32 [2048, 3, 2048], P('dp', None, 'tensor')
- attend_smooth: float32 [2048, 3, 2048], P('dp', None, 'tensor')
- attend_copy: bfloat16 [2048, 3, 2048], P('dp', None, 'tensor')
- combine_master: float32 [2048, 2048], P('tensor', 'dp')
- combine_moment: float32 [2048, 2048], P('tensor', 'dp')
- combine_square: float32 [2048, 2048], P('tensor', 'dp')
- combine_smooth: float32 [2048, 2048], P('tensor', 'dp')
- combine_copy: bfloat16 [2048, 2048], P('tensor', 'dp')
- expand_master: float32 [2048, 8192], P('dp', 'tensor')
- expand_moment: float32 [2048, 8192], P('dp', 'tensor')
- expand_square: float32 [2048, 8192], P('dp', 'tensor')
- expand_smooth: float32 [2048, 8192], P('dp', 'tensor')
- expand_copy: bfloat16 [2048, 8192], P('dp', 'tensor')
- shrink_master: float32 [8192, 2048], P('tensor', 'dp')
- shrink_moment: float32 [8192, 2048], P('tensor', 'dp')
- shrink_square: float32 [8192, 2048], P('tensor', 'dp')
- shrink_smooth: float32 [8192, 2048], P('tensor', 'dp')
- shrink_copy: bfloat16 [8192, 2048], P('tensor', 'dp')
- layernorm_master: float32 [4, 2048], P(None, 'dp')
- layernorm_moment: float32 [4, 2048], P(None, 'dp')
- layernorm_square: float32 [4, 2048], P(None, 'dp')
- layernorm_smooth: float32 [4, 2048], P(None, 'dp')
- layernorm_copy: bfloat16 [4, 2048], P(None, 'dp')
The draws below stay inside these ranges and needn't reach their ends.
Inputs may be any that keep to these rules, and one draw needn't show every extreme that they name: `layernorm_params`: gains about one, biases of either sign. `layernorm_average`: gains about one, biases of either sign.
All inputs are finite; a program needn't handle non-finite values. No bound on the sum of `self_generated` on one device may be relied on, other than what follows from the above.
Results may differ from the reference program's by a relative error of at most 0.012.
The reference program's roundings to bfloat16 on the way count: a program that leaves them out, or rounds other values in their place, can miss the bound.
Values may be sent and summed in bfloat16 or wider, within the bound.
No kernel may reach another device: no remote copies, remote signals or barrier semaphores. Data moves between devices by JAX's collectives and lax.ppermute only.
A program may use at most 320 MiB of HBM per device.

```python
import math
import jax
import jax.numpy as jnp
import numpy as np
from jax import lax

D = 2048
HEADS = 16
HEAD_DIM = 128
FF = 8192
SEQ = 1024
EPIS = 8
STEP = 10
ROWS_DEV = 1
ROWS = 8
TOKENS = 8192
N_DP = 8


def norm_law(key):
    gain_key, shift_key = jax.random.split(key)
    gain_rows = 1.0 + jax.random.uniform(gain_key, (2, D), jnp.float32, -0.3, 0.3)
    shift_rows = jnp.clip(0.3 * jax.random.normal(shift_key, (2, D), jnp.float32), -1.0, 1.0)
    return jnp.stack([gain_rows[0], shift_rows[0], gain_rows[1], shift_rows[1]]).astype(jnp.float32)


def draw_layernorm_params(key, part):
    return norm_law(jax.random.fold_in(key, 3))


def draw_layernorm_average(key, part):
    return norm_law(jax.random.fold_in(key, 7))


def plant(entries, key, smallest, top_value):
    extent = entries.shape
    place = [jax.random.randint(jax.random.fold_in(key, axis), (), 0, extent[axis]) for axis in range(len(extent))]
    entries = entries.at[tuple(place)].set(smallest)
    longest = extent.index(max(extent))
    place[longest] = (place[longest] + 1) % extent[longest]
    return entries.at[tuple(place)].set(top_value)


def spiked(result, own_key, source, target, blocks, factor):
    owner, partner = [(jnp.arange(result.shape[axis_at]) // (result.shape[axis_at] // blocks)).reshape([-1 if axis == axis_at else 1 for axis in range(result.ndim)]) for axis_at in (source, target)]
    chosen = jax.random.permutation(own_key, blocks)[partner]
    strong = (owner == chosen) | (owner == (partner + blocks // 2) % blocks)
    return jnp.where(strong, factor * result, result)


def level_of(rng, extent, cuts, least, largest):
    def one(dim, blocks):
        steps = jax.random.uniform(jax.random.fold_in(jax.random.fold_in(rng, 6), dim), (blocks,), jnp.float32, least / len(cuts), largest / len(cuts))
        return jnp.repeat(jnp.exp(steps), extent[dim] // blocks).reshape((-1,) + (1,) * (len(extent) - dim - 1))

    loudness = one(*cuts[0])
    for cut in cuts[1:]:
        loudness = loudness * one(*cut)
    return loudness


def split_up(number_of, total, reach, lean):
    loads = [(1 << 20) // math.isqrt(standing ** lean) + 1 for standing in range(2, number_of + 1)]
    spare, holding = total - reach - (number_of - 1), [1] * (number_of - 1)
    while spare > 0:
        movable = [i for i in range(number_of - 1) if holding[i] < reach]
        whole, budget = sum([loads[i] for i in movable]), spare
        for i in movable:
            more = min(reach - holding[i], max(1, budget * loads[i] // whole), spare)
            holding[i] = holding[i] + more
            spare = spare - more
    return np.array([reach] + holding)


def ragged_sizes(rng, amount, total, reach, skew):
    if amount == 2:
        one = jax.random.randint(rng, (), max(1, total - reach), min(reach, total - 1) + 1)
        return jnp.stack([one, total - one])
    lengths = jnp.asarray(split_up(amount, total, reach, skew), jnp.int32)
    couples = (amount - 1) // 2
    donor, sink = lengths[1:1 + 2 * couples:2], lengths[2:2 + 2 * couples:2]
    slack = jnp.minimum(donor - 1, reach - sink)
    shifted = jax.random.randint(jax.random.fold_in(rng, 1), (couples,), 0, 1 << 20) % (slack + 1)
    lengths = lengths.at[1:1 + 2 * couples:2].set(donor - shifted).at[2:2 + 2 * couples:2].set(sink + shifted)
    return lengths[jax.random.permutation(jax.random.fold_in(rng, 2), amount)]


def bell_draw(own_key, dims, deviation, bound, cuts=(), kind=jnp.bfloat16):
    values = jax.random.normal(own_key, dims, jnp.float32) * deviation
    if len(cuts) > 0:
        values = level_of(own_key, dims, cuts, -0.22, 0.18) * values
    return jnp.clip(values, min=-bound, max=bound).astype(kind)


def heavy_noise(own_key, shape, scale, bound, cuts, heavy, kind=jnp.bfloat16):
    entries = scale * jax.random.normal(own_key, shape, jnp.float32)
    if cuts:
        entries = entries * level_of(own_key, shape, cuts, -0.22, 0.18)
    return jnp.clip(spiked(entries, jax.random.fold_in(own_key, 3), *heavy), -bound, bound).astype(kind)


def setup_inputs(seed: int = 0) -> dict:
    key_list = jax.random.split(jax.random.key(seed), 26)
    hidden_in = bell_draw(key_list[0], (TOKENS, D), 1.0, 6.0, ((0, 8),))
    out_cotangent = heavy_noise(key_list[1], (TOKENS, D), 1.0, 6.0, ((0, 8),), (0, 1, 8, 2.0))
    episode_lengths = jax.vmap(lambda own: ragged_sizes(own, EPIS, SEQ, SEQ // 2, 2))(jax.random.split(key_list[2], ROWS)).reshape((ROWS, EPIS)).astype(jnp.int32)
    self_generated = plant((jax.random.randint(key_list[3], (TOKENS,), 0, 4) < 1).astype(jnp.int32), jax.random.fold_in(key_list[3], 1), 0, 1)
    loss_numerator = plant(jax.random.randint(key_list[4], (TOKENS,), 1, 9), jax.random.fold_in(key_list[4], 1), 1, 8).astype(jnp.int32)
    attend_weights = bell_draw(key_list[5], (D, 3, D), D ** -0.5, 0.125, ((0, 8), (2, 4)), jnp.float32)
    attend_first = bell_draw(key_list[6], (D, 3, D), (TOKENS ** 0.5), 512.0, ((0, 8), (2, 4)), jnp.float32)
    attend_second = jnp.clip(jnp.exp(math.log(65536.0) - 2.7725887 * jax.random.uniform(key_list[7], (D, 3, D), jnp.float32) ** level_of(key_list[7], (D, 3, D), ((0, 8), (2, 4)), -0.2, 0.2)), 4096.0, 65536.0)
    attend_average = bell_draw(key_list[8], (D, 3, D), D ** -0.5, 0.125, ((0, 8), (2, 4)), jnp.float32)
    combine_weights = bell_draw(key_list[9], (D, D), (D * 16 // SEQ) ** -0.5, 1.0, ((0, 4), (1, 8)), jnp.float32)
    combine_first = bell_draw(key_list[10], (D, D), (5 * (TOKENS / SEQ) ** 0.5), 80.0, ((0, 4), (1, 8)), jnp.float32)
    combine_second = jnp.clip(jnp.exp(math.log(1600.0) - 2.8134107 * jax.random.uniform(key_list[11], (D, D), jnp.float32) ** level_of(key_list[11], (D, D), ((0, 4), (1, 8)), -0.2, 0.2)), 96.0, 1600.0)
    combine_average = bell_draw(key_list[12], (D, D), (D * 16 // SEQ) ** -0.5, 1.0, ((0, 4), (1, 8)), jnp.float32)
    expand_weights = bell_draw(key_list[13], (D, FF), D ** -0.5, 0.125, ((0, 8), (1, 4)), jnp.float32)
    expand_first = bell_draw(key_list[14], (D, FF), (0.25 * TOKENS ** 0.5), 128.0, ((0, 8), (1, 4)), jnp.float32)
    expand_second = jnp.clip(jnp.exp(math.log(4096.0) - 2.8134107 * jax.random.uniform(key_list[15], (D, FF), jnp.float32) ** level_of(key_list[15], (D, FF), ((0, 8), (1, 4)), -0.2, 0.2)), 245.76, 4096.0)
    expand_average = bell_draw(key_list[16], (D, FF), D ** -0.5, 0.125, ((0, 8), (1, 4)), jnp.float32)
    shrink_weights = bell_draw(key_list[17], (FF, D), FF ** -0.5, 0.0625, ((0, 4), (1, 8)), jnp.float32)
    shrink_first = bell_draw(key_list[18], (FF, D), (0.5 * TOKENS ** 0.5), 256.0, ((0, 4), (1, 8)), jnp.float32)
    shrink_second = jnp.clip(jnp.exp(math.log(16384.0) - 2.8134107 * jax.random.uniform(key_list[19], (FF, D), jnp.float32) ** level_of(key_list[19], (FF, D), ((0, 4), (1, 8)), -0.2, 0.2)), 983.04, 16384.0)
    shrink_average = bell_draw(key_list[20], (FF, D), FF ** -0.5, 0.0625, ((0, 4), (1, 8)), jnp.float32)
    layernorm_params = draw_layernorm_params(jax.random.fold_in(key_list[25], 71), 0)
    layernorm_first = bell_draw(key_list[22], (4, D), (0.7 * TOKENS ** 0.5), 384.0, ((1, 8),), jnp.float32)
    layernorm_second = jnp.clip(jnp.exp(math.log(32768.0) - 2.7725887 * jax.random.uniform(key_list[23], (4, D), jnp.float32) ** level_of(key_list[23], (4, D), ((1, 8),), -0.2, 0.2)), 2048.0, 32768.0)
    layernorm_average = draw_layernorm_average(jax.random.fold_in(key_list[25], 71), 0)
    return {"hidden_in": hidden_in, "out_cotangent": out_cotangent, "episode_lengths": episode_lengths, "self_generated": self_generated, "loss_numerator": loss_numerator, "attend_weights": attend_weights, "attend_first": attend_first, "attend_second": attend_second, "attend_average": attend_average, "combine_weights": combine_weights, "combine_first": combine_first, "combine_second": combine_second, "combine_average": combine_average, "expand_weights": expand_weights, "expand_first": expand_first, "expand_second": expand_second, "expand_average": expand_average, "shrink_weights": shrink_weights, "shrink_first": shrink_first, "shrink_second": shrink_second, "shrink_average": shrink_average, "layernorm_params": layernorm_params, "layernorm_first": layernorm_first, "layernorm_second": layernorm_second, "layernorm_average": layernorm_average}


highest = lax.Precision.HIGHEST
beta_first = 0.5
beta_second = 0.5
average_decay = 0.5
adam_epsilon = 1e-08
weight_decay = 0.1
matrix_rate = 0.02
norm_rate = 0.2
norm_epsilon = 1e-05

@jax.custom_vjp
def low(v):
    return lax.optimization_barrier(v.astype(jnp.bfloat16)).astype(jnp.float32)

@jax.custom_vjp
def low_back(v):
    return v

def low_keep(v):
    return (low(v), None)

def low_pass(kept, grad):
    return (grad,)

def back_keep(v):
    return (v, None)

def back_low(kept, grad):
    return (low(grad),)
low.defvjp(low_keep, low_pass)
low_back.defvjp(back_keep, back_low)

def rounded_both(values):
    return low(low_back(values))

def layer_norm(values, gain_row, shift_row):
    center = values - lax.optimization_barrier(jnp.mean(values, axis=-1, keepdims=True))
    spread = lax.optimization_barrier(jnp.mean(center * center, axis=-1, keepdims=True))
    return center * lax.rsqrt(spread + norm_epsilon) * gain_row + shift_row

def segment_ids(lengths_row):
    bounds = jnp.cumsum(lengths_row).astype(jnp.int32)
    places = jnp.arange(SEQ, dtype=jnp.int32)
    return lax.optimization_barrier(jnp.sum((places[:, None] >= bounds[None, :]).astype(jnp.int32), axis=1))

def row_attention(packed):
    queries, keys_row, values_row, segment = packed
    places = jnp.arange(SEQ, dtype=jnp.int32)
    allowed = (segment[:, None] == segment[None, :]) & (places[None, :] <= places[:, None])
    scores = jnp.einsum('qhd,khd->hqk', queries, keys_row, precision=highest) * HEAD_DIM ** (-0.5)
    scores = low_back(scores)
    masked = jnp.where(allowed[None], scores, -1e+30)
    row_top = lax.optimization_barrier(jnp.max(masked, axis=-1, keepdims=True))
    exponent = jnp.exp(masked - row_top)
    softmax_out = low(exponent / lax.optimization_barrier(jnp.sum(exponent, axis=-1, keepdims=True)))
    return jnp.einsum('hqk,khd->qhd', softmax_out, values_row, precision=highest)

def block_forward(hidden, attend_matrix, combine_matrix, expand_matrix, shrink_matrix, norm_matrix, segments):
    row_count = segments.shape[0]
    normed = low(layer_norm(hidden, norm_matrix[0], norm_matrix[1]))
    projected = rounded_both(jnp.einsum('nd,dke->nke', normed, attend_matrix, precision=highest))
    shaped = projected.reshape(row_count, SEQ, 3, HEADS, HEAD_DIM)
    mixed_heads = lax.map(jax.checkpoint(row_attention), (shaped[:, :, 0], shaped[:, :, 1], shaped[:, :, 2], segments))
    mixed_heads = rounded_both(mixed_heads.reshape(row_count * SEQ, D))
    attended = low_back(jnp.dot(mixed_heads, combine_matrix, precision=highest))
    residual = hidden + attended
    normed_two = low(layer_norm(residual, norm_matrix[2], norm_matrix[3]))
    expanded = low_back(jnp.dot(normed_two, expand_matrix, precision=highest))
    activated = low(jax.nn.gelu(expanded))
    branch = low_back(jnp.dot(activated, shrink_matrix, precision=highest))
    return residual + branch

def adam_update(master, moment, square, gradient, rate_value, decay_value):
    moment_new = beta_first * moment + (1.0 - beta_first) * gradient
    square_new = beta_second * square + (1.0 - beta_second) * gradient * gradient
    fix_first = 1.0 - beta_first ** STEP
    fix_second = 1.0 - beta_second ** STEP
    direction = moment_new / fix_first / (jnp.sqrt(square_new / fix_second) + adam_epsilon)
    master_new = master - rate_value * (direction + decay_value * master)
    return (master_new, moment_new, square_new)

def reference(hidden_in, out_cotangent, episode_lengths, self_generated, loss_numerator, attend_weights, attend_first, attend_second, attend_average, combine_weights, combine_first, combine_second, combine_average, expand_weights, expand_first, expand_second, expand_average, shrink_weights, shrink_first, shrink_second, shrink_average, layernorm_params, layernorm_first, layernorm_second, layernorm_average):
    masters = (attend_weights, combine_weights, expand_weights, shrink_weights, layernorm_params)
    params_used = tuple((master.astype(jnp.bfloat16).astype(jnp.float32) for master in masters))
    segments = jax.vmap(segment_ids)(episode_lengths)
    factor = loss_numerator.astype(jnp.float32) / (4.0 * (1.0 + self_generated.astype(jnp.float32)))
    group_tokens = ROWS_DEV * SEQ
    inputs = (hidden_in.reshape(N_DP, group_tokens, D), out_cotangent.reshape(N_DP, group_tokens, D), segments.reshape(N_DP, ROWS_DEV, SEQ), factor.reshape(N_DP, group_tokens))

    def group_step(running, group):
        hidden_grp, cotangent_grp, segment_grp, factor_grp = group

        def forward_fn(hidden, attend_matrix, combine_matrix, expand_matrix, shrink_matrix, norm_matrix):
            return block_forward(hidden, attend_matrix, combine_matrix, expand_matrix, shrink_matrix, norm_matrix, segment_grp)
        output, pullback = jax.vjp(forward_fn, hidden_grp.astype(jnp.float32), *params_used)
        gradients = pullback(factor_grp[:, None] * cotangent_grp.astype(jnp.float32))
        running = tuple((summed + fresh for summed, fresh in zip(running, gradients[1:])))
        return (running, (output.astype(jnp.bfloat16), gradients[0]))
    start_grads = tuple((jnp.zeros(param_used.shape, jnp.float32) for param_used in params_used))
    totals, (outputs, input_grads) = lax.scan(group_step, start_grads, inputs)
    layer_output = outputs.reshape(TOKENS, D)
    input_gradient = input_grads.reshape(TOKENS, D)
    states = ((attend_first, attend_second, attend_average, matrix_rate, weight_decay), (combine_first, combine_second, combine_average, matrix_rate, weight_decay), (expand_first, expand_second, expand_average, matrix_rate, weight_decay), (shrink_first, shrink_second, shrink_average, matrix_rate, weight_decay), (layernorm_first, layernorm_second, layernorm_average, norm_rate, 0.0))
    results = [layer_output, input_gradient]
    for master, gradient, state in zip(masters, totals, states):
        moment, square, average, rate_value, decay_value = state
        master_new, moment_new, square_new = adam_update(master, moment, square, gradient, rate_value, decay_value)
        smooth_new = average_decay * average + (1.0 - average_decay) * master_new
        results.extend([master_new, moment_new, square_new, smooth_new, master_new.astype(jnp.bfloat16)])
    return tuple(results)
```

```python
import jax
import jax.numpy as jnp
from jax import lax
from jax.sharding import PartitionSpec as P

HEAD_DIM = 128
STEP = 10


beta_first = 0.5
beta_second = 0.5
average_decay = 0.5
adam_epsilon = 1e-08
weight_decay = 0.1
matrix_rate = 0.02
norm_rate = 0.2
norm_epsilon = 1e-05


def layer_norm(values, gain_row, shift_row):
    center = values - jnp.mean(values, axis=-1, keepdims=True)
    spread = jnp.mean(center * center, axis=-1, keepdims=True)
    return center * lax.rsqrt(spread + norm_epsilon) * gain_row + shift_row


def segment_ids(lengths_row, row_length):
    order = jnp.arange(lengths_row.shape[0], dtype=jnp.int32)
    earlier = order[None, :] <= order[:, None]
    bounds = jnp.sum(jnp.where(earlier, lengths_row[None, :], 0), axis=1)
    places = jnp.arange(row_length, dtype=jnp.int32)
    return jnp.sum((places[:, None] >= bounds[None, :]).astype(jnp.int32), axis=1)


def allowed_mask(segment, first_row, block_rows):
    row_length = segment.shape[0]
    query_places = first_row + jnp.arange(block_rows, dtype=jnp.int32)
    key_places = jnp.arange(row_length, dtype=jnp.int32)
    query_segment = segment[first_row : first_row + block_rows]
    return (query_segment[:, None] == segment[None, :]) & (
        key_places[None, :] <= query_places[:, None]
    )


def attend_row(packed):
    queries, keys_row, values_row, segment = packed
    row_length = queries.shape[0]
    block_rows = min(512, row_length)
    score_scale = HEAD_DIM ** (-0.5)
    out_parts = []
    logsum_parts = []
    for first_row in range(0, row_length, block_rows):
        query_block = queries[first_row : first_row + block_rows]
        allowed = allowed_mask(segment, first_row, block_rows)
        scores = (
            jnp.einsum("qhd,khd->hqk", query_block, keys_row, preferred_element_type=jnp.float32)
            * score_scale
        )
        masked = jnp.where(allowed[None], scores, -1e30)
        row_top = jnp.max(masked, axis=-1, keepdims=True)
        exponent = jnp.exp(masked - row_top)
        row_total = jnp.sum(exponent, axis=-1, keepdims=True)
        softmax_low = (exponent / row_total).astype(jnp.bfloat16)
        out_parts.append(
            jnp.einsum("hqk,khd->qhd", softmax_low, values_row, preferred_element_type=jnp.float32)
        )
        logsum_parts.append((row_top + jnp.log(row_total))[..., 0])
    return (jnp.concatenate(out_parts, axis=0), jnp.concatenate(logsum_parts, axis=1))


def attend_row_back(packed):
    queries, keys_row, values_row, segment, logsum, grad_row = packed
    row_length = queries.shape[0]
    block_rows = min(512, row_length)
    score_scale = HEAD_DIM ** (-0.5)
    keys_grad = jnp.zeros(keys_row.shape, jnp.float32)
    values_grad = jnp.zeros(values_row.shape, jnp.float32)
    query_parts = []
    for first_row in range(0, row_length, block_rows):
        query_block = queries[first_row : first_row + block_rows]
        grad_block = grad_row[first_row : first_row + block_rows]
        allowed = allowed_mask(segment, first_row, block_rows)
        scores = (
            jnp.einsum("qhd,khd->hqk", query_block, keys_row, preferred_element_type=jnp.float32)
            * score_scale
        )
        masked = jnp.where(allowed[None], scores, -1e30)
        softmax_full = jnp.exp(masked - logsum[:, first_row : first_row + block_rows, None])
        softmax_low = softmax_full.astype(jnp.bfloat16)
        values_grad = values_grad + jnp.einsum(
            "hqk,qhd->khd", softmax_low, grad_block, preferred_element_type=jnp.float32
        )
        prob_grad = jnp.einsum(
            "qhd,khd->hqk", grad_block, values_row, preferred_element_type=jnp.float32
        )
        row_delta = jnp.sum(prob_grad * softmax_full, axis=-1, keepdims=True)
        score_grad = (softmax_full * (prob_grad - row_delta)).astype(jnp.bfloat16)
        query_parts.append(
            jnp.einsum("hqk,khd->qhd", score_grad, keys_row, preferred_element_type=jnp.float32)
            * score_scale
        )
        keys_grad = (
            keys_grad
            + jnp.einsum(
                "hqk,qhd->khd", score_grad, query_block, preferred_element_type=jnp.float32
            )
            * score_scale
        )
    stacked = jnp.stack([jnp.concatenate(query_parts, axis=0), keys_grad, values_grad], axis=1)
    return stacked.astype(jnp.bfloat16)


def adam_update(master, moment, square, gradient, rate_value, decay_value):
    moment_new = beta_first * moment + (1.0 - beta_first) * gradient
    square_new = beta_second * square + (1.0 - beta_second) * gradient * gradient
    fix_first = 1.0 - beta_first**STEP
    fix_second = 1.0 - beta_second**STEP
    direction = moment_new / fix_first / (jnp.sqrt(square_new / fix_second) + adam_epsilon)
    master_new = master - rate_value * (direction + decay_value * master)
    return (master_new, moment_new, square_new)


def shards(
    hidden_in,
    out_cotangent,
    episode_lengths,
    self_generated,
    loss_numerator,
    attend_weights,
    attend_first,
    attend_second,
    attend_average,
    combine_weights,
    combine_first,
    combine_second,
    combine_average,
    expand_weights,
    expand_first,
    expand_second,
    expand_average,
    shrink_weights,
    shrink_first,
    shrink_second,
    shrink_average,
    layernorm_params,
    layernorm_first,
    layernorm_second,
    layernorm_average,
):
    local_tokens = hidden_in.shape[0]
    row_count = episode_lengths.shape[0]
    row_length = local_tokens // row_count
    attend_low = attend_weights.astype(jnp.bfloat16)
    combine_low = combine_weights.astype(jnp.bfloat16)
    expand_low = expand_weights.astype(jnp.bfloat16)
    shrink_low = shrink_weights.astype(jnp.bfloat16)
    norm_low = layernorm_params.astype(jnp.bfloat16)
    attend_full, combine_full, expand_full, shrink_full, norm_full = (
        lax.all_gather(attend_low, "dp", axis=0, tiled=True),
        lax.all_gather(combine_low, "dp", axis=1, tiled=True),
        lax.all_gather(expand_low, "dp", axis=0, tiled=True),
        lax.all_gather(shrink_low, "dp", axis=1, tiled=True),
        lax.all_gather(norm_low, "dp", axis=1, tiled=True),
    )
    norm_values = norm_full.astype(jnp.float32)
    hidden = hidden_in.astype(jnp.float32)
    normed_one, pull_one = jax.vjp(layer_norm, hidden, norm_values[0], norm_values[1])
    normed_low = normed_one.astype(jnp.bfloat16)
    projected = jnp.einsum(
        "nd,dke->nke", normed_low, attend_full, preferred_element_type=jnp.float32
    ).astype(jnp.bfloat16)
    local_width = projected.shape[2]
    head_count = local_width // HEAD_DIM
    shaped = projected.reshape(row_count, row_length, 3, head_count, HEAD_DIM)
    segments = jax.vmap(lambda lengths_row: segment_ids(lengths_row, row_length))(episode_lengths)
    queries_all = shaped[:, :, 0]
    keys_all = shaped[:, :, 1]
    values_all = shaped[:, :, 2]
    mixed_heads, logsum = lax.map(attend_row, (queries_all, keys_all, values_all, segments))
    mixed_low = mixed_heads.reshape(local_tokens, local_width).astype(jnp.bfloat16)
    attended = lax.psum(
        jnp.dot(mixed_low, combine_full, preferred_element_type=jnp.float32).astype(jnp.bfloat16), "tensor"
    ).astype(jnp.float32)
    residual = hidden + attended
    normed_two, pull_two = jax.vjp(layer_norm, residual, norm_values[2], norm_values[3])
    normed_two_low = normed_two.astype(jnp.bfloat16)
    expanded = jnp.dot(normed_two_low, expand_full, preferred_element_type=jnp.float32)
    activated, pull_gelu = jax.vjp(jax.nn.gelu, expanded)
    activated_low = activated.astype(jnp.bfloat16)
    branch = lax.psum(
        jnp.dot(activated_low, shrink_full, preferred_element_type=jnp.float32).astype(jnp.bfloat16), "tensor"
    ).astype(jnp.float32)
    layer_output = (residual + branch).astype(jnp.bfloat16)
    factor = loss_numerator.astype(jnp.float32) / (4.0 * (1.0 + self_generated.astype(jnp.float32)))
    out_grad = factor[:, None] * out_cotangent.astype(jnp.float32)
    attend_back, combine_back, expand_back, shrink_back = (
        lax.all_gather(attend_low, "dp", axis=0, tiled=True),
        lax.all_gather(combine_low, "dp", axis=1, tiled=True),
        lax.all_gather(expand_low, "dp", axis=0, tiled=True),
        lax.all_gather(shrink_low, "dp", axis=1, tiled=True),
    )
    branch_grad_low = out_grad.astype(jnp.bfloat16)
    shrink_grad = jnp.einsum(
        "nf,nd->fd", activated_low, branch_grad_low, preferred_element_type=jnp.float32
    )
    activated_grad = jnp.einsum(
        "nd,fd->nf", branch_grad_low, shrink_back, preferred_element_type=jnp.float32
    )
    expanded_grad_low = pull_gelu(activated_grad)[0].astype(jnp.bfloat16)
    expand_grad = jnp.einsum(
        "nd,nf->df", normed_two_low, expanded_grad_low, preferred_element_type=jnp.float32
    )
    normed_two_grad = lax.psum(
        jnp.einsum("nf,df->nd", expanded_grad_low, expand_back, preferred_element_type=jnp.float32).astype(jnp.bfloat16),
        "tensor",
    ).astype(jnp.float32)
    residual_from_norm, gain_two_grad, shift_two_grad = pull_two(normed_two_grad)
    residual_grad = out_grad + residual_from_norm
    attended_grad_low = residual_grad.astype(jnp.bfloat16)
    combine_grad = jnp.einsum(
        "ne,nd->ed", mixed_low, attended_grad_low, preferred_element_type=jnp.float32
    )
    mixed_grad = jnp.einsum(
        "nd,ed->ne", attended_grad_low, combine_back, preferred_element_type=jnp.float32
    ).astype(jnp.bfloat16)
    mixed_grad_rows = mixed_grad.reshape(row_count, row_length, head_count, HEAD_DIM)
    projected_grad = lax.map(
        attend_row_back, (queries_all, keys_all, values_all, segments, logsum, mixed_grad_rows)
    )
    projected_grad = projected_grad.reshape(local_tokens, 3, local_width)
    attend_grad = jnp.einsum(
        "nd,nke->dke", normed_low, projected_grad, preferred_element_type=jnp.float32
    )
    normed_one_grad = lax.psum(
        jnp.einsum("nke,dke->nd", projected_grad, attend_back, preferred_element_type=jnp.float32).astype(jnp.bfloat16),
        "tensor",
    ).astype(jnp.float32)
    hidden_from_norm, gain_one_grad, shift_one_grad = pull_one(normed_one_grad)
    input_gradient = residual_grad + hidden_from_norm
    norm_grad = jnp.stack([gain_one_grad, shift_one_grad, gain_two_grad, shift_two_grad])
    attend_sum, combine_sum, expand_sum, shrink_sum, norm_sum = (
        lax.psum_scatter(attend_grad.astype(jnp.bfloat16), "dp", scatter_dimension=0, tiled=True),
        lax.psum_scatter(combine_grad.astype(jnp.bfloat16), "dp", scatter_dimension=1, tiled=True),
        lax.psum_scatter(expand_grad.astype(jnp.bfloat16), "dp", scatter_dimension=0, tiled=True),
        lax.psum_scatter(shrink_grad.astype(jnp.bfloat16), "dp", scatter_dimension=1, tiled=True),
        lax.psum_scatter(norm_grad, "dp", scatter_dimension=1, tiled=True),
    )
    kinds = (
        (
            attend_weights,
            attend_first,
            attend_second,
            attend_average,
            attend_sum,
            matrix_rate,
            weight_decay,
        ),
        (
            combine_weights,
            combine_first,
            combine_second,
            combine_average,
            combine_sum,
            matrix_rate,
            weight_decay,
        ),
        (
            expand_weights,
            expand_first,
            expand_second,
            expand_average,
            expand_sum,
            matrix_rate,
            weight_decay,
        ),
        (
            shrink_weights,
            shrink_first,
            shrink_second,
            shrink_average,
            shrink_sum,
            matrix_rate,
            weight_decay,
        ),
        (
            layernorm_params,
            layernorm_first,
            layernorm_second,
            layernorm_average,
            norm_sum,
            norm_rate,
            0.0,
        ),
    )
    results = [layer_output, input_gradient]
    for master, moment, square, average, gradient, rate_value, decay_value in kinds:
        gradient = gradient.astype(jnp.float32)
        master_new, moment_new, square_new = adam_update(
            master, moment, square, gradient, rate_value, decay_value
        )
        smooth_new = average_decay * average + (1.0 - average_decay) * master_new
        results.extend(
            [master_new, moment_new, square_new, smooth_new, master_new.astype(jnp.bfloat16)]
        )
    return tuple(results)


def solution(mesh):
    placed = (
        P("dp", None),
        P("dp", None),
        P("dp", None),
        P("dp"),
        P("dp"),
        P("dp", None, "tensor"),
        P("dp", None, "tensor"),
        P("dp", None, "tensor"),
        P("dp", None, "tensor"),
        P("tensor", "dp"),
        P("tensor", "dp"),
        P("tensor", "dp"),
        P("tensor", "dp"),
        P("dp", "tensor"),
        P("dp", "tensor"),
        P("dp", "tensor"),
        P("dp", "tensor"),
        P("tensor", "dp"),
        P("tensor", "dp"),
        P("tensor", "dp"),
        P("tensor", "dp"),
        P(None, "dp"),
        P(None, "dp"),
        P(None, "dp"),
        P(None, "dp"),
    )
    return jax.shard_map(
        shards,
        mesh=mesh,
        in_specs=placed,
        out_specs=(
            P("dp", None),
            P("dp", None),
            P("dp", None, "tensor"),
            P("dp", None, "tensor"),
            P("dp", None, "tensor"),
            P("dp", None, "tensor"),
            P("dp", None, "tensor"),
            P("tensor", "dp"),
            P("tensor", "dp"),
            P("tensor", "dp"),
            P("tensor", "dp"),
            P("tensor", "dp"),
            P("dp", "tensor"),
            P("dp", "tensor"),
            P("dp", "tensor"),
            P("dp", "tensor"),
            P("dp", "tensor"),
            P("tensor", "dp"),
            P("tensor", "dp"),
            P("tensor", "dp"),
            P("tensor", "dp"),
            P("tensor", "dp"),
            P(None, "dp"),
            P(None, "dp"),
            P(None, "dp"),
            P(None, "dp"),
            P(None, "dp"),
        ),
        check_vma=False,
    )
```

```python
import functools
import math

import jax
import jax.numpy as jnp
from jax import lax
from jax.sharding import PartitionSpec as P

HEAD_DIM = 128
STEP = 10


beta_first = 0.5
beta_second = 0.5
average_decay = 0.5
adam_epsilon = 1e-08
weight_decay = 0.1
matrix_rate = 0.02
norm_rate = 0.2
norm_epsilon = 1e-05
low_type = jnp.bfloat16
wide = jnp.float32


def norm_parts(values):
    center = values - jnp.mean(values, axis=-1, keepdims=True)
    spread = jnp.mean(center * center, axis=-1, keepdims=True)
    inverse = lax.rsqrt(spread + norm_epsilon)
    return center * inverse, inverse


def norm_back(grad, scaled, inverse, gain_row):
    inner = grad * gain_row
    mean_inner = jnp.mean(inner, axis=-1, keepdims=True)
    mean_scaled = jnp.mean(inner * scaled, axis=-1, keepdims=True)
    result = inverse * (inner - mean_inner - scaled * mean_scaled)
    return result, jnp.sum(grad * scaled, axis=0), jnp.sum(grad, axis=0)


def gelu_parts(v):
    scale = math.sqrt(2.0 / math.pi)
    bend = jnp.tanh(scale * (v + 0.044715 * (v * v * v)))
    slope = 0.5 * (1.0 + bend) + 0.5 * v * (1.0 - bend * bend) * scale * (
        1.0 + 3.0 * 0.044715 * (v * v)
    )
    return 0.5 * v * (1.0 + bend), slope


def segment_ids(lengths_row, row_length):
    order = jnp.arange(lengths_row.shape[0], dtype=jnp.int32)
    earlier = order[None, :] <= order[:, None]
    bounds = jnp.sum(jnp.where(earlier, lengths_row[None, :], 0), axis=1)
    places = jnp.arange(row_length, dtype=jnp.int32)
    return jnp.sum((places[:, None] >= bounds[None, :]).astype(jnp.int32), axis=1)


def allowed_mask(segment, first_row, block_rows):
    row_length = segment.shape[0]
    query_places = first_row + jnp.arange(block_rows, dtype=jnp.int32)
    key_places = jnp.arange(row_length, dtype=jnp.int32)
    query_segment = segment[first_row : first_row + block_rows]
    return (query_segment[:, None] == segment[None, :]) & (
        key_places[None, :] <= query_places[:, None]
    )


def attend_row(packed):
    queries, keys_row, values_row, segment = packed
    row_length = queries.shape[0]
    block_rows = min(512, row_length)
    score_scale = HEAD_DIM ** (-0.5)
    out_parts = []
    logsum_parts = []
    for first_row in range(0, row_length, block_rows):
        query_block = queries[first_row : first_row + block_rows]
        allowed = allowed_mask(segment, first_row, block_rows)
        scores = (
            jnp.einsum("qhd,khd->hqk", query_block, keys_row, preferred_element_type=jnp.float32)
            * score_scale
        )
        masked = jnp.where(allowed[None], scores, -1e30)
        row_top = jnp.max(masked, axis=-1, keepdims=True)
        exponent = jnp.exp(masked - row_top)
        row_total = jnp.sum(exponent, axis=-1, keepdims=True)
        softmax_low = (exponent / row_total).astype(jnp.bfloat16)
        out_parts.append(
            jnp.einsum("hqk,khd->qhd", softmax_low, values_row, preferred_element_type=jnp.float32)
        )
        logsum_parts.append((row_top + jnp.log(row_total))[..., 0])
    return (jnp.concatenate(out_parts, axis=0), jnp.concatenate(logsum_parts, axis=1))


def attend_row_back(packed):
    queries, keys_row, values_row, segment, logsum, grad_row = packed
    row_length = queries.shape[0]
    block_rows = min(512, row_length)
    score_scale = HEAD_DIM ** (-0.5)
    keys_grad = jnp.zeros(keys_row.shape, jnp.float32)
    values_grad = jnp.zeros(values_row.shape, jnp.float32)
    query_parts = []
    for first_row in range(0, row_length, block_rows):
        query_block = queries[first_row : first_row + block_rows]
        grad_block = grad_row[first_row : first_row + block_rows]
        allowed = allowed_mask(segment, first_row, block_rows)
        scores = (
            jnp.einsum("qhd,khd->hqk", query_block, keys_row, preferred_element_type=jnp.float32)
            * score_scale
        )
        masked = jnp.where(allowed[None], scores, -1e30)
        softmax_full = jnp.exp(masked - logsum[:, first_row : first_row + block_rows, None])
        softmax_low = softmax_full.astype(jnp.bfloat16)
        values_grad = values_grad + jnp.einsum(
            "hqk,qhd->khd", softmax_low, grad_block, preferred_element_type=jnp.float32
        )
        prob_grad = jnp.einsum(
            "qhd,khd->hqk", grad_block, values_row, preferred_element_type=jnp.float32
        )
        row_delta = jnp.sum(prob_grad * softmax_full, axis=-1, keepdims=True)
        score_grad = (softmax_full * (prob_grad - row_delta)).astype(jnp.bfloat16)
        query_parts.append(
            jnp.einsum("hqk,khd->qhd", score_grad, keys_row, preferred_element_type=jnp.float32)
            * score_scale
        )
        keys_grad = (
            keys_grad
            + jnp.einsum(
                "hqk,qhd->khd", score_grad, query_block, preferred_element_type=jnp.float32
            )
            * score_scale
        )
    stacked = jnp.stack([jnp.concatenate(query_parts, axis=0), keys_grad, values_grad], axis=1)
    return stacked.astype(jnp.bfloat16)


def after(value, *earlier):
    return lax.optimization_barrier((value,) + earlier)[0]


class Links:
    def __init__(self, mesh):
        self.count = mesh.shape["dp"]
        self.outer = 4 if self.count % 4 == 0 else 1
        self.inner = self.count // self.outer
        self.group = mesh.shape["tensor"]
        self.cores = 2 if self.group % 2 == 0 else 1
        self.chips = self.group // self.cores

    def place(self):
        index = lax.axis_index("dp")
        self.out_at, self.in_at = index // self.inner, index % self.inner
        index = lax.axis_index("tensor")
        self.chip_at, self.core_at = index // self.cores, index % self.cores

    def shift(self, value, over_outer, over_inner):
        pairs = []
        for a in range(self.outer):
            for b in range(self.inner):
                to = (a + over_outer) % self.outer * self.inner + (b + over_inner) % self.inner
                pairs.append((a * self.inner + b, to))
        return lax.ppermute(value, "dp", pairs)

    def turn(self, value, over_chips, over_cores):
        pairs = []
        for a in range(self.chips):
            for b in range(self.cores):
                to = (a + over_chips) % self.chips * self.cores + (b + over_cores) % self.cores
                pairs.append((a * self.cores + b, to))
        return lax.ppermute(value, "tensor", pairs)

    def outer_order(self):
        return sorted(range(1, self.outer), key=lambda k: min(k, self.outer - k))

    def gather(self, shard, gate):
        rows = shard.shape[0]
        full = jnp.zeros((rows * self.count,) + shard.shape[1:], shard.dtype)
        arrived = {0: shard}
        if gate:
            shard = after(shard, *gate)
        for k in self.outer_order():
            arrived[k] = self.shift(shard, k, 0)
        for k, piece in arrived.items():
            for j in range(self.inner):
                part = self.shift(piece, 0, j) if j else piece
                owner = (self.out_at - k) % self.outer * self.inner + (self.in_at - j) % self.inner
                full = lax.dynamic_update_slice_in_dim(full, part, owner * rows, 0)
        return full, [arrived[k] for k in self.outer_order()]

    def reduce(self, partial):
        rows = partial.shape[0] // self.count

        def block(k, j):
            owner = (self.out_at + k) % self.outer * self.inner + (self.in_at + j) % self.inner
            return lax.dynamic_slice_in_dim(partial, owner * rows, rows, 0)

        total = None
        for k in self.outer_order() + [0]:
            sums = block(k, 0).astype(wide)
            for j in range(1, self.inner):
                sums = sums + self.shift(block(k, j), 0, j).astype(wide)
            if k:
                sums = self.shift(sums.astype(low_type), k, 0).astype(wide)
            total = sums if total is None else total + sums
        return total

    def gather_small(self, shard):
        columns = shard.shape[1]
        full = jnp.zeros((shard.shape[0], self.count, columns), shard.dtype)
        for k in range(self.outer):
            for j in range(self.inner):
                part = self.shift(shard, k, j) if k or j else shard
                owner = (self.out_at - k) % self.outer * self.inner + (self.in_at - j) % self.inner
                full = lax.dynamic_update_slice_in_dim(full, part[:, None], owner, 1)
        return full.reshape(shard.shape[0], -1)

    def reduce_small(self, partial):
        split = partial.reshape(partial.shape[0], self.count, -1)
        total = None
        for k in range(self.outer):
            for j in range(self.inner):
                owner = (self.out_at + k) % self.outer * self.inner + (self.in_at + j) % self.inner
                part = lax.dynamic_index_in_dim(split, owner, 1, keepdims=False)
                part = self.shift(part, k, j) if k or j else part
                total = part if total is None else total + part
        for parts, step in ((self.cores, (0, 1)), (self.chips, (1, 0))):
            moving = total
            for _ in range(parts - 1):
                moving = self.turn(moving, *step)
                total = total + moving
        return total

    def own_rows(self, value):
        rows = value.shape[0] // self.group
        return lax.dynamic_slice_in_dim(
            value, (self.core_at * self.chips + self.chip_at) * rows, rows, 0
        )

    def reduce_tensor(self, partial):
        rows = partial.shape[0] // self.cores

        def half(j):
            return lax.dynamic_slice_in_dim(
                partial, (self.core_at + j) % self.cores * rows, rows, 0
            )

        sums = half(0).astype(wide)
        for j in range(1, self.cores):
            sums = sums + self.turn(half(j), 0, j).astype(wide)
        rows = rows // self.chips

        def quarter(values, j):
            return lax.dynamic_slice_in_dim(
                values, (self.chip_at + j) % self.chips * rows, rows, 0
            )

        total = quarter(sums, 0)
        low_sums = sums.astype(low_type)
        for j in range(1, self.chips):
            total = total + self.turn(quarter(low_sums, j), j, 0).astype(wide)
        return total

    def gather_tensor(self, own):
        for parts, at, step in (
            (self.chips, self.chip_at, (1, 0)),
            (self.cores, self.core_at, (0, 1)),
        ):
            rows = own.shape[0]
            full = jnp.zeros((parts * rows,) + own.shape[1:], own.dtype)
            full = lax.dynamic_update_slice_in_dim(full, own, at * rows, 0)
            moving = own
            for j in range(1, parts):
                moving = self.turn(moving, *step)
                full = lax.dynamic_update_slice_in_dim(full, moving, (at - j) % parts * rows, 0)
            own = full
        return own


def adam_update(master, moment, square, gradient, rate_value, decay_value):
    moment_new = beta_first * moment + (1.0 - beta_first) * gradient
    square_new = beta_second * square + (1.0 - beta_second) * gradient * gradient
    fix_first = 1.0 - beta_first**STEP
    fix_second = 1.0 - beta_second**STEP
    direction = moment_new / fix_first / (jnp.sqrt(square_new / fix_second) + adam_epsilon)
    master_new = master - rate_value * (direction + decay_value * master)
    return (master_new, moment_new, square_new)


def dot_low(spec, left, right):
    return jnp.einsum(spec, left, right, preferred_element_type=wide).astype(low_type)


def shards(
    links,
    hidden_in,
    out_cotangent,
    episode_lengths,
    self_generated,
    loss_numerator,
    attend_weights,
    attend_first,
    attend_second,
    attend_average,
    combine_weights,
    combine_first,
    combine_second,
    combine_average,
    expand_weights,
    expand_first,
    expand_second,
    expand_average,
    shrink_weights,
    shrink_first,
    shrink_second,
    shrink_average,
    layernorm_params,
    layernorm_first,
    layernorm_second,
    layernorm_average,
):
    links.place()
    local_tokens, width = hidden_in.shape
    row_count = episode_lengths.shape[0]
    row_length = local_tokens // row_count
    shard_rows, kinds_count, local_width = attend_weights.shape
    head_count = local_width // HEAD_DIM

    norm_values = links.gather_small(layernorm_params.astype(low_type)).astype(wide)
    attend_low = attend_weights.astype(low_type).reshape(shard_rows, kinds_count * local_width)
    combine_low = combine_weights.astype(low_type).T
    expand_low = expand_weights.astype(low_type)
    shrink_low = shrink_weights.astype(low_type).T
    attend_full, gate = links.gather(attend_low, ())
    combine_full, gate_two = links.gather(combine_low, gate[-1:])
    expand_full, gate_three = links.gather(expand_low, gate_two[:1])
    shrink_full, _ = links.gather(shrink_low, gate_three[-1:])

    hidden = hidden_in.astype(wide)
    scaled_one, _ = norm_parts(hidden)
    normed_low = (scaled_one * norm_values[0] + norm_values[1]).astype(low_type)
    projected = dot_low("nd,de->ne", normed_low, attend_full)
    shaped = projected.reshape(row_count, row_length, kinds_count, head_count, HEAD_DIM)
    rows = [
        (shaped[r, :, 0], shaped[r, :, 1], shaped[r, :, 2], segment_ids(episode_lengths[r], row_length))
        for r in range(row_count)
    ]
    forward = [attend_row(row) for row in rows]
    mixed_low = jnp.concatenate(
        [mixed.reshape(row_length, local_width).astype(low_type) for mixed, _ in forward], axis=0
    )
    attended = links.reduce_tensor(dot_low("ne,de->nd", mixed_low, combine_full))
    hidden_own = links.own_rows(hidden_in).astype(wide)
    residual = hidden_own + attended
    scaled_two, inverse_two = norm_parts(residual)
    normed_two_low = links.gather_tensor(
        (scaled_two * norm_values[2] + norm_values[3]).astype(low_type)
    )
    expanded = jnp.einsum("nd,df->nf", normed_two_low, expand_full, preferred_element_type=wide)
    activated, slope = gelu_parts(expanded)
    activated_low = activated.astype(low_type)

    factor = loss_numerator.astype(wide) / (4.0 * (1.0 + self_generated.astype(wide)))
    branch_grad_low = (factor[:, None] * out_cotangent.astype(wide)).astype(low_type)
    out_grad_own = links.own_rows(factor)[:, None] * links.own_rows(out_cotangent).astype(wide)
    shrink_grad = dot_low("nd,nf->df", branch_grad_low, activated_low)
    shrink_sum = links.reduce(shrink_grad).T

    activated_grad = jnp.einsum(
        "nd,df->nf", branch_grad_low, shrink_full, preferred_element_type=wide
    )
    expanded_grad_low = (activated_grad * slope).astype(low_type)
    normed_two_grad = links.reduce_tensor(dot_low("nf,df->nd", expanded_grad_low, expand_full))
    expand_grad = dot_low("nd,nf->df", normed_two_low, expanded_grad_low)
    expand_sum = links.reduce(expand_grad)
    residual_from_norm, gain_two_grad, shift_two_grad = norm_back(
        normed_two_grad, scaled_two, inverse_two, norm_values[2]
    )
    residual_grad = out_grad_own + residual_from_norm
    attended_grad_low = links.gather_tensor(residual_grad.astype(low_type))
    mixed_grad = dot_low("nd,de->ne", attended_grad_low, combine_full)
    combine_grad = dot_low("nd,ne->de", attended_grad_low, mixed_low)
    combine_sum = links.reduce(combine_grad).T
    branch = links.reduce_tensor(dot_low("nf,df->nd", activated_low, shrink_full))
    layer_output = links.gather_tensor((residual + branch).astype(low_type))
    mixed_grad_rows = mixed_grad.reshape(row_count, row_length, head_count, HEAD_DIM)
    projected_grad = jnp.concatenate(
        [
            attend_row_back(row + (kept[1], mixed_grad_rows[r]))
            for r, (row, kept) in enumerate(zip(rows, forward))
        ],
        axis=0,
    ).reshape(local_tokens, kinds_count * local_width)
    attend_grad = dot_low("nd,ne->de", normed_low, projected_grad)
    attend_sum = links.reduce(attend_grad).reshape(attend_weights.shape)
    normed_one_grad = links.reduce_tensor(dot_low("ne,de->nd", projected_grad, attend_full))
    scaled_own, inverse_own = norm_parts(hidden_own)
    hidden_from_norm, gain_one_grad, shift_one_grad = norm_back(
        normed_one_grad, scaled_own, inverse_own, norm_values[0]
    )
    input_gradient = links.gather_tensor((residual_grad + hidden_from_norm).astype(low_type)).astype(
        wide
    )
    norm_sum = links.reduce_small(
        jnp.stack([gain_one_grad, shift_one_grad, gain_two_grad, shift_two_grad])
    )
    kinds = (
        (
            attend_weights,
            attend_first,
            attend_second,
            attend_average,
            attend_sum,
            matrix_rate,
            weight_decay,
        ),
        (
            combine_weights,
            combine_first,
            combine_second,
            combine_average,
            combine_sum,
            matrix_rate,
            weight_decay,
        ),
        (
            expand_weights,
            expand_first,
            expand_second,
            expand_average,
            expand_sum,
            matrix_rate,
            weight_decay,
        ),
        (
            shrink_weights,
            shrink_first,
            shrink_second,
            shrink_average,
            shrink_sum,
            matrix_rate,
            weight_decay,
        ),
        (
            layernorm_params,
            layernorm_first,
            layernorm_second,
            layernorm_average,
            norm_sum,
            norm_rate,
            0.0,
        ),
    )
    results = [layer_output, input_gradient]
    for master, moment, square, average, gradient, rate_value, decay_value in kinds:
        master_new, moment_new, square_new = adam_update(
            master, moment, square, gradient, rate_value, decay_value
        )
        smooth_new = average_decay * average + (1.0 - average_decay) * master_new
        results.extend(
            [master_new, moment_new, square_new, smooth_new, master_new.astype(jnp.bfloat16)]
        )
    return tuple(results)


def solution(mesh):
    placed = (
        P("dp", None),
        P("dp", None),
        P("dp", None),
        P("dp"),
        P("dp"),
        P("dp", None, "tensor"),
        P("dp", None, "tensor"),
        P("dp", None, "tensor"),
        P("dp", None, "tensor"),
        P("tensor", "dp"),
        P("tensor", "dp"),
        P("tensor", "dp"),
        P("tensor", "dp"),
        P("dp", "tensor"),
        P("dp", "tensor"),
        P("dp", "tensor"),
        P("dp", "tensor"),
        P("tensor", "dp"),
        P("tensor", "dp"),
        P("tensor", "dp"),
        P("tensor", "dp"),
        P(None, "dp"),
        P(None, "dp"),
        P(None, "dp"),
        P(None, "dp"),
    )
    return jax.shard_map(
        functools.partial(shards, Links(mesh)),
        mesh=mesh,
        in_specs=placed,
        out_specs=(
            P("dp", None),
            P("dp", None),
            P("dp", None, "tensor"),
            P("dp", None, "tensor"),
            P("dp", None, "tensor"),
            P("dp", None, "tensor"),
            P("dp", None, "tensor"),
            P("tensor", "dp"),
            P("tensor", "dp"),
            P("tensor", "dp"),
            P("tensor", "dp"),
            P("tensor", "dp"),
            P("dp", "tensor"),
            P("dp", "tensor"),
            P("dp", "tensor"),
            P("dp", "tensor"),
            P("dp", "tensor"),
            P("tensor", "dp"),
            P("tensor", "dp"),
            P("tensor", "dp"),
            P("tensor", "dp"),
            P("tensor", "dp"),
            P(None, "dp"),
            P(None, "dp"),
            P(None, "dp"),
            P(None, "dp"),
            P(None, "dp"),
        ),
        check_vma=False,
    )
```

```python
import functools
import math

import jax
import jax.numpy as jnp
from jax import lax
from jax.sharding import PartitionSpec as P

HEAD_DIM = 128
STEP = 10


beta_first = 0.5
beta_second = 0.5
average_decay = 0.5
adam_epsilon = 1e-08
weight_decay = 0.1
matrix_rate = 0.02
norm_rate = 0.2
norm_epsilon = 1e-05
low_type = jnp.bfloat16
wide = jnp.float32


def norm_parts(values):
    center = values - jnp.mean(values, axis=-1, keepdims=True)
    spread = jnp.mean(center * center, axis=-1, keepdims=True)
    inverse = lax.rsqrt(spread + norm_epsilon)
    return center * inverse, inverse


def norm_back(grad, scaled, inverse, gain_row):
    inner = grad * gain_row
    mean_inner = jnp.mean(inner, axis=-1, keepdims=True)
    mean_scaled = jnp.mean(inner * scaled, axis=-1, keepdims=True)
    result = inverse * (inner - mean_inner - scaled * mean_scaled)
    return result, jnp.sum(grad * scaled, axis=0), jnp.sum(grad, axis=0)


def gelu_parts(v):
    scale = math.sqrt(2.0 / math.pi)
    bend = jnp.tanh(scale * (v + 0.044715 * (v * v * v)))
    slope = 0.5 * (1.0 + bend) + 0.5 * v * (1.0 - bend * bend) * scale * (
        1.0 + 3.0 * 0.044715 * (v * v)
    )
    return 0.5 * v * (1.0 + bend), slope


def segment_ids(lengths_row, row_length):
    order = jnp.arange(lengths_row.shape[0], dtype=jnp.int32)
    earlier = order[None, :] <= order[:, None]
    bounds = jnp.sum(jnp.where(earlier, lengths_row[None, :], 0), axis=1)
    places = jnp.arange(row_length, dtype=jnp.int32)
    return jnp.sum((places[:, None] >= bounds[None, :]).astype(jnp.int32), axis=1)


def allowed_mask(segment, first_row, block_rows):
    row_length = segment.shape[0]
    query_places = first_row + jnp.arange(block_rows, dtype=jnp.int32)
    key_places = jnp.arange(row_length, dtype=jnp.int32)
    query_segment = segment[first_row : first_row + block_rows]
    return (query_segment[:, None] == segment[None, :]) & (
        key_places[None, :] <= query_places[:, None]
    )


def attend_row(packed):
    queries, keys_row, values_row, segment = packed
    row_length = queries.shape[0]
    block_rows = min(512, row_length)
    score_scale = HEAD_DIM ** (-0.5)
    out_parts = []
    logsum_parts = []
    for first_row in range(0, row_length, block_rows):
        query_block = queries[first_row : first_row + block_rows]
        allowed = allowed_mask(segment, first_row, block_rows)
        scores = (
            jnp.einsum("qhd,khd->hqk", query_block, keys_row, preferred_element_type=jnp.float32)
            * score_scale
        )
        masked = jnp.where(allowed[None], scores, -1e30)
        row_top = jnp.max(masked, axis=-1, keepdims=True)
        exponent = jnp.exp(masked - row_top)
        row_total = jnp.sum(exponent, axis=-1, keepdims=True)
        softmax_low = (exponent / row_total).astype(jnp.bfloat16)
        out_parts.append(
            jnp.einsum("hqk,khd->qhd", softmax_low, values_row, preferred_element_type=jnp.float32)
        )
        logsum_parts.append((row_top + jnp.log(row_total))[..., 0])
    return (jnp.concatenate(out_parts, axis=0), jnp.concatenate(logsum_parts, axis=1))


def attend_row_back(packed):
    queries, keys_row, values_row, segment, logsum, grad_row = packed
    row_length = queries.shape[0]
    block_rows = min(512, row_length)
    score_scale = HEAD_DIM ** (-0.5)
    keys_grad = jnp.zeros(keys_row.shape, jnp.float32)
    values_grad = jnp.zeros(values_row.shape, jnp.float32)
    query_parts = []
    for first_row in range(0, row_length, block_rows):
        query_block = queries[first_row : first_row + block_rows]
        grad_block = grad_row[first_row : first_row + block_rows]
        allowed = allowed_mask(segment, first_row, block_rows)
        scores = (
            jnp.einsum("qhd,khd->hqk", query_block, keys_row, preferred_element_type=jnp.float32)
            * score_scale
        )
        masked = jnp.where(allowed[None], scores, -1e30)
        softmax_full = jnp.exp(masked - logsum[:, first_row : first_row + block_rows, None])
        softmax_low = softmax_full.astype(jnp.bfloat16)
        values_grad = values_grad + jnp.einsum(
            "hqk,qhd->khd", softmax_low, grad_block, preferred_element_type=jnp.float32
        )
        prob_grad = jnp.einsum(
            "qhd,khd->hqk", grad_block, values_row, preferred_element_type=jnp.float32
        )
        row_delta = jnp.sum(prob_grad * softmax_full, axis=-1, keepdims=True)
        score_grad = (softmax_full * (prob_grad - row_delta)).astype(jnp.bfloat16)
        query_parts.append(
            jnp.einsum("hqk,khd->qhd", score_grad, keys_row, preferred_element_type=jnp.float32)
            * score_scale
        )
        keys_grad = (
            keys_grad
            + jnp.einsum(
                "hqk,qhd->khd", score_grad, query_block, preferred_element_type=jnp.float32
            )
            * score_scale
        )
    stacked = jnp.stack([jnp.concatenate(query_parts, axis=0), keys_grad, values_grad], axis=1)
    return stacked.astype(jnp.bfloat16)


def after(value, earlier):
    return lax.optimization_barrier((value, *earlier))[0] if earlier else value


class Links:
    def __init__(self, mesh):
        self.count = mesh.shape["dp"]
        self.outer = 4 if self.count % 4 == 0 else 1
        self.inner = self.count // self.outer
        self.group = mesh.shape["tensor"]
        self.cores = 2 if self.group % 2 == 0 else 1
        self.chips = self.group // self.cores
        shifts = range(1, self.outer)
        self.near = [k for k in shifts if min(k, self.outer - k) == 1]
        self.far = [k for k in shifts if min(k, self.outer - k) > 1]

    def place(self):
        index = lax.axis_index("dp")
        self.out_at, self.in_at = lax.div(index, self.inner), lax.rem(index, self.inner)
        index = lax.axis_index("tensor")
        self.chip_at, self.core_at = lax.div(index, self.cores), lax.rem(index, self.cores)
        self.last = []

    def owner(self, k, j):
        over_outer = lax.rem(self.out_at + k % self.outer, self.outer)
        over_inner = lax.rem(self.in_at + j % self.inner, self.inner)
        return over_outer * self.inner + over_inner

    def shift(self, value, over_outer, over_inner):
        pairs = []
        for a in range(self.outer):
            for b in range(self.inner):
                to = (a + over_outer) % self.outer * self.inner + (b + over_inner) % self.inner
                pairs.append((a * self.inner + b, to))
        return lax.ppermute(value, "dp", pairs)

    def turn(self, value, over_chips, over_cores):
        pairs = []
        for a in range(self.chips):
            for b in range(self.cores):
                to = (a + over_chips) % self.chips * self.cores + (b + over_cores) % self.cores
                pairs.append((a * self.cores + b, to))
        return lax.ppermute(value, "tensor", pairs)

    def round(self, *moves):
        results = []
        for value, k, j, kept, key in moves:
            kept[key] = self.shift(after(value, self.last), k, j)
            results.append(kept[key])
        self.last = results

    def reduce_small(self, partial):
        total = partial
        for parts, step in ((self.cores, (0, 1)), (self.chips, (1, 0))):
            moving = total
            for _ in range(parts - 1):
                moving = self.turn(moving, *step)
                total = total + moving
        columns = total.shape[1] // self.count
        split = total.reshape(total.shape[0], self.outer, self.inner, columns)

        def column(j):
            at = lax.rem(self.in_at + j, self.inner)
            return lax.dynamic_index_in_dim(split, at, 2, keepdims=False)

        sums = column(0)
        for j in range(1, self.inner):
            sums = sums + self.shift(column(j), 0, j)

        def block(k):
            at = lax.rem(self.out_at + k, self.outer)
            return lax.dynamic_index_in_dim(sums, at, 1, keepdims=False)

        result = block(0)
        for k in range(1, self.outer):
            result = result + self.shift(block(k), k, 0)
        return result

    def own_rows(self, value):
        rows = value.shape[0] // self.group
        return lax.dynamic_slice_in_dim(
            value, (self.core_at * self.chips + self.chip_at) * rows, rows, 0
        )

    def reduce_tensor(self, partial):
        rows = partial.shape[0] // self.cores

        def half(j):
            at = lax.rem(self.core_at + j, self.cores)
            return lax.dynamic_slice_in_dim(partial, at * rows, rows, 0)

        sums = half(0).astype(wide)
        for j in range(1, self.cores):
            sums = sums + self.turn(half(j), 0, j).astype(wide)
        rows = rows // self.chips

        def quarter(values, j):
            at = lax.rem(self.chip_at + j, self.chips)
            return lax.dynamic_slice_in_dim(values, at * rows, rows, 0)

        total = quarter(sums, 0)
        low_sums = sums.astype(low_type)
        for j in range(1, self.chips):
            total = total + self.turn(quarter(low_sums, j), j, 0).astype(wide)
        return total

    def gather_tensor(self, own):
        for parts, at, step in (
            (self.chips, self.chip_at, (1, 0)),
            (self.cores, self.core_at, (0, 1)),
        ):
            rows = own.shape[0]
            full = jnp.zeros((parts * rows,) + own.shape[1:], own.dtype)
            full = lax.dynamic_update_slice_in_dim(full, own, at * rows, 0)
            moving = own
            for j in range(1, parts):
                moving = self.turn(moving, *step)
                place = lax.rem(at + parts - j, parts) * rows
                full = lax.dynamic_update_slice_in_dim(full, moving, place, 0)
            own = full
        return own


class Gather:
    def __init__(self, links, shard):
        self.links = links
        self.held = {(0, 0): shard}

    def outward(self, steps):
        return [(self.held[0, 0], k, 0, self.held, (k, 0)) for k in steps]

    def across(self, steps):
        inner = range(1, self.links.inner)
        return [(self.held[k, 0], 0, j, self.held, (k, j)) for k in steps for j in inner]

    def first(self):
        return self.outward(self.links.near) + self.across([0])

    def second(self):
        return self.outward(self.links.far) + self.across(self.links.near)

    def third(self):
        return self.across(self.links.far)

    def full(self, rows):
        shape = (rows * self.links.count,) + self.held[0, 0].shape[1:]
        result = jnp.zeros(shape, self.held[0, 0].dtype)
        for (k, j), part in self.held.items():
            place = self.links.owner(-k, -j) * rows
            result = lax.dynamic_update_slice_in_dim(result, part[:rows], place, 0)
        return result


class Reduce:
    def __init__(self, links, partial):
        self.links, self.partial = links, partial
        self.rows = partial.shape[0] // links.count
        self.crossed, self.arrived = {}, {}

    def block(self, k, j):
        place = self.links.owner(k, j) * self.rows
        return lax.dynamic_slice_in_dim(self.partial, place, self.rows, 0)

    def across(self, steps):
        inner = range(1, self.links.inner)
        return [(self.block(k, j), 0, j, self.crossed, (k, j)) for k in steps for j in inner]

    def sums(self, k):
        total = self.block(k, 0).astype(wide)
        for j in range(1, self.links.inner):
            total = total + self.crossed[k, j].astype(wide)
        return total

    def outward(self, steps):
        return [(self.sums(k).astype(low_type), k, 0, self.arrived, k) for k in steps]

    def first(self):
        return self.across(self.links.near)

    def second(self):
        return self.outward(self.links.near) + self.across(self.links.far + [0])

    def third(self):
        return self.outward(self.links.far)

    def total(self):
        result = self.sums(0)
        for part in self.arrived.values():
            result = result + part.astype(wide)
        return result


def adam_update(master, moment, square, gradient, rate_value, decay_value):
    moment_new = beta_first * moment + (1.0 - beta_first) * gradient
    square_new = beta_second * square + (1.0 - beta_second) * gradient * gradient
    fix_first = 1.0 - beta_first**STEP
    fix_second = 1.0 - beta_second**STEP
    direction = moment_new / fix_first / (jnp.sqrt(square_new / fix_second) + adam_epsilon)
    master_new = master - rate_value * (direction + decay_value * master)
    return (master_new, moment_new, square_new)


def dot_low(spec, left, right):
    return jnp.einsum(spec, left, right, preferred_element_type=wide).astype(low_type)


def shards(
    links,
    hidden_in,
    out_cotangent,
    episode_lengths,
    self_generated,
    loss_numerator,
    attend_weights,
    attend_first,
    attend_second,
    attend_average,
    combine_weights,
    combine_first,
    combine_second,
    combine_average,
    expand_weights,
    expand_first,
    expand_second,
    expand_average,
    shrink_weights,
    shrink_first,
    shrink_second,
    shrink_average,
    layernorm_params,
    layernorm_first,
    layernorm_second,
    layernorm_average,
):
    links.place()
    local_tokens, width = hidden_in.shape
    row_count = episode_lengths.shape[0]
    row_length = local_tokens // row_count
    shard_rows, kinds_count, local_width = attend_weights.shape
    head_count = local_width // HEAD_DIM

    attend_low = attend_weights.astype(low_type).reshape(shard_rows, kinds_count * local_width)
    combine_low = combine_weights.astype(low_type).T
    expand_low = expand_weights.astype(low_type)
    shrink_low = shrink_weights.astype(low_type).T
    norm_low = layernorm_params.astype(low_type).reshape(1, -1)
    spare = attend_low.shape[1] - norm_low.shape[1]
    norm_low = jnp.pad(norm_low, ((0, 7), (0, spare)))
    attend_move = Gather(links, jnp.concatenate([attend_low, norm_low], axis=0))
    combine_move, expand_move, shrink_move = (
        Gather(links, shard) for shard in (combine_low, expand_low, shrink_low)
    )
    links.round(*attend_move.first())
    links.round(*attend_move.second())
    links.round(*attend_move.third(), *combine_move.first())
    links.round(*combine_move.second())
    links.round(*combine_move.third(), *expand_move.first())
    links.round(*expand_move.second())
    links.round(*expand_move.third(), *shrink_move.first())
    links.round(*shrink_move.second())

    norm_rows = layernorm_params.shape[0]
    norm_values = jnp.zeros((norm_rows, links.count, width // links.count), low_type)
    for (k, j), part in attend_move.held.items():
        part = part[shard_rows, : norm_rows * (width // links.count)].reshape(norm_rows, 1, -1)
        norm_values = lax.dynamic_update_slice_in_dim(norm_values, part, links.owner(-k, -j), 1)
    norm_values = norm_values.reshape(norm_rows, width).astype(wide)
    attend_full = attend_move.full(shard_rows)
    combine_full = combine_move.full(shard_rows)
    expand_full = expand_move.full(shard_rows)

    hidden = hidden_in.astype(wide)
    scaled_one, _ = norm_parts(hidden)
    normed_low = (scaled_one * norm_values[0] + norm_values[1]).astype(low_type)
    projected = dot_low("nd,de->ne", normed_low, attend_full)
    shaped = projected.reshape(row_count, row_length, kinds_count, head_count, HEAD_DIM)
    rows = [
        (shaped[r, :, 0], shaped[r, :, 1], shaped[r, :, 2], segment_ids(episode_lengths[r], row_length))
        for r in range(row_count)
    ]
    forward = [attend_row(row) for row in rows]
    mixed_low = jnp.concatenate(
        [mixed.reshape(row_length, local_width).astype(low_type) for mixed, _ in forward], axis=0
    )
    attended = links.reduce_tensor(dot_low("ne,de->nd", mixed_low, combine_full))
    hidden_own = links.own_rows(hidden_in).astype(wide)
    residual = hidden_own + attended
    scaled_two, inverse_two = norm_parts(residual)
    normed_two_low = links.gather_tensor(
        (scaled_two * norm_values[2] + norm_values[3]).astype(low_type)
    )
    expanded = jnp.einsum("nd,df->nf", normed_two_low, expand_full, preferred_element_type=wide)
    activated, slope = gelu_parts(expanded)
    activated_low = activated.astype(low_type)

    factor = loss_numerator.astype(wide) / (4.0 * (1.0 + self_generated.astype(wide)))
    branch_grad_low = (factor[:, None] * out_cotangent.astype(wide)).astype(low_type)
    out_grad_own = links.own_rows(factor)[:, None] * links.own_rows(out_cotangent).astype(wide)
    shrink_back = Reduce(links, dot_low("nd,nf->df", branch_grad_low, activated_low))
    links.round(*shrink_move.third(), *shrink_back.first())
    shrink_full = shrink_move.full(shard_rows)
    links.round(*shrink_back.second())

    activated_grad = jnp.einsum(
        "nd,df->nf", branch_grad_low, shrink_full, preferred_element_type=wide
    )
    expanded_grad_low = (activated_grad * slope).astype(low_type)
    normed_two_grad = links.reduce_tensor(dot_low("nf,df->nd", expanded_grad_low, expand_full))
    expand_back = Reduce(links, dot_low("nd,nf->df", normed_two_low, expanded_grad_low))
    links.round(*shrink_back.third(), *expand_back.first())
    shrink_sum = shrink_back.total().T
    links.round(*expand_back.second())
    residual_from_norm, gain_two_grad, shift_two_grad = norm_back(
        normed_two_grad, scaled_two, inverse_two, norm_values[2]
    )
    residual_grad = out_grad_own + residual_from_norm
    attended_grad_low = links.gather_tensor(residual_grad.astype(low_type))
    mixed_grad = dot_low("nd,de->ne", attended_grad_low, combine_full)
    combine_back = Reduce(links, dot_low("nd,ne->de", attended_grad_low, mixed_low))
    links.round(*expand_back.third(), *combine_back.first())
    expand_sum = expand_back.total()
    links.round(*combine_back.second())
    mixed_grad_rows = mixed_grad.reshape(row_count, row_length, head_count, HEAD_DIM)
    projected_grad = jnp.concatenate(
        [
            attend_row_back(row + (kept[1], mixed_grad_rows[r]))
            for r, (row, kept) in enumerate(zip(rows, forward))
        ],
        axis=0,
    ).reshape(local_tokens, kinds_count * local_width)
    attend_back = Reduce(links, dot_low("nd,ne->de", normed_low, projected_grad))
    links.round(*combine_back.third(), *attend_back.first())
    combine_sum = combine_back.total().T
    links.round(*attend_back.second())
    links.round(*attend_back.third())
    attend_sum = attend_back.total().reshape(attend_weights.shape)
    normed_one_grad = links.reduce_tensor(dot_low("ne,de->nd", projected_grad, attend_full))
    scaled_own, inverse_own = norm_parts(hidden_own)
    hidden_from_norm, gain_one_grad, shift_one_grad = norm_back(
        normed_one_grad, scaled_own, inverse_own, norm_values[0]
    )
    input_gradient = links.gather_tensor((residual_grad + hidden_from_norm).astype(low_type)).astype(
        wide
    )
    norm_sum = links.reduce_small(
        jnp.stack([gain_one_grad, shift_one_grad, gain_two_grad, shift_two_grad])
    )
    branch = links.reduce_tensor(dot_low("nf,df->nd", activated_low, shrink_full))
    layer_output = links.gather_tensor((residual + branch).astype(low_type))
    kinds = (
        (
            attend_weights,
            attend_first,
            attend_second,
            attend_average,
            attend_sum,
            matrix_rate,
            weight_decay,
        ),
        (
            combine_weights,
            combine_first,
            combine_second,
            combine_average,
            combine_sum,
            matrix_rate,
            weight_decay,
        ),
        (
            expand_weights,
            expand_first,
            expand_second,
            expand_average,
            expand_sum,
            matrix_rate,
            weight_decay,
        ),
        (
            shrink_weights,
            shrink_first,
            shrink_second,
            shrink_average,
            shrink_sum,
            matrix_rate,
            weight_decay,
        ),
        (
            layernorm_params,
            layernorm_first,
            layernorm_second,
            layernorm_average,
            norm_sum,
            norm_rate,
            0.0,
        ),
    )
    results = [layer_output, input_gradient]
    for master, moment, square, average, gradient, rate_value, decay_value in kinds:
        master_new, moment_new, square_new = adam_update(
            master, moment, square, gradient, rate_value, decay_value
        )
        smooth_new = average_decay * average + (1.0 - average_decay) * master_new
        results.extend(
            [master_new, moment_new, square_new, smooth_new, master_new.astype(jnp.bfloat16)]
        )
    return tuple(results)


def solution(mesh):
    placed = (
        P("dp", None),
        P("dp", None),
        P("dp", None),
        P("dp"),
        P("dp"),
        P("dp", None, "tensor"),
        P("dp", None, "tensor"),
        P("dp", None, "tensor"),
        P("dp", None, "tensor"),
        P("tensor", "dp"),
        P("tensor", "dp"),
        P("tensor", "dp"),
        P("tensor", "dp"),
        P("dp", "tensor"),
        P("dp", "tensor"),
        P("dp", "tensor"),
        P("dp", "tensor"),
        P("tensor", "dp"),
        P("tensor", "dp"),
        P("tensor", "dp"),
        P("tensor", "dp"),
        P(None, "dp"),
        P(None, "dp"),
        P(None, "dp"),
        P(None, "dp"),
    )
    return jax.shard_map(
        functools.partial(shards, Links(mesh)),
        mesh=mesh,
        in_specs=placed,
        out_specs=(
            P("dp", None),
            P("dp", None),
            P("dp", None, "tensor"),
            P("dp", None, "tensor"),
            P("dp", None, "tensor"),
            P("dp", None, "tensor"),
            P("dp", None, "tensor"),
            P("tensor", "dp"),
            P("tensor", "dp"),
            P("tensor", "dp"),
            P("tensor", "dp"),
            P("tensor", "dp"),
            P("dp", "tensor"),
            P("dp", "tensor"),
            P("dp", "tensor"),
            P("dp", "tensor"),
            P("dp", "tensor"),
            P("tensor", "dp"),
            P("tensor", "dp"),
            P("tensor", "dp"),
            P("tensor", "dp"),
            P("tensor", "dp"),
            P(None, "dp"),
            P(None, "dp"),
            P(None, "dp"),
            P(None, "dp"),
            P(None, "dp"),
        ),
        check_vma=False,
    )
```

```python
import functools
import math

import jax
import jax.numpy as jnp
from jax import lax
from jax.experimental import pallas as pl
from jax.experimental.pallas import tpu as pltpu
from jax.sharding import PartitionSpec as P

HEAD_DIM = 128
STEP = 10


beta_first = 0.5
beta_second = 0.5
average_decay = 0.5
adam_epsilon = 1e-08
weight_decay = 0.1
matrix_rate = 0.02
norm_rate = 0.2
norm_epsilon = 1e-05
low_type = jnp.bfloat16
wide = jnp.float32


def norm_parts(values):
    center = values - jnp.mean(values, axis=-1, keepdims=True)
    spread = jnp.mean(center * center, axis=-1, keepdims=True)
    inverse = lax.rsqrt(spread + norm_epsilon)
    return center * inverse, inverse


def norm_back(grad, scaled, inverse, gain_row):
    inner = grad * gain_row
    mean_inner = jnp.mean(inner, axis=-1, keepdims=True)
    mean_scaled = jnp.mean(inner * scaled, axis=-1, keepdims=True)
    result = inverse * (inner - mean_inner - scaled * mean_scaled)
    return result, jnp.sum(grad * scaled, axis=0), jnp.sum(grad, axis=0)


def gelu_parts(v):
    scale = math.sqrt(2.0 / math.pi)
    bend = jnp.tanh(scale * (v + 0.044715 * (v * v * v)))
    slope = 0.5 * (1.0 + bend) + 0.5 * v * (1.0 - bend * bend) * scale * (
        1.0 + 3.0 * 0.044715 * (v * v)
    )
    return 0.5 * v * (1.0 + bend), slope


def segment_ids(lengths_row, row_length):
    order = jnp.arange(lengths_row.shape[0], dtype=jnp.int32)
    earlier = order[None, :] <= order[:, None]
    bounds = jnp.sum(jnp.where(earlier, lengths_row[None, :], 0), axis=1)
    places = jnp.arange(row_length, dtype=jnp.int32)
    return jnp.sum((places[:, None] >= bounds[None, :]).astype(jnp.int32), axis=1)


def allowed_mask(segment, first_row, block_rows):
    query_places = first_row + jnp.arange(block_rows, dtype=jnp.int32)
    last_row = first_row + block_rows
    key_places = jnp.arange(last_row, dtype=jnp.int32)
    query_segment = segment[first_row:last_row]
    return (query_segment[:, None] == segment[None, :last_row]) & (
        key_places[None, :] <= query_places[:, None]
    )


def attend_row(packed):
    queries, keys_row, values_row, segment = packed
    row_length = queries.shape[0]
    block_rows = min(512, row_length)
    score_scale = HEAD_DIM ** (-0.5)
    out_parts = []
    logsum_parts = []
    for first_row in range(0, row_length, block_rows):
        query_block = queries[first_row : first_row + block_rows]
        keys_seen = keys_row[: first_row + block_rows]
        values_seen = values_row[: first_row + block_rows]
        allowed = allowed_mask(segment, first_row, block_rows)
        scores = (
            jnp.einsum("qhd,khd->hqk", query_block, keys_seen, preferred_element_type=jnp.float32)
            * score_scale
        )
        masked = jnp.where(allowed[None], scores, -1e30)
        row_top = jnp.max(masked, axis=-1, keepdims=True)
        exponent = jnp.exp(masked - row_top)
        row_total = jnp.sum(exponent, axis=-1, keepdims=True)
        softmax_low = (exponent / row_total).astype(jnp.bfloat16)
        out_parts.append(
            jnp.einsum("hqk,khd->qhd", softmax_low, values_seen, preferred_element_type=jnp.float32)
        )
        logsum_parts.append((row_top + jnp.log(row_total))[..., 0])
    return (jnp.concatenate(out_parts, axis=0), jnp.concatenate(logsum_parts, axis=1))


def attend_row_back(packed):
    queries, keys_row, values_row, segment, logsum, grad_row = packed
    row_length = queries.shape[0]
    block_rows = min(512, row_length)
    score_scale = HEAD_DIM ** (-0.5)
    keys_grad = []
    values_grad = []
    query_parts = []
    for first_row in range(0, row_length, block_rows):
        last_row = first_row + block_rows
        query_block = queries[first_row:last_row]
        grad_block = grad_row[first_row:last_row]
        keys_seen, values_seen = keys_row[:last_row], values_row[:last_row]
        allowed = allowed_mask(segment, first_row, block_rows)
        scores = (
            jnp.einsum("qhd,khd->hqk", query_block, keys_seen, preferred_element_type=jnp.float32)
            * score_scale
        )
        masked = jnp.where(allowed[None], scores, -1e30)
        softmax_full = jnp.exp(masked - logsum[:, first_row:last_row, None])
        softmax_low = softmax_full.astype(jnp.bfloat16)
        values_grad.append(
            jnp.einsum(
                "hqk,qhd->khd", softmax_low, grad_block, preferred_element_type=jnp.float32
            )
        )
        prob_grad = jnp.einsum(
            "qhd,khd->hqk", grad_block, values_seen, preferred_element_type=jnp.float32
        )
        row_delta = jnp.sum(prob_grad * softmax_full, axis=-1, keepdims=True)
        score_grad = (softmax_full * (prob_grad - row_delta)).astype(jnp.bfloat16)
        query_parts.append(
            jnp.einsum("hqk,khd->qhd", score_grad, keys_seen, preferred_element_type=jnp.float32)
            * score_scale
        )
        keys_grad.append(
            jnp.einsum(
                "hqk,qhd->khd", score_grad, query_block, preferred_element_type=jnp.float32
            )
            * score_scale
        )

    def added(parts):
        total = parts[-1]
        for part in parts[:-1]:
            missing = row_length - part.shape[0]
            total = total + jnp.pad(part, ((0, missing), (0, 0), (0, 0)))
        return total

    query_grad = jnp.concatenate(query_parts, axis=0)
    stacked = jnp.stack([query_grad, added(keys_grad), added(values_grad)], axis=1)
    return stacked.astype(jnp.bfloat16)


def after(value, *earlier):
    return lax.optimization_barrier((value, *earlier))[0] if earlier else value


def copy_block(order_ref, in_ref, out_ref):
    out_ref[...] = in_ref[...]


def reorder_columns(values, order):
    rows, width = values.shape
    count = order.shape[0]
    columns = width // count
    if columns % 128:
        blocks = [
            lax.dynamic_slice_in_dim(values, order[i] * columns, columns, 1) for i in range(count)
        ]
        return jnp.concatenate(blocks, axis=1)
    return pl.pallas_call(
        copy_block,
        out_shape=jax.ShapeDtypeStruct(values.shape, values.dtype),
        grid_spec=pltpu.PrefetchScalarGridSpec(
            num_scalar_prefetch=1,
            grid=(count,),
            in_specs=[pl.BlockSpec((rows, columns), lambda i, order_ref: (0, order_ref[i]))],
            out_specs=pl.BlockSpec((rows, columns), lambda i, order_ref: (0, i)),
        ),
        cost_estimate=pl.CostEstimate(
            flops=0, bytes_accessed=2 * values.size * values.dtype.itemsize, transcendentals=0
        ),
    )(order, values)


def turn_block(in_ref, out_ref):
    out_ref[...] = in_ref[...].T


def turned(values):
    rows, width = values.shape
    columns = min(512, width)
    return pl.pallas_call(
        turn_block,
        out_shape=jax.ShapeDtypeStruct((width, rows), values.dtype),
        grid=(width // columns,),
        in_specs=[pl.BlockSpec((rows, columns), lambda i: (0, i))],
        out_specs=pl.BlockSpec((columns, rows), lambda i: (i, 0)),
        cost_estimate=pl.CostEstimate(
            flops=0, bytes_accessed=2 * values.size * values.dtype.itemsize, transcendentals=0
        ),
    )(values)


class Links:
    outer_order = (0, 2, 1, 3)

    def __init__(self, mesh):
        self.count = mesh.shape["dp"]
        self.outer = len(self.outer_order)
        self.inner = self.count // self.outer
        self.group = mesh.shape["tensor"]
        self.cores = 2
        self.chips = self.group // self.cores

    def place(self):
        index = lax.axis_index("dp")
        out_at, in_at = lax.div(index, self.inner), lax.rem(index, self.inner)
        index = lax.axis_index("tensor")
        self.chip_at, self.core_at = lax.div(index, self.cores), lax.rem(index, self.cores)
        order = jnp.asarray(self.outer_order, jnp.int32)
        inner = jnp.arange(self.inner, dtype=jnp.int32)
        self.to_own = (
            (out_at ^ order)[None, :] * self.inner + (in_at ^ inner)[:, None]
        ).reshape(-1)
        outer = jnp.arange(self.outer, dtype=jnp.int32) ^ out_at
        placed = (outer & 1) * 2 + (outer >> 1)
        self.from_own = ((inner ^ in_at)[None, :] * self.outer + placed[:, None]).reshape(-1)
        self.running = []

    def flip(self, value, over_outer, over_inner):
        pairs = []
        for a in range(self.outer):
            for b in range(self.inner):
                to = (a ^ over_outer) * self.inner + (b ^ over_inner)
                pairs.append((a * self.inner + b, to))
        return lax.ppermute(value, "dp", pairs)

    def round(self, moves, carried=()):
        before = self.running
        held = [moved[0] for moved in moves] + [store[key] for store, key in before]
        held = [*lax.optimization_barrier(tuple(held)), *carried]
        for value, (_, over_outer, over_inner, store, key) in zip(held, moves):
            store[key] = self.flip(value, over_outer, over_inner)
        self.running = [moved[3:] for moved in moves]
        return held[len(moves) + len(before) :]

    def turn(self, value, over_chips, over_cores):
        pairs = []
        for a in range(self.chips):
            for b in range(self.cores):
                to = (a + over_chips) % self.chips * self.cores + (b + over_cores) % self.cores
                pairs.append((a * self.cores + b, to))
        return lax.ppermute(value, "tensor", pairs)

    def reduce_small(self, partial):
        total = partial
        for parts, step in ((self.cores, (0, 1)), (self.chips, (1, 0))):
            moving = total
            for _ in range(parts - 1):
                moving = self.turn(moving, *step)
                total = total + moving
        split = total.reshape(total.shape[0], self.inner, self.outer, -1)
        sums = split[:, 0]
        for j in range(1, self.inner):
            sums = sums + self.flip(split[:, j], 0, j)
        half = sums[:, :2] + self.flip(sums[:, 2:], 1, 0)
        return half[:, 0] + self.flip(half[:, 1], 2, 0)

    def own_rows(self, value):
        rows = value.shape[0] // self.group
        return lax.dynamic_slice_in_dim(
            value, (self.core_at * self.chips + self.chip_at) * rows, rows, 0
        )

    def reduce_tensor(self, partial):
        rows = partial.shape[0] // self.cores

        def half(j):
            at = lax.rem(self.core_at + j, self.cores)
            return lax.dynamic_slice_in_dim(partial, at * rows, rows, 0)

        sums = half(0).astype(wide)
        for j in range(1, self.cores):
            sums = sums + self.turn(half(j), 0, j).astype(wide)
        rows = rows // self.chips

        def quarter(values, j):
            at = lax.rem(self.chip_at + j, self.chips)
            return lax.dynamic_slice_in_dim(values, at * rows, rows, 0)

        total = quarter(sums, 0)
        low_sums = sums.astype(low_type)
        for j in range(1, self.chips):
            total = total + self.turn(quarter(low_sums, j), j, 0).astype(wide)
        return total

    def gather_tensor(self, own):
        for parts, at, step in (
            (self.chips, self.chip_at, (1, 0)),
            (self.cores, self.core_at, (0, 1)),
        ):
            rows = own.shape[0]
            full = jnp.zeros((parts * rows,) + own.shape[1:], own.dtype)
            full = lax.dynamic_update_slice_in_dim(full, own, at * rows, 0)
            moving = own
            for j in range(1, parts):
                moving = self.turn(moving, *step)
                place = lax.rem(at + parts - j, parts) * rows
                full = lax.dynamic_update_slice_in_dim(full, moving, place, 0)
            own = full
        return own


class Gather:
    def __init__(self, links, shard):
        self.links = links
        self.held = {"own": shard}

    def far(self):
        return [(self.held["own"], 2, 0, self.held, "far")]

    def near(self):
        pair = jnp.concatenate([self.held["own"], self.held["far"]], axis=0)
        return [(pair, 1, 0, self.held, "near")]

    def across(self, name):
        if name == "pair":
            value = jnp.concatenate([self.held["own"], self.held["far"]], axis=0)
        else:
            value = self.held[name]
        partners = range(1, self.links.inner)
        return [(value, 0, j, self.held, (name, j)) for j in partners]

    def parts(self):
        rows = self.held["own"].shape[0]
        names = [name for name in ("own", "far", "near")]
        for j in range(1, self.links.inner):
            names += [(name, j) for name in ("pair", "own", "far", "near") if (name, j) in self.held]
        for name in names:
            for first in range(0, self.held[name].shape[0], rows):
                yield self.held[name], first

    def full(self, rows):
        return jnp.concatenate([part[first : first + rows] for part, first in self.parts()], axis=0)


class Reduce:
    def __init__(self, links, rows, make):
        self.links, self.rows = links, rows
        size = 2 * rows
        starts = [j * 2 * size for j in range(links.inner)]
        self.away = {j: make(starts[j] + size, starts[j] + 2 * size) for j in range(1, links.inner)}
        self.close = {j: make(starts[j], starts[j] + size) for j in range(1, links.inner)}
        self.mine = make(0, 2 * size)
        self.size = size
        self.held = {}

    def terms(self):
        return [*self.away.values(), *self.close.values(), self.mine]

    def first(self):
        return [(part, 0, j, self.held, ("away", j)) for j, part in self.away.items()]

    def second(self):
        return [(part, 0, j, self.held, ("close", j)) for j, part in self.close.items()]

    def near(self):
        sums = self.mine[self.size :].astype(wide)
        for j in self.away:
            sums = sums + self.held["away", j].astype(wide)
        return [(sums.astype(low_type), 1, 0, self.held, "near")]

    def sums(self, first, last):
        sums = self.mine[first:last].astype(wide) + self.held["near"][first:last].astype(wide)
        for j in self.close:
            sums = sums + self.held["close", j][first:last].astype(wide)
        return sums

    def far(self):
        sums = self.sums(self.rows, self.size)
        return [(sums.astype(low_type), 2, 0, self.held, "far")]

    def total(self):
        return self.sums(0, self.rows) + self.held["far"].astype(wide)


def adam_update(master, moment, square, gradient, rate_value, decay_value):
    moment_new = beta_first * moment + (1.0 - beta_first) * gradient
    square_new = beta_second * square + (1.0 - beta_second) * gradient * gradient
    fix_first = 1.0 - beta_first**STEP
    fix_second = 1.0 - beta_second**STEP
    direction = moment_new / fix_first / (jnp.sqrt(square_new / fix_second) + adam_epsilon)
    master_new = master - rate_value * (direction + decay_value * master)
    return (master_new, moment_new, square_new)


def dot_low(spec, left, right):
    return jnp.einsum(spec, left, right, preferred_element_type=wide).astype(low_type)


def shards(
    links,
    hidden_in,
    out_cotangent,
    episode_lengths,
    self_generated,
    loss_numerator,
    attend_weights,
    attend_first,
    attend_second,
    attend_average,
    combine_weights,
    combine_first,
    combine_second,
    combine_average,
    expand_weights,
    expand_first,
    expand_second,
    expand_average,
    shrink_weights,
    shrink_first,
    shrink_second,
    shrink_average,
    layernorm_params,
    layernorm_first,
    layernorm_second,
    layernorm_average,
):
    links.place()
    local_tokens, width = hidden_in.shape
    row_count = episode_lengths.shape[0]
    row_length = local_tokens // row_count
    shard_rows, kinds_count, local_width = attend_weights.shape
    head_count = local_width // HEAD_DIM

    attend_low = attend_weights.astype(low_type).reshape(shard_rows, kinds_count * local_width)
    combine_low = combine_weights.astype(low_type).T
    expand_low = expand_weights.astype(low_type)
    shrink_low = shrink_weights.astype(low_type).T
    norm_rows, norm_columns = layernorm_params.shape
    norm_low = layernorm_params.astype(low_type).reshape(1, -1)
    spare = attend_low.shape[1] - norm_low.shape[1]
    norm_low = jnp.pad(norm_low, ((0, 7), (0, spare)))
    attend_move = Gather(links, jnp.concatenate([attend_low, norm_low], axis=0))
    combine_move, expand_move, shrink_move = (
        Gather(links, shard) for shard in (combine_low, expand_low, shrink_low)
    )
    links.round(attend_move.far() + combine_move.far() + attend_move.across("own"))
    links.round(attend_move.near() + attend_move.across("far") + combine_move.across("pair"))
    links.round(combine_move.near() + expand_move.far() + attend_move.across("near"))
    links.round(expand_move.near() + combine_move.across("near") + expand_move.across("pair"))

    norm_values = jnp.concatenate(
        [
            part[first + shard_rows, : norm_rows * norm_columns].reshape(norm_rows, -1)
            for part, first in attend_move.parts()
        ],
        axis=1,
    ).astype(wide)
    attend_full = attend_move.full(shard_rows)

    hidden_low = reorder_columns(hidden_in, links.to_own)
    cotangent_low = reorder_columns(out_cotangent, links.to_own)
    scaled_one, _ = norm_parts(hidden_low.astype(wide))
    normed_low = (scaled_one * norm_values[0] + norm_values[1]).astype(low_type)
    projected = dot_low("nd,de->ne", normed_low, attend_full)
    shaped = projected.reshape(row_count, row_length, kinds_count, head_count, HEAD_DIM)
    rows = [
        (shaped[r, :, 0], shaped[r, :, 1], shaped[r, :, 2], segment_ids(episode_lengths[r], row_length))
        for r in range(row_count)
    ]
    forward = [attend_row(row) for row in rows]
    mixed_low = jnp.concatenate(
        [mixed.reshape(row_length, local_width).astype(low_type) for mixed, _ in forward], axis=0
    )
    (mixed_low,) = links.round(shrink_move.far() + expand_move.across("near"), [mixed_low])
    combine_full = combine_move.full(shard_rows)
    attended = links.reduce_tensor(dot_low("ne,de->nd", mixed_low, combine_full))
    hidden_own = links.own_rows(hidden_low).astype(wide)
    residual = hidden_own + attended
    scaled_two, inverse_two = norm_parts(residual)
    normed_two_low = links.gather_tensor(
        (scaled_two * norm_values[2] + norm_values[3]).astype(low_type)
    )
    (normed_two_low,) = links.round(
        shrink_move.near() + shrink_move.across("pair"), [normed_two_low]
    )
    expand_full = expand_move.full(shard_rows)
    expanded = jnp.einsum("nd,df->nf", normed_two_low, expand_full, preferred_element_type=wide)
    activated_low = gelu_parts(expanded)[0].astype(low_type)

    factor = loss_numerator.astype(wide) / (4.0 * (1.0 + self_generated.astype(wide)))
    branch_grad_low = (factor[:, None] * cotangent_low.astype(wide)).astype(low_type)
    out_grad_own = links.own_rows(factor)[:, None] * links.own_rows(cotangent_low).astype(wide)

    def gradient_rows(left, right):
        return lambda first, last: dot_low("nd,nf->df", left[:, first:last], right)

    activated_low, expanded = links.round(shrink_move.across("near"), [activated_low, expanded])
    slope = gelu_parts(expanded)[1]
    shrink_back = Reduce(links, shard_rows, gradient_rows(branch_grad_low, activated_low))
    links.round(shrink_back.first(), shrink_back.terms())

    shrink_full = shrink_move.full(shard_rows)
    activated_grad = jnp.einsum(
        "nd,df->nf", branch_grad_low, shrink_full, preferred_element_type=wide
    )
    expanded_grad_low = (activated_grad * slope).astype(low_type)
    normed_two_partial = dot_low("nf,df->nd", expanded_grad_low, expand_full)
    normed_two_partial, expanded_grad_low = links.round(
        shrink_back.second() + shrink_back.near(), [normed_two_partial, expanded_grad_low]
    )
    normed_two_grad = links.reduce_tensor(normed_two_partial)
    residual_from_norm, gain_two_grad, shift_two_grad = norm_back(
        normed_two_grad, scaled_two, inverse_two, norm_values[2]
    )
    residual_grad = out_grad_own + residual_from_norm
    attended_grad_low = links.gather_tensor(residual_grad.astype(low_type))
    expand_back = Reduce(links, shard_rows, gradient_rows(normed_two_low, expanded_grad_low))
    attended_grad_low, *_ = links.round(
        expand_back.first() + shrink_back.far(), [attended_grad_low, *expand_back.terms()]
    )
    mixed_grad = dot_low("nd,de->ne", attended_grad_low, combine_full)
    combine_back = Reduce(links, shard_rows, gradient_rows(attended_grad_low, mixed_low))
    mixed_grad_rows = mixed_grad.reshape(row_count, row_length, head_count, HEAD_DIM)
    projected_grad = jnp.concatenate(
        [
            attend_row_back(row + (kept[1], mixed_grad_rows[r]))
            for r, (row, kept) in enumerate(zip(rows, forward))
        ],
        axis=0,
    ).reshape(local_tokens, kinds_count * local_width)
    projected_grad, activated_low, *_ = links.round(
        expand_back.second() + expand_back.near(),
        [projected_grad, activated_low, *combine_back.terms()],
    )
    shrink_sum = turned(shrink_back.total())
    attend_back = Reduce(links, shard_rows, gradient_rows(normed_low, projected_grad))
    normed_one_partial = dot_low("ne,de->nd", projected_grad, attend_full)
    links.round(
        combine_back.first() + combine_back.second() + expand_back.far(),
        [normed_one_partial, *attend_back.terms()],
    )
    normed_one_grad = links.reduce_tensor(normed_one_partial)
    scaled_own, inverse_own = norm_parts(hidden_own)
    hidden_from_norm, gain_one_grad, shift_one_grad = norm_back(
        normed_one_grad, scaled_own, inverse_own, norm_values[0]
    )
    input_own = reorder_columns((residual_grad + hidden_from_norm).astype(low_type), links.from_own)
    links.round(attend_back.first() + combine_back.near())
    expand_sum = expand_back.total()
    input_gradient = links.gather_tensor(input_own).astype(wide)
    norm_sum = links.reduce_small(
        jnp.stack([gain_one_grad, shift_one_grad, gain_two_grad, shift_two_grad])
    )
    branch = links.reduce_tensor(dot_low("nf,df->nd", activated_low, shrink_full))
    output_own = reorder_columns((residual + branch).astype(low_type), links.from_own)
    layer_output = links.gather_tensor(output_own)
    links.round(attend_back.second() + attend_back.near() + combine_back.far())
    links.round(attend_back.far())
    combine_sum = turned(combine_back.total())
    attend_sum = attend_back.total().reshape(attend_weights.shape)
    kinds = (
        (
            attend_weights,
            attend_first,
            attend_second,
            attend_average,
            attend_sum,
            matrix_rate,
            weight_decay,
        ),
        (
            combine_weights,
            combine_first,
            combine_second,
            combine_average,
            combine_sum,
            matrix_rate,
            weight_decay,
        ),
        (
            expand_weights,
            expand_first,
            expand_second,
            expand_average,
            expand_sum,
            matrix_rate,
            weight_decay,
        ),
        (
            shrink_weights,
            shrink_first,
            shrink_second,
            shrink_average,
            shrink_sum,
            matrix_rate,
            weight_decay,
        ),
        (
            layernorm_params,
            layernorm_first,
            layernorm_second,
            layernorm_average,
            norm_sum,
            norm_rate,
            0.0,
        ),
    )
    results = [layer_output, input_gradient]
    for master, moment, square, average, gradient, rate_value, decay_value in kinds:
        master_new, moment_new, square_new = adam_update(
            master, moment, square, gradient, rate_value, decay_value
        )
        smooth_new = average_decay * average + (1.0 - average_decay) * master_new
        results.extend(
            [master_new, moment_new, square_new, smooth_new, master_new.astype(jnp.bfloat16)]
        )
    return tuple(results)


def solution(mesh):
    placed = (
        P("dp", None),
        P("dp", None),
        P("dp", None),
        P("dp"),
        P("dp"),
        P("dp", None, "tensor"),
        P("dp", None, "tensor"),
        P("dp", None, "tensor"),
        P("dp", None, "tensor"),
        P("tensor", "dp"),
        P("tensor", "dp"),
        P("tensor", "dp"),
        P("tensor", "dp"),
        P("dp", "tensor"),
        P("dp", "tensor"),
        P("dp", "tensor"),
        P("dp", "tensor"),
        P("tensor", "dp"),
        P("tensor", "dp"),
        P("tensor", "dp"),
        P("tensor", "dp"),
        P(None, "dp"),
        P(None, "dp"),
        P(None, "dp"),
        P(None, "dp"),
    )
    return jax.shard_map(
        functools.partial(shards, Links(mesh)),
        mesh=mesh,
        in_specs=placed,
        out_specs=(
            P("dp", None),
            P("dp", None),
            P("dp", None, "tensor"),
            P("dp", None, "tensor"),
            P("dp", None, "tensor"),
            P("dp", None, "tensor"),
            P("dp", None, "tensor"),
            P("tensor", "dp"),
            P("tensor", "dp"),
            P("tensor", "dp"),
            P("tensor", "dp"),
            P("tensor", "dp"),
            P("dp", "tensor"),
            P("dp", "tensor"),
            P("dp", "tensor"),
            P("dp", "tensor"),
            P("dp", "tensor"),
            P("tensor", "dp"),
            P("tensor", "dp"),
            P("tensor", "dp"),
            P("tensor", "dp"),
            P("tensor", "dp"),
            P(None, "dp"),
            P(None, "dp"),
            P(None, "dp"),
            P(None, "dp"),
            P(None, "dp"),
        ),
        check_vma=False,
    )
```

```python
import functools
import math

import jax
import jax.numpy as jnp
from jax import lax
from jax.experimental import pallas as pl
from jax.experimental.pallas import tpu as pltpu
from jax.sharding import PartitionSpec as P

HEAD_DIM = 128
STEP = 10


beta_first = 0.5
beta_second = 0.5
average_decay = 0.5
adam_epsilon = 1e-08
weight_decay = 0.1
matrix_rate = 0.02
norm_rate = 0.2
norm_epsilon = 1e-05
low_type = jnp.bfloat16
wide = jnp.float32
work_share = 0.1
kernel_memory = 40 * 1024 * 1024


def norm_parts(values):
    center = values - jnp.mean(values, axis=-1, keepdims=True)
    spread = jnp.mean(center * center, axis=-1, keepdims=True)
    inverse = lax.rsqrt(spread + norm_epsilon)
    return center * inverse, inverse


def norm_back(grad, scaled, inverse, gain_row):
    inner = grad * gain_row
    mean_inner = jnp.mean(inner, axis=-1, keepdims=True)
    mean_scaled = jnp.mean(inner * scaled, axis=-1, keepdims=True)
    result = inverse * (inner - mean_inner - scaled * mean_scaled)
    return result, jnp.sum(grad * scaled, axis=0), jnp.sum(grad, axis=0)


def gelu_parts(v):
    scale = math.sqrt(2.0 / math.pi)
    bend = jnp.tanh(scale * (v + 0.044715 * (v * v * v)))
    slope = 0.5 * (1.0 + bend) + 0.5 * v * (1.0 - bend * bend) * scale * (
        1.0 + 3.0 * 0.044715 * (v * v)
    )
    return 0.5 * v * (1.0 + bend), slope


def segment_ids(lengths_row, row_length):
    order = jnp.arange(lengths_row.shape[0], dtype=jnp.int32)
    earlier = order[None, :] <= order[:, None]
    bounds = jnp.sum(jnp.where(earlier, lengths_row[None, :], 0), axis=1)
    places = jnp.arange(row_length, dtype=jnp.int32)
    return jnp.sum((places[:, None] >= bounds[None, :]).astype(jnp.int32), axis=1)


def work(flops, size, exponents=0):
    return pl.CostEstimate(
        flops=int(flops * work_share), bytes_accessed=int(size * work_share), transcendentals=exponents
    )


def tile(size, most):
    return math.gcd(size, most)


product_dims = {
    "nn": (((1,), (0,)), ((), ())),
    "nt": (((1,), (1,)), ((), ())),
    "tn": (((0,), (0,)), ((), ())),
}


def product(left, right, kind):
    return lax.dot_general(left, right, product_dims[kind], preferred_element_type=wide)


class Pieces:
    def __init__(self, parts, rows):
        self.rows = rows
        self.arrays, self.places = [], []
        for array, first in parts:
            if not self.arrays or self.arrays[-1] is not array:
                self.arrays.append(array)
            self.places.append((len(self.arrays) - 1, first))
        self.shape = (rows * len(self.places), self.arrays[0].shape[1])

    def read(self, refs):
        start = 0
        while start < len(self.places):
            which, first = self.places[start]
            last = start + 1
            while (
                last < len(self.places)
                and self.places[last] == (which, first + (last - start) * self.rows)
            ):
                last += 1
            count = (last - start) * self.rows
            yield start * self.rows, count, refs[which][first : first + count, :]
            start = last


def matmul(left, right, kind, body, kinds_out, beside=None, first=0, last=None, most=(512, 512)):
    depth = left.shape[0 if kind == "tn" else 1]
    rows = (last or left.shape[1 if kind == "tn" else 0]) - first
    columns = right.shape[0 if kind == "nt" else 1]
    pieces = right if isinstance(right, Pieces) else None
    rights = pieces.arrays if pieces else [right]
    down, along = tile(math.gcd(rows, first), most[0]), tile(columns, most[1])
    if pieces and kind == "nt":
        down, along = tile(rows, 256), columns
    skip = first // down
    if kind == "tn":
        left_spec = pl.BlockSpec((depth, down), lambda j, i: (0, i + skip))
    else:
        left_spec = pl.BlockSpec((down, depth), lambda j, i: (i + skip, 0))
    if kind == "nt":
        height = [x.shape[0] if pieces else along for x in rights]
        right_specs = [pl.BlockSpec((x, depth), lambda j, i: (j, 0)) for x in height]
    else:
        right_specs = [pl.BlockSpec((x.shape[0], along), lambda j, i: (0, j)) for x in rights]
    out_spec = pl.BlockSpec((down, along), lambda j, i: (i, j))
    more = [] if beside is None else [beside]

    def kernel(left_ref, *refs):
        rights_in, refs = refs[: len(rights)], refs[len(rights) :]
        values = [ref[...] for ref in refs[: len(more)]]
        outs = refs[len(more) :]
        if pieces and kind == "nt":
            for start, count, piece in pieces.read(rights_in):
                made = body(product(left_ref[...], piece, kind), *values)
                for ref, value in zip(outs, made):
                    ref[:, start : start + count] = value.astype(ref.dtype)
            return
        if pieces:
            total = sum(
                product(left_ref[:, start : start + count], piece, kind)
                for start, count, piece in pieces.read(rights_in)
            )
        else:
            total = product(left_ref[...], rights_in[0][...], kind)
        for ref, value in zip(outs, body(total, *values)):
            ref[...] = value.astype(ref.dtype)

    shapes = [jax.ShapeDtypeStruct((rows, columns), kind_out) for kind_out in kinds_out]
    size = sum(x.size * x.dtype.itemsize for x in (left, *rights, *more, *shapes))
    return pl.pallas_call(
        kernel,
        out_shape=shapes,
        grid=(columns // along, rows // down),
        in_specs=[left_spec] + right_specs + [out_spec] * len(more),
        out_specs=[out_spec] * len(shapes),
        compiler_params=pltpu.CompilerParams(vmem_limit_bytes=kernel_memory),
        cost_estimate=work(2 * rows * columns * depth, size),
    )(left, *rights, *more)


def dot_low(left, right, kind, first=0, last=None):
    return matmul(left, right, kind, lambda made: (made,), [low_type], first=first, last=last)[0]


def block_softmax(queries, keys_seen, segment_down, segment_along, first_row):
    scores = product(queries, keys_seen, "nt") * HEAD_DIM ** (-0.5)
    places = lax.broadcasted_iota(jnp.int32, scores.shape, 0) + first_row
    key_places = lax.broadcasted_iota(jnp.int32, scores.shape, 1)
    allowed = (segment_down == segment_along) & (key_places <= places)
    masked = jnp.where(allowed, scores, -1e30)
    exponent = jnp.exp(masked - jnp.max(masked, axis=-1, keepdims=True))
    return exponent * (1.0 / jnp.sum(exponent, axis=-1, keepdims=True))


def attend_kernel(query_ref, key_ref, value_ref, down_ref, along_ref, out_ref):
    row_length = query_ref.shape[0]
    block = tile(row_length, 256)
    for first in range(0, row_length, block):
        last = first + block
        soft = block_softmax(
            query_ref[first:last, :],
            key_ref[:last, :],
            down_ref[first:last, :],
            along_ref[:, :last],
            first,
        )
        made = product(soft.astype(low_type), value_ref[:last, :], "nn")
        out_ref[first:last, :] = made.astype(low_type)


def attend_back_kernel(
    query_ref, key_ref, value_ref, grad_ref, down_ref, along_ref, out_ref, key_sum, value_sum
):
    row_length = query_ref.shape[0]
    block = tile(row_length, 256)
    scale = HEAD_DIM ** (-0.5)
    kind = pl.program_id(2)

    @pl.when(kind == 0)
    def _():
        key_sum[...] = jnp.zeros_like(key_sum)
        value_sum[...] = jnp.zeros_like(value_sum)
        for first in range(0, row_length, block):
            last = first + block
            queries, grads = query_ref[first:last, :], grad_ref[first:last, :]
            soft = block_softmax(
                queries, key_ref[:last, :], down_ref[first:last, :], along_ref[:, :last], first
            )
            value_sum[:last, :] += product(soft.astype(low_type), grads, "tn")
            prob_grad = product(grads, value_ref[:last, :], "nt")
            row_delta = jnp.sum(prob_grad * soft, axis=-1, keepdims=True)
            score_grad = (soft * (prob_grad - row_delta)).astype(low_type)
            made = product(score_grad, key_ref[:last, :], "nn") * scale
            out_ref[first:last, :] = made.astype(low_type)
            key_sum[:last, :] += product(score_grad, queries, "tn")

    @pl.when(kind == 1)
    def _():
        out_ref[...] = (key_sum[...] * scale).astype(low_type)

    @pl.when(kind == 2)
    def _():
        out_ref[...] = value_sum[...].astype(low_type)


def attention(projected, segments, grads=None):
    row_count, row_length = segments.shape
    tokens, columns = projected.shape
    head_count = columns // (3 * HEAD_DIM)
    shape = (row_length, HEAD_DIM)
    down = segments.reshape(tokens, 1)
    along = segments.reshape(row_count, 1, row_length)

    def spec(kind):
        return pl.BlockSpec(shape, lambda r, h, *_: (r, kind * head_count + h))

    in_specs = [spec(0), spec(1), spec(2)] + ([] if grads is None else [spec(0)])
    in_specs += [
        pl.BlockSpec((row_length, 1), lambda r, h, *_: (r, 0)),
        pl.BlockSpec((None, 1, row_length), lambda r, h, *_: (r, 0, 0)),
    ]
    square = 2 * row_count * head_count * row_length * row_length * HEAD_DIM
    params = pltpu.CompilerParams(vmem_limit_bytes=kernel_memory)
    if grads is None:
        return pl.pallas_call(
            attend_kernel,
            out_shape=jax.ShapeDtypeStruct((tokens, head_count * HEAD_DIM), low_type),
            grid=(row_count, head_count),
            in_specs=in_specs,
            out_specs=spec(0),
            compiler_params=params,
            cost_estimate=work(2 * square, projected.size * 4),
        )(projected, projected, projected, down, along)
    return pl.pallas_call(
        attend_back_kernel,
        out_shape=jax.ShapeDtypeStruct(projected.shape, low_type),
        grid=(row_count, head_count, 3),
        in_specs=in_specs,
        out_specs=pl.BlockSpec(shape, lambda r, h, kind: (r, kind * head_count + h)),
        scratch_shapes=[pltpu.VMEM(shape, wide), pltpu.VMEM(shape, wide)],
        compiler_params=params,
        cost_estimate=work(5 * square, projected.size * 6),
    )(projected, projected, projected, grads, down, along)


def after(value, *earlier):
    return lax.optimization_barrier((value, *earlier))[0] if earlier else value


def copy_block(order_ref, in_ref, out_ref):
    out_ref[...] = in_ref[...]


def reorder_columns(values, order):
    rows, width = values.shape
    count = order.shape[0]
    columns = width // count
    if columns % 128:
        blocks = [
            lax.dynamic_slice_in_dim(values, order[i] * columns, columns, 1) for i in range(count)
        ]
        return jnp.concatenate(blocks, axis=1)
    return pl.pallas_call(
        copy_block,
        out_shape=jax.ShapeDtypeStruct(values.shape, values.dtype),
        grid_spec=pltpu.PrefetchScalarGridSpec(
            num_scalar_prefetch=1,
            grid=(count,),
            in_specs=[pl.BlockSpec((rows, columns), lambda i, order_ref: (0, order_ref[i]))],
            out_specs=pl.BlockSpec((rows, columns), lambda i, order_ref: (0, i)),
        ),
        cost_estimate=pl.CostEstimate(
            flops=0, bytes_accessed=2 * values.size * values.dtype.itemsize, transcendentals=0
        ),
    )(order, values)


def turn_block(in_ref, out_ref):
    out_ref[...] = in_ref[...].T


def turned(values):
    rows, width = values.shape
    columns = min(512, width)
    return pl.pallas_call(
        turn_block,
        out_shape=jax.ShapeDtypeStruct((width, rows), values.dtype),
        grid=(width // columns,),
        in_specs=[pl.BlockSpec((rows, columns), lambda i: (0, i))],
        out_specs=pl.BlockSpec((columns, rows), lambda i: (i, 0)),
        cost_estimate=pl.CostEstimate(
            flops=0, bytes_accessed=2 * values.size * values.dtype.itemsize, transcendentals=0
        ),
    )(values)


class Links:
    outer_order = (0, 2, 1, 3)

    def __init__(self, mesh):
        self.count = mesh.shape["dp"]
        self.outer = len(self.outer_order)
        self.inner = self.count // self.outer
        self.group = mesh.shape["tensor"]
        self.cores = 2
        self.chips = self.group // self.cores

    def place(self):
        index = lax.axis_index("dp")
        out_at, in_at = lax.div(index, self.inner), lax.rem(index, self.inner)
        index = lax.axis_index("tensor")
        self.chip_at, self.core_at = lax.div(index, self.cores), lax.rem(index, self.cores)
        order = jnp.asarray(self.outer_order, jnp.int32)
        inner = jnp.arange(self.inner, dtype=jnp.int32)
        self.to_own = (
            (out_at ^ order)[None, :] * self.inner + (in_at ^ inner)[:, None]
        ).reshape(-1)
        outer = jnp.arange(self.outer, dtype=jnp.int32) ^ out_at
        placed = (outer & 1) * 2 + (outer >> 1)
        self.from_own = ((inner ^ in_at)[None, :] * self.outer + placed[:, None]).reshape(-1)
        self.running = []

    def flip(self, value, over_outer, over_inner):
        pairs = []
        for a in range(self.outer):
            for b in range(self.inner):
                to = (a ^ over_outer) * self.inner + (b ^ over_inner)
                pairs.append((a * self.inner + b, to))
        return lax.ppermute(value, "dp", pairs)

    def across(self, over_outer, over_inner):
        return lambda value: self.flip(value, over_outer, over_inner)

    def round(self, make_moves, carried=()):
        held = [store[key] for store, key in self.running]
        held = lax.optimization_barrier((*held, *carried))
        for (store, key), value in zip(self.running, held):
            store[key] = value
        moves = make_moves()
        values = lax.optimization_barrier((*(value for value, *_ in moves), *held))
        for value, (_, send, store, key) in zip(values, moves):
            store[key] = send(value)
        count = len(self.running)
        self.running = [(store, key) for *_, store, key in moves]
        return held[count:]

    def turn(self, value, over_chips, over_cores):
        pairs = []
        for a in range(self.chips):
            for b in range(self.cores):
                to = (a + over_chips) % self.chips * self.cores + (b + over_cores) % self.cores
                pairs.append((a * self.cores + b, to))
        return lax.ppermute(value, "tensor", pairs)

    def sum_tensor(self, total):
        for parts, step in ((self.cores, (0, 1)), (self.chips, (1, 0))):
            moving = total
            for _ in range(parts - 1):
                moving = self.turn(moving, *step)
                total = total + moving
        return total

    def along(self, over_chips, over_cores):
        return lambda value: self.turn(value, over_chips, over_cores)

    def own_rows(self, value):
        rows = value.shape[0] // self.group
        return lax.dynamic_slice_in_dim(
            value, (self.core_at * self.chips + self.chip_at) * rows, rows, 0
        )


class Gather:
    here = ("own", "far", "far0", "far1", "near", "near_own", "near_far")
    there = ("pair", "own", "far", "near", "near0", "near1", "near_own", "near_far")

    def __init__(self, links, shard, step=None):
        self.links = links
        self.step = step or shard.shape[0]
        self.held = {"own": shard}

    def out(self, name, value, distance):
        return [(value, self.links.across(distance, 0), self.held, name)]

    def joined(self, *names):
        return jnp.concatenate([self.held[name] for name in names], axis=0)

    def far(self):
        return self.out("far", self.held["own"], 2)

    def near(self):
        return self.out("near", self.joined("own", "far"), 1)

    def across(self, name, value=None):
        if value is None:
            value = self.joined("own", "far") if name == "pair" else self.held[name]
        partners = range(1, self.links.inner)
        return [(value, self.links.across(0, j), self.held, (name, j)) for j in partners]

    def half(self, name, part):
        value = self.held[name]
        rows = value.shape[0] // 2
        return value[part * rows : (part + 1) * rows]

    def parts(self):
        names = [name for name in self.here if name in self.held]
        for j in range(1, self.links.inner):
            names += [(name, j) for name in self.there if (name, j) in self.held]
        for name in names:
            for first in range(0, self.held[name].shape[0], self.step):
                yield self.held[name], first

    def full(self, rows):
        return Pieces(self.parts(), rows)


class Reduce:
    def __init__(self, links, rows, make):
        self.links, self.rows = links, rows
        size = 2 * rows
        starts = [j * 2 * size for j in range(links.inner)]
        self.away = {j: make(starts[j] + size, starts[j] + 2 * size) for j in range(1, links.inner)}
        self.close = {j: make(starts[j], starts[j] + size) for j in range(1, links.inner)}
        self.mine = make(0, 2 * size)
        self.size = size
        self.held = {}

    def terms(self):
        return [*self.away.values(), *self.close.values(), self.mine]

    def span(self, part, size):
        return (0, size) if part is None else (part * size // 2, (part + 1) * size // 2)

    def move(self, name, j, part, value, send):
        key = (name, j) if part is None else (name, j, part)
        return (value, send, self.held, key)

    def got(self, name, j, first, last, size):
        if (name, j) in self.held:
            return self.held[name, j][first:last]
        if last - first > size // 2:
            halves = [self.held[name, j, 0], self.held[name, j, 1]]
            return jnp.concatenate(halves, axis=0)[first:last]
        part = first // (size // 2)
        skip = part * (size // 2)
        return self.held[name, j, part][first - skip : last - skip]

    def inward(self, name, terms, part):
        first, last = self.span(part, self.size)
        return [
            self.move(name, j, part, term[first:last], self.links.across(0, j))
            for j, term in terms.items()
        ]

    def first(self, part=None):
        return self.inward("away", self.away, part)

    def second(self, part=None):
        return self.inward("close", self.close, part)

    def both(self):
        return [
            (
                jnp.concatenate([self.close[j], self.away[j]], axis=0),
                self.links.across(0, j),
                self.held,
                ("both", j),
            )
            for j in self.away
        ]

    def split_both(self):
        for j in self.away:
            self.held["close", j] = self.held["both", j][: self.size]
            self.held["away", j] = self.held["both", j][self.size :]

    def near(self, part=None):
        first, last = self.span(part, self.size)
        sums = self.mine[self.size + first : self.size + last].astype(wide)
        for j in self.away:
            sums = sums + self.got("away", j, first, last, self.size).astype(wide)
        return [self.move("near", 0, part, sums.astype(low_type), self.links.across(1, 0))]

    def sums(self, first, last):
        sums = self.mine[first:last].astype(wide)
        sums = sums + self.got("near", 0, first, last, self.size).astype(wide)
        for j in self.close:
            sums = sums + self.got("close", j, first, last, self.size).astype(wide)
        return sums

    def far(self, part=None):
        first, last = self.span(part, self.rows)
        sums = self.sums(self.rows + first, self.rows + last).astype(low_type)
        return [self.move("far", 0, part, sums, self.links.across(2, 0))]

    def total(self):
        parts = [None] if ("far", 0) in self.held else [0, 1]
        spans = [self.span(part, self.rows) for part in parts]
        sums = [
            self.sums(*span) + self.got("far", 0, *span, self.rows).astype(wide) for span in spans
        ]
        return jnp.concatenate(sums, axis=0)


class ReduceTensor:
    def __init__(self, links, partial):
        self.links, self.partial = links, partial
        self.held = {}

    def half(self, j):
        rows = self.partial.shape[0] // self.links.cores
        at = lax.rem(self.links.core_at + j, self.links.cores)
        return lax.dynamic_slice_in_dim(self.partial, at * rows, rows, 0)

    def first(self):
        return [(self.half(1), self.links.along(0, 1), self.held, "half")]

    def quarter(self, j):
        links = self.links
        sums = self.half(0).astype(wide) + self.held["half"].astype(wide)
        rows = sums.shape[0] // links.chips
        at = lax.rem(links.chip_at + j, links.chips)
        return lax.dynamic_slice_in_dim(sums, at * rows, rows, 0)

    def second(self):
        return [
            (self.quarter(j).astype(low_type), self.links.along(j, 0), self.held, j)
            for j in range(1, self.links.chips)
        ]

    def second_now(self):
        for value, send, store, key in self.second():
            store[key] = send(value)

    def total(self):
        return self.quarter(0) + sum(
            self.held[j].astype(wide) for j in range(1, self.links.chips)
        )


class GatherTensor:
    def __init__(self, links, own):
        self.links, self.own = links, own
        self.held = {}

    def first(self):
        return [
            (self.own, self.links.along(j, 0), self.held, j) for j in range(1, self.links.chips)
        ]

    def first_now(self):
        for value, send, store, key in self.first():
            store[key] = send(value)

    def terms(self):
        return [self.half()]

    def carry(self, joined, *_):
        self.whole_half = joined

    @staticmethod
    def joined(parts, at):
        count, rows = len(parts), parts[0].shape[0]
        full = jnp.zeros((count * rows,) + parts[0].shape[1:], parts[0].dtype)
        for j, part in enumerate(parts):
            place = lax.rem(at + count - j, count) * rows
            full = lax.dynamic_update_slice_in_dim(full, part, place, 0)
        return full

    whole_half = None

    def half(self):
        links = self.links
        if self.whole_half is not None:
            return self.whole_half
        return self.joined([self.own, *(self.held[j] for j in range(1, links.chips))], links.chip_at)

    def second(self):
        return [(self.half(), self.links.along(0, 1), self.held, "other")]

    def second_now(self):
        for value, send, store, key in self.second():
            store[key] = send(value)

    def full(self):
        return self.joined([self.half(), self.held["other"]], self.links.core_at)


class ReduceSmall:
    def __init__(self, links, partial):
        self.links = links
        self.split = partial.reshape(partial.shape[0], links.inner, links.outer, -1)
        self.held = {}

    def first(self):
        return [
            (self.split[:, j], self.links.across(0, j), self.held, j + 2)
            for j in range(1, self.links.inner)
        ]

    def outward(self):
        self.sums = self.split[:, 0] + sum(
            self.held[j + 2] for j in range(1, self.links.inner)
        )
        order = self.links.outer_order
        return [
            (self.sums[:, i], self.links.across(order[i], 0), self.held, -i)
            for i in range(1, len(order))
        ]

    def total(self):
        return self.sums[:, 0] + sum(self.held[-i] for i in range(1, self.links.outer))


def adam_update(master, moment, square, gradient, rate_value, decay_value):
    moment_new = beta_first * moment + (1.0 - beta_first) * gradient
    square_new = beta_second * square + (1.0 - beta_second) * gradient * gradient
    fix_first = 1.0 - beta_first**STEP
    fix_second = 1.0 - beta_second**STEP
    direction = moment_new / fix_first / (jnp.sqrt(square_new / fix_second) + adam_epsilon)
    master_new = master - rate_value * (direction + decay_value * master)
    return (master_new, moment_new, square_new)


def shards(
    links,
    hidden_in,
    out_cotangent,
    episode_lengths,
    self_generated,
    loss_numerator,
    attend_weights,
    attend_first,
    attend_second,
    attend_average,
    combine_weights,
    combine_first,
    combine_second,
    combine_average,
    expand_weights,
    expand_first,
    expand_second,
    expand_average,
    shrink_weights,
    shrink_first,
    shrink_second,
    shrink_average,
    layernorm_params,
    layernorm_first,
    layernorm_second,
    layernorm_average,
):
    links.place()
    local_tokens, width = hidden_in.shape
    row_count = episode_lengths.shape[0]
    row_length = local_tokens // row_count
    shard_rows, kinds_count, local_width = attend_weights.shape

    attend_low = attend_weights.astype(low_type).reshape(shard_rows, kinds_count * local_width)
    combine_low = combine_weights.astype(low_type).T
    expand_low = expand_weights.astype(low_type)
    shrink_low = shrink_weights.astype(low_type).T
    norm_rows, norm_columns = layernorm_params.shape
    norm_low = layernorm_params.astype(low_type).reshape(1, -1)
    spare = attend_low.shape[1] - norm_low.shape[1]
    norm_low = jnp.pad(norm_low, ((0, 15), (0, spare)))
    attend_move = Gather(links, jnp.concatenate([attend_low, norm_low], axis=0))
    combine_move, expand_move = Gather(links, combine_low), Gather(links, expand_low)
    half_rows = shard_rows // 2
    shrink_move = Gather(links, shrink_low, half_rows)
    moves = (attend_move, combine_move, expand_move, shrink_move)
    hidden_in, out_cotangent, *shards_low = lax.optimization_barrier(
        (hidden_in, out_cotangent, *(move.held["own"] for move in moves))
    )
    for move, shard in zip(moves, shards_low):
        move.held["own"] = shard
    links.round(
        lambda: attend_move.far()
        + combine_move.far()
        + attend_move.across("own")
        + expand_move.across("own")
    )
    hidden_low = reorder_columns(hidden_in, links.to_own)
    cotangent_low = reorder_columns(out_cotangent, links.to_own)
    factor = loss_numerator.astype(wide) / (4.0 * (1.0 + self_generated.astype(wide)))
    branch_grad_low = (factor[:, None] * cotangent_low.astype(wide)).astype(low_type)
    out_grad_own = links.own_rows(factor)[:, None] * links.own_rows(cotangent_low).astype(wide)
    segments = jnp.stack([segment_ids(lengths, row_length) for lengths in episode_lengths])
    scaled_one, _ = norm_parts(hidden_low.astype(wide))
    scaled_one, branch_grad_low, segments = links.round(
        lambda: attend_move.near() + attend_move.across("far") + combine_move.across("pair"),
        [scaled_one, branch_grad_low, segments],
    )
    links.round(lambda: combine_move.near() + expand_move.far() + attend_move.across("near"))

    norm_values = jnp.concatenate(
        [
            part[first + shard_rows, : norm_rows * norm_columns].reshape(norm_rows, -1)
            for part, first in attend_move.parts()
        ],
        axis=1,
    ).astype(wide)
    normed_low = (scaled_one * norm_values[0] + norm_values[1]).astype(low_type)

    (normed_low,) = links.round(
        lambda: expand_move.near() + combine_move.across("near") + expand_move.across("far"),
        [normed_low],
    )
    attend_full = attend_move.full(shard_rows)
    projected = dot_low(normed_low, attend_full, "nn")
    mixed_low = attention(projected, segments)
    combine_full = combine_move.full(shard_rows)
    attended = ReduceTensor(links, dot_low(mixed_low, combine_full, "nt"))

    links.round(
        lambda: attended.first()
        + shrink_move.out("far0", shrink_move.half("own", 0), 2)
        + expand_move.across("near0", expand_move.half("near", 0)),
        [attended.partial],
    )
    hidden_own = links.own_rows(hidden_low).astype(wide)
    links.round(
        lambda: attended.second()
        + shrink_move.out("far1", shrink_move.half("own", 1), 2)
        + expand_move.across("near1", expand_move.half("near", 1))
    )
    residual = hidden_own + attended.total()
    scaled_two, inverse_two = norm_parts(residual)
    normed_two = GatherTensor(
        links, (scaled_two * norm_values[2] + norm_values[3]).astype(low_type)
    )
    (normed_two.own,) = links.round(
        lambda: normed_two.first()
        + shrink_move.out("near_own", shrink_move.held["own"], 1)
        + shrink_move.across("own"),
        [normed_two.own],
    )
    links.round(
        lambda: normed_two.second()
        + shrink_move.out("near_far", shrink_move.joined("far0", "far1"), 1)
        + shrink_move.across("far", shrink_move.joined("far0", "far1"))
    )
    links.round(lambda: shrink_move.across("near_own") + shrink_move.across("near_far"))
    normed_two_low = normed_two.full()
    expand_full = expand_move.full(shard_rows)
    expanded, activated_low = matmul(
        normed_two_low,
        expand_full,
        "nn",
        lambda made: (made, gelu_parts(made)[0]),
        [wide, low_type],
    )

    def gradient_rows(left, right):
        return lambda first, last: dot_low(left, right, "tn", first, last)

    shrink_back = Reduce(links, shard_rows, gradient_rows(branch_grad_low, activated_low))

    expanded, activated_low, *_ = links.round(
        shrink_back.first, [expanded, activated_low, *shrink_back.terms()]
    )
    shrink_full = shrink_move.full(half_rows)
    (expanded_grad_low,) = matmul(
        branch_grad_low,
        shrink_full,
        "nn",
        lambda made, before: (made * gelu_parts(before)[1],),
        [low_type],
        expanded,
    )
    normed_two_back = ReduceTensor(links, dot_low(expanded_grad_low, expand_full, "nt"))

    normed_two_back.partial, expanded_grad_low, activated_low = links.round(
        lambda: normed_two_back.first() + shrink_back.second(1) + shrink_back.near(1),
        [normed_two_back.partial, expanded_grad_low, activated_low],
    )
    expand_back = Reduce(links, shard_rows, gradient_rows(normed_two_low, expanded_grad_low))
    links.round(
        lambda: normed_two_back.second() + shrink_back.second(0) + shrink_back.near(0),
        [*expand_back.away.values()],
    )
    residual_from_norm, gain_two_grad, shift_two_grad = norm_back(
        normed_two_back.total(), scaled_two, inverse_two, norm_values[2]
    )
    residual_grad = out_grad_own + residual_from_norm
    attended_grad = GatherTensor(links, residual_grad.astype(low_type))

    attended_grad.own, activated_low = links.round(
        lambda: attended_grad.first() + expand_back.first(1) + shrink_back.far(1),
        [attended_grad.own, activated_low],
    )
    branch = ReduceTensor(links, dot_low(activated_low, shrink_full, "nt"))
    links.round(
        lambda: attended_grad.second()
        + branch.first()
        + expand_back.first(0)
        + shrink_back.far(0),
        [branch.partial],
    )
    links.round(
        lambda: branch.second() + expand_back.second() + expand_back.near(),
        expand_back.terms(),
    )
    attended_grad_low = attended_grad.full()
    mixed_grad = dot_low(attended_grad_low, combine_full, "nn")
    projected_grad = attention(projected, segments, mixed_grad)
    combine_back = Reduce(links, shard_rows, gradient_rows(attended_grad_low, mixed_low))
    attend_back = Reduce(links, shard_rows, gradient_rows(normed_low, projected_grad))
    normed_one_back = ReduceTensor(links, dot_low(projected_grad, attend_full, "nt"))

    shrink_back.mine, *_ = links.round(
        lambda: normed_one_back.first() + combine_back.both() + expand_back.far(1),
        [shrink_back.mine, normed_one_back.partial, *attend_back.terms(), *combine_back.terms()],
    )
    output = GatherTensor(
        links,
        reorder_columns((residual + branch.total()).astype(low_type), links.from_own),
    )
    combine_back.split_both()
    links.round(
        lambda: normed_one_back.second()
        + attend_back.first()
        + combine_back.near()
        + expand_back.far(0)
    )
    shrink_sum = turned(shrink_back.total())
    scaled_own, inverse_own = norm_parts(hidden_own)
    links.round(
        lambda: output.first() + attend_back.second() + attend_back.near() + combine_back.far(),
        [output.own],
    )
    hidden_from_norm, gain_one_grad, shift_one_grad = norm_back(
        normed_one_back.total(), scaled_own, inverse_own, norm_values[0]
    )
    input_own = reorder_columns((residual_grad + hidden_from_norm).astype(low_type), links.from_own)
    input_back = GatherTensor(links, input_own)
    input_back.first_now()
    norm_grads = ReduceSmall(
        links,
        links.sum_tensor(jnp.stack([gain_one_grad, shift_one_grad, gain_two_grad, shift_two_grad])),
    )
    for value, send, store, key in norm_grads.first():
        store[key] = send(value)
    input_half = input_back.terms()

    expand_back.mine, *input_half = links.round(
        lambda: input_back.second() + output.second() + attend_back.far(),
        [expand_back.mine, *input_half],
    )
    expand_sum = expand_back.total()
    combine_sum = turned(combine_back.total())
    input_back.carry(*input_half)
    layer_output = output.full()
    input_gradient = input_back.full().astype(wide)
    (input_gradient, layer_output) = links.round(norm_grads.outward, [input_gradient, layer_output])
    norm_sum = norm_grads.total()
    attend_sum = attend_back.total().reshape(attend_weights.shape)
    kinds = (
        (
            attend_weights,
            attend_first,
            attend_second,
            attend_average,
            attend_sum,
            matrix_rate,
            weight_decay,
        ),
        (
            combine_weights,
            combine_first,
            combine_second,
            combine_average,
            combine_sum,
            matrix_rate,
            weight_decay,
        ),
        (
            expand_weights,
            expand_first,
            expand_second,
            expand_average,
            expand_sum,
            matrix_rate,
            weight_decay,
        ),
        (
            shrink_weights,
            shrink_first,
            shrink_second,
            shrink_average,
            shrink_sum,
            matrix_rate,
            weight_decay,
        ),
        (
            layernorm_params,
            layernorm_first,
            layernorm_second,
            layernorm_average,
            norm_sum,
            norm_rate,
            0.0,
        ),
    )
    results = [layer_output, input_gradient]
    for master, moment, square, average, gradient, rate_value, decay_value in kinds:
        master_new, moment_new, square_new = adam_update(
            master, moment, square, gradient, rate_value, decay_value
        )
        smooth_new = average_decay * average + (1.0 - average_decay) * master_new
        results.extend(
            [master_new, moment_new, square_new, smooth_new, master_new.astype(jnp.bfloat16)]
        )
    return tuple(results)


def solution(mesh):
    placed = (
        P("dp", None),
        P("dp", None),
        P("dp", None),
        P("dp"),
        P("dp"),
        P("dp", None, "tensor"),
        P("dp", None, "tensor"),
        P("dp", None, "tensor"),
        P("dp", None, "tensor"),
        P("tensor", "dp"),
        P("tensor", "dp"),
        P("tensor", "dp"),
        P("tensor", "dp"),
        P("dp", "tensor"),
        P("dp", "tensor"),
        P("dp", "tensor"),
        P("dp", "tensor"),
        P("tensor", "dp"),
        P("tensor", "dp"),
        P("tensor", "dp"),
        P("tensor", "dp"),
        P(None, "dp"),
        P(None, "dp"),
        P(None, "dp"),
        P(None, "dp"),
    )
    return jax.shard_map(
        functools.partial(shards, Links(mesh)),
        mesh=mesh,
        in_specs=placed,
        out_specs=(
            P("dp", None),
            P("dp", None),
            P("dp", None, "tensor"),
            P("dp", None, "tensor"),
            P("dp", None, "tensor"),
            P("dp", None, "tensor"),
            P("dp", None, "tensor"),
            P("tensor", "dp"),
            P("tensor", "dp"),
            P("tensor", "dp"),
            P("tensor", "dp"),
            P("tensor", "dp"),
            P("dp", "tensor"),
            P("dp", "tensor"),
            P("dp", "tensor"),
            P("dp", "tensor"),
            P("dp", "tensor"),
            P("tensor", "dp"),
            P("tensor", "dp"),
            P("tensor", "dp"),
            P("tensor", "dp"),
            P("tensor", "dp"),
            P(None, "dp"),
            P(None, "dp"),
            P(None, "dp"),
            P(None, "dp"),
            P(None, "dp"),
        ),
        check_vma=False,
    )
```

```python
import functools
import math

import jax
import jax.numpy as jnp
from jax import lax
from jax.experimental import pallas as pl
from jax.experimental.pallas import tpu as pltpu
from jax.sharding import PartitionSpec as P

HEAD_DIM = 128
STEP = 10


beta_first = 0.5
beta_second = 0.5
average_decay = 0.5
adam_epsilon = 1e-08
weight_decay = 0.1
matrix_rate = 0.02
norm_rate = 0.2
norm_epsilon = 1e-05
low_type = jnp.bfloat16
wide = jnp.float32
work_share = 0.1
kernel_memory = 40 * 1024 * 1024


def norm_parts(values):
    center = values - jnp.mean(values, axis=-1, keepdims=True)
    spread = jnp.mean(center * center, axis=-1, keepdims=True)
    inverse = lax.rsqrt(spread + norm_epsilon)
    return center * inverse, inverse


def norm_back(grad, scaled, inverse, gain_row):
    inner = grad * gain_row
    mean_inner = jnp.mean(inner, axis=-1, keepdims=True)
    mean_scaled = jnp.mean(inner * scaled, axis=-1, keepdims=True)
    result = inverse * (inner - mean_inner - scaled * mean_scaled)
    return result, jnp.sum(grad * scaled, axis=0), jnp.sum(grad, axis=0)


def gelu_parts(v):
    scale = math.sqrt(2.0 / math.pi)
    bend = jnp.tanh(scale * (v + 0.044715 * (v * v * v)))
    slope = 0.5 * (1.0 + bend) + 0.5 * v * (1.0 - bend * bend) * scale * (
        1.0 + 3.0 * 0.044715 * (v * v)
    )
    return 0.5 * v * (1.0 + bend), slope


def segment_ids(lengths_row, row_length):
    order = jnp.arange(lengths_row.shape[0], dtype=jnp.int32)
    earlier = order[None, :] <= order[:, None]
    bounds = jnp.sum(jnp.where(earlier, lengths_row[None, :], 0), axis=1)
    places = jnp.arange(row_length, dtype=jnp.int32)
    return jnp.sum((places[:, None] >= bounds[None, :]).astype(jnp.int32), axis=1)


def work(flops, size, exponents=0):
    return pl.CostEstimate(
        flops=int(flops * work_share), bytes_accessed=int(size * work_share), transcendentals=exponents
    )


def tile(size, most):
    return math.gcd(size, most)


product_dims = {
    "nn": (((1,), (0,)), ((), ())),
    "nt": (((1,), (1,)), ((), ())),
    "tn": (((0,), (0,)), ((), ())),
}


def product(left, right, kind):
    return lax.dot_general(left, right, product_dims[kind], preferred_element_type=wide)


class Pieces:
    def __init__(self, parts, rows):
        self.rows = rows
        self.arrays, self.places = [], []
        for array, first in parts:
            if not self.arrays or self.arrays[-1] is not array:
                self.arrays.append(array)
            self.places.append((len(self.arrays) - 1, first))
        self.shape = (rows * len(self.places), self.arrays[0].shape[1])

    def read(self, refs):
        start = 0
        while start < len(self.places):
            which, first = self.places[start]
            last = start + 1
            while (
                last < len(self.places)
                and self.places[last] == (which, first + (last - start) * self.rows)
            ):
                last += 1
            count = (last - start) * self.rows
            yield start * self.rows, count, refs[which][first : first + count, :]
            start = last


def matmul(left, right, kind, body, kinds_out, beside=None, first=0, last=None, most=(512, 512)):
    depth = left.shape[0 if kind == "tn" else 1]
    rows = (last or left.shape[1 if kind == "tn" else 0]) - first
    columns = right.shape[0 if kind == "nt" else 1]
    pieces = right if isinstance(right, Pieces) else None
    rights = pieces.arrays if pieces else [right]
    down, along = tile(math.gcd(rows, first), most[0]), tile(columns, most[1])
    if pieces and kind == "nt":
        down, along = tile(rows, 256), columns
    skip = first // down
    if kind == "tn":
        left_spec = pl.BlockSpec((depth, down), lambda j, i: (0, i + skip))
    else:
        left_spec = pl.BlockSpec((down, depth), lambda j, i: (i + skip, 0))
    if kind == "nt":
        height = [x.shape[0] if pieces else along for x in rights]
        right_specs = [pl.BlockSpec((x, depth), lambda j, i: (j, 0)) for x in height]
    else:
        right_specs = [pl.BlockSpec((x.shape[0], along), lambda j, i: (0, j)) for x in rights]
    out_spec = pl.BlockSpec((down, along), lambda j, i: (i, j))
    more = [] if beside is None else [beside]

    def kernel(left_ref, *refs):
        rights_in, refs = refs[: len(rights)], refs[len(rights) :]
        values = [ref[...] for ref in refs[: len(more)]]
        outs = refs[len(more) :]
        if pieces and kind == "nt":
            for start, count, piece in pieces.read(rights_in):
                made = body(product(left_ref[...], piece, kind), *values)
                for ref, value in zip(outs, made):
                    ref[:, start : start + count] = value.astype(ref.dtype)
            return
        if pieces:
            total = sum(
                product(left_ref[:, start : start + count], piece, kind)
                for start, count, piece in pieces.read(rights_in)
            )
        else:
            total = product(left_ref[...], rights_in[0][...], kind)
        for ref, value in zip(outs, body(total, *values)):
            ref[...] = value.astype(ref.dtype)

    shapes = [jax.ShapeDtypeStruct((rows, columns), kind_out) for kind_out in kinds_out]
    size = sum(x.size * x.dtype.itemsize for x in (left, *rights, *more, *shapes))
    return pl.pallas_call(
        kernel,
        out_shape=shapes,
        grid=(columns // along, rows // down),
        in_specs=[left_spec] + right_specs + [out_spec] * len(more),
        out_specs=[out_spec] * len(shapes),
        compiler_params=pltpu.CompilerParams(vmem_limit_bytes=kernel_memory),
        cost_estimate=work(2 * rows * columns * depth, size),
    )(left, *rights, *more)


def dot_low(left, right, kind, first=0, last=None):
    return matmul(left, right, kind, lambda made: (made,), [low_type], first=first, last=last)[0]


def block_softmax(queries, keys_seen, segment_down, segment_along, first_row):
    scores = product(queries, keys_seen, "nt") * HEAD_DIM ** (-0.5)
    places = lax.broadcasted_iota(jnp.int32, scores.shape, 0) + first_row
    key_places = lax.broadcasted_iota(jnp.int32, scores.shape, 1)
    allowed = (segment_down == segment_along) & (key_places <= places)
    masked = jnp.where(allowed, scores, -1e30)
    exponent = jnp.exp(masked - jnp.max(masked, axis=-1, keepdims=True))
    return exponent * (1.0 / jnp.sum(exponent, axis=-1, keepdims=True))


def attend_kernel(query_ref, key_ref, value_ref, down_ref, along_ref, out_ref):
    row_length = query_ref.shape[0]
    block = tile(row_length, 256)
    for first in range(0, row_length, block):
        last = first + block
        soft = block_softmax(
            query_ref[first:last, :],
            key_ref[:last, :],
            down_ref[first:last, :],
            along_ref[:, :last],
            first,
        )
        made = product(soft.astype(low_type), value_ref[:last, :], "nn")
        out_ref[first:last, :] = made.astype(low_type)


def attend_back_kernel(
    query_ref, key_ref, value_ref, grad_ref, down_ref, along_ref, out_ref, key_sum, value_sum
):
    row_length = query_ref.shape[0]
    block = tile(row_length, 256)
    scale = HEAD_DIM ** (-0.5)
    kind = pl.program_id(2)

    @pl.when(kind == 0)
    def _():
        key_sum[...] = jnp.zeros_like(key_sum)
        value_sum[...] = jnp.zeros_like(value_sum)
        for first in range(0, row_length, block):
            last = first + block
            queries, grads = query_ref[first:last, :], grad_ref[first:last, :]
            soft = block_softmax(
                queries, key_ref[:last, :], down_ref[first:last, :], along_ref[:, :last], first
            )
            value_sum[:last, :] += product(soft.astype(low_type), grads, "tn")
            prob_grad = product(grads, value_ref[:last, :], "nt")
            row_delta = jnp.sum(prob_grad * soft, axis=-1, keepdims=True)
            score_grad = (soft * (prob_grad - row_delta)).astype(low_type)
            made = product(score_grad, key_ref[:last, :], "nn") * scale
            out_ref[first:last, :] = made.astype(low_type)
            key_sum[:last, :] += product(score_grad, queries, "tn")

    @pl.when(kind == 1)
    def _():
        out_ref[...] = (key_sum[...] * scale).astype(low_type)

    @pl.when(kind == 2)
    def _():
        out_ref[...] = value_sum[...].astype(low_type)


def attention(projected, segments, grads=None):
    row_count, row_length = segments.shape
    tokens, columns = projected.shape
    head_count = columns // (3 * HEAD_DIM)
    shape = (row_length, HEAD_DIM)
    down = segments.reshape(tokens, 1)
    along = segments.reshape(row_count, 1, row_length)

    def spec(kind):
        return pl.BlockSpec(shape, lambda r, h, *_: (r, kind * head_count + h))

    in_specs = [spec(0), spec(1), spec(2)] + ([] if grads is None else [spec(0)])
    in_specs += [
        pl.BlockSpec((row_length, 1), lambda r, h, *_: (r, 0)),
        pl.BlockSpec((None, 1, row_length), lambda r, h, *_: (r, 0, 0)),
    ]
    square = 2 * row_count * head_count * row_length * row_length * HEAD_DIM
    params = pltpu.CompilerParams(vmem_limit_bytes=kernel_memory)
    if grads is None:
        return pl.pallas_call(
            attend_kernel,
            out_shape=jax.ShapeDtypeStruct((tokens, head_count * HEAD_DIM), low_type),
            grid=(row_count, head_count),
            in_specs=in_specs,
            out_specs=spec(0),
            compiler_params=params,
            cost_estimate=work(2 * square, projected.size * 4),
        )(projected, projected, projected, down, along)
    return pl.pallas_call(
        attend_back_kernel,
        out_shape=jax.ShapeDtypeStruct(projected.shape, low_type),
        grid=(row_count, head_count, 3),
        in_specs=in_specs,
        out_specs=pl.BlockSpec(shape, lambda r, h, kind: (r, kind * head_count + h)),
        scratch_shapes=[pltpu.VMEM(shape, wide), pltpu.VMEM(shape, wide)],
        compiler_params=params,
        cost_estimate=work(5 * square, projected.size * 6),
    )(projected, projected, projected, grads, down, along)


def after(value, *earlier):
    return lax.optimization_barrier((value, *earlier))[0] if earlier else value


def copy_block(order_ref, in_ref, out_ref):
    out_ref[...] = in_ref[...]


def reorder_columns(values, order):
    rows, width = values.shape
    count = order.shape[0]
    columns = width // count
    if columns % 128:
        blocks = [
            lax.dynamic_slice_in_dim(values, order[i] * columns, columns, 1) for i in range(count)
        ]
        return jnp.concatenate(blocks, axis=1)
    return pl.pallas_call(
        copy_block,
        out_shape=jax.ShapeDtypeStruct(values.shape, values.dtype),
        grid_spec=pltpu.PrefetchScalarGridSpec(
            num_scalar_prefetch=1,
            grid=(count,),
            in_specs=[pl.BlockSpec((rows, columns), lambda i, order_ref: (0, order_ref[i]))],
            out_specs=pl.BlockSpec((rows, columns), lambda i, order_ref: (0, i)),
        ),
        cost_estimate=pl.CostEstimate(
            flops=0, bytes_accessed=2 * values.size * values.dtype.itemsize, transcendentals=0
        ),
    )(order, values)


def turn_block(in_ref, out_ref):
    out_ref[...] = in_ref[...].T


def turned(values):
    rows, width = values.shape
    columns = min(512, width)
    return pl.pallas_call(
        turn_block,
        out_shape=jax.ShapeDtypeStruct((width, rows), values.dtype),
        grid=(width // columns,),
        in_specs=[pl.BlockSpec((rows, columns), lambda i: (0, i))],
        out_specs=pl.BlockSpec((columns, rows), lambda i: (i, 0)),
        cost_estimate=pl.CostEstimate(
            flops=0, bytes_accessed=2 * values.size * values.dtype.itemsize, transcendentals=0
        ),
    )(values)


def adam_kernel(rate_value, decay_value, terms, *refs):
    gradient = sum(ref[...].astype(wide) for ref in refs[:terms])
    states, outs = refs[terms : terms + 4], refs[terms + 4 :]
    width = states[0].shape[2]
    for j in range(states[0].shape[1]):
        master, moment, square, average = (ref[:, j, :] for ref in states)
        made = adam_update(
            master,
            moment,
            square,
            gradient[:, j * width : (j + 1) * width],
            rate_value,
            decay_value,
        )
        smooth = average_decay * average + (1.0 - average_decay) * made[0]
        for ref, value in zip(outs, (*made, smooth)):
            ref[:, j, :] = value


def adam_planes(terms, states, rate_value, decay_value):
    rows, planes, width = states[0].shape
    block = tile(rows, 32)
    flat = pl.BlockSpec((block, planes * width), lambda i: (i, 0))
    deep = pl.BlockSpec((block, planes, width), lambda i: (i, 0, 0))
    size = sum(x.size * x.dtype.itemsize for x in terms) + 32 * states[0].size
    return pl.pallas_call(
        functools.partial(adam_kernel, rate_value, decay_value, len(terms)),
        out_shape=[jax.ShapeDtypeStruct(states[0].shape, wide)] * 4,
        grid=(rows // block,),
        in_specs=[flat] * len(terms) + [deep] * 4,
        out_specs=[deep] * 4,
        compiler_params=pltpu.CompilerParams(vmem_limit_bytes=kernel_memory),
        cost_estimate=pl.CostEstimate(flops=0, bytes_accessed=size, transcendentals=0),
    )(*terms, *states)


class Links:
    outer_order = (0, 2, 1, 3)

    def __init__(self, mesh):
        self.count = mesh.shape["dp"]
        self.outer = len(self.outer_order)
        self.inner = self.count // self.outer
        self.group = mesh.shape["tensor"]
        self.cores = 2
        self.chips = self.group // self.cores

    def place(self):
        index = lax.axis_index("dp")
        out_at, in_at = lax.div(index, self.inner), lax.rem(index, self.inner)
        index = lax.axis_index("tensor")
        self.chip_at, self.core_at = lax.div(index, self.cores), lax.rem(index, self.cores)
        order = jnp.asarray(self.outer_order, jnp.int32)
        inner = jnp.arange(self.inner, dtype=jnp.int32)
        self.to_own = (
            (out_at ^ order)[None, :] * self.inner + (in_at ^ inner)[:, None]
        ).reshape(-1)
        outer = jnp.arange(self.outer, dtype=jnp.int32) ^ out_at
        placed = (outer & 1) * 2 + (outer >> 1)
        self.from_own = ((inner ^ in_at)[None, :] * self.outer + placed[:, None]).reshape(-1)
        self.running = []

    def flip(self, value, over_outer, over_inner):
        pairs = []
        for a in range(self.outer):
            for b in range(self.inner):
                to = (a ^ over_outer) * self.inner + (b ^ over_inner)
                pairs.append((a * self.inner + b, to))
        return lax.ppermute(value, "dp", pairs)

    def across(self, over_outer, over_inner):
        return lambda value: self.flip(value, over_outer, over_inner)

    def round(self, make_moves, carried=()):
        held = [store[key] for store, key in self.running]
        held = lax.optimization_barrier((*held, *carried))
        for (store, key), value in zip(self.running, held):
            store[key] = value
        moves = make_moves()
        for value, send, store, key in moves:
            store[key] = send(after(value, *held))
        count = len(self.running)
        self.running = [(store, key) for *_, store, key in moves]
        return held[count:]

    def turn(self, value, over_chips, over_cores):
        pairs = []
        for a in range(self.chips):
            for b in range(self.cores):
                to = (a + over_chips) % self.chips * self.cores + (b + over_cores) % self.cores
                pairs.append((a * self.cores + b, to))
        return lax.ppermute(value, "tensor", pairs)

    def sum_tensor(self, total):
        for parts, step in ((self.cores, (0, 1)), (self.chips, (1, 0))):
            moving = total
            for _ in range(parts - 1):
                moving = self.turn(moving, *step)
                total = total + moving
        return total

    def along(self, over_chips, over_cores):
        return lambda value: self.turn(value, over_chips, over_cores)

    def own_rows(self, value):
        rows = value.shape[0] // self.group
        return lax.dynamic_slice_in_dim(
            value, (self.core_at * self.chips + self.chip_at) * rows, rows, 0
        )


class Gather:
    here = ("own", "far", "far0", "far1", "near", "near_own", "near_far")
    there = ("pair", "own", "far", "near", "near0", "near1", "near_own", "near_far")

    def __init__(self, links, shard, step=None):
        self.links = links
        self.step = step or shard.shape[0]
        self.held = {"own": shard}

    def out(self, name, value, distance):
        return [(value, self.links.across(distance, 0), self.held, name)]

    def joined(self, *names):
        return jnp.concatenate([self.held[name] for name in names], axis=0)

    def far(self):
        return self.out("far", self.held["own"], 2)

    def near(self):
        return self.out("near", self.joined("own", "far"), 1)

    def across(self, name, value=None):
        if value is None:
            value = self.joined("own", "far") if name == "pair" else self.held[name]
        partners = range(1, self.links.inner)
        return [(value, self.links.across(0, j), self.held, (name, j)) for j in partners]

    def half(self, name, part):
        value = self.held[name]
        rows = value.shape[0] // 2
        return value[part * rows : (part + 1) * rows]

    def parts(self):
        names = [name for name in self.here if name in self.held]
        for j in range(1, self.links.inner):
            names += [(name, j) for name in self.there if (name, j) in self.held]
        for name in names:
            for first in range(0, self.held[name].shape[0], self.step):
                yield self.held[name], first

    def full(self, rows):
        return Pieces(self.parts(), rows)


class Reduce:
    def __init__(self, links, rows, make, joint=False):
        self.links, self.rows = links, rows
        size = 2 * rows
        starts = [j * 2 * size for j in range(links.inner)]
        self.whole = {}
        if joint:
            self.whole = {j: make(starts[j], starts[j] + 2 * size) for j in range(1, links.inner)}
            self.away = {j: made[size:] for j, made in self.whole.items()}
            self.close = {j: made[:size] for j, made in self.whole.items()}
        else:
            ends = [start + 2 * size for start in starts]
            self.away = {j: make(starts[j] + size, ends[j]) for j in range(1, links.inner)}
            self.close = {j: make(starts[j], starts[j] + size) for j in range(1, links.inner)}
        self.mine = make(0, 2 * size)
        self.size = size
        self.held = {}

    def terms(self):
        if self.whole:
            return [*self.whole.values(), self.mine]
        return [*self.away.values(), *self.close.values(), self.mine]

    def span(self, part, size):
        return (0, size) if part is None else (part * size // 2, (part + 1) * size // 2)

    def move(self, name, j, part, value, send):
        key = (name, j) if part is None else (name, j, part)
        return (value, send, self.held, key)

    def got(self, name, j, first, last, size):
        if (name, j) in self.held:
            return self.held[name, j][first:last]
        if last - first > size // 2:
            halves = [self.held[name, j, 0], self.held[name, j, 1]]
            return jnp.concatenate(halves, axis=0)[first:last]
        part = first // (size // 2)
        skip = part * (size // 2)
        return self.held[name, j, part][first - skip : last - skip]

    def inward(self, name, terms, part):
        first, last = self.span(part, self.size)
        return [
            self.move(name, j, part, term[first:last], self.links.across(0, j))
            for j, term in terms.items()
        ]

    def first(self, part=None):
        return self.inward("away", self.away, part)

    def second(self, part=None):
        return self.inward("close", self.close, part)

    def both(self):
        return [
            (made, self.links.across(0, j), self.held, ("both", j))
            for j, made in self.whole.items()
        ]

    def split_both(self):
        for j in self.away:
            self.held["close", j] = self.held["both", j][: self.size]
            self.held["away", j] = self.held["both", j][self.size :]

    def near(self, part=None):
        first, last = self.span(part, self.size)
        sums = self.mine[self.size + first : self.size + last].astype(wide)
        for j in self.away:
            sums = sums + self.got("away", j, first, last, self.size).astype(wide)
        return [self.move("near", 0, part, sums.astype(low_type), self.links.across(1, 0))]

    def sums(self, first, last):
        sums = self.mine[first:last].astype(wide)
        sums = sums + self.got("near", 0, first, last, self.size).astype(wide)
        for j in self.close:
            sums = sums + self.got("close", j, first, last, self.size).astype(wide)
        return sums

    def far(self, part=None):
        first, last = self.span(part, self.rows)
        sums = self.sums(self.rows + first, self.rows + last).astype(low_type)
        return [self.move("far", 0, part, sums, self.links.across(2, 0))]

    def last_terms(self):
        near = self.held["near", 0]
        return [self.mine, near, *(self.held["close", j] for j in self.close), self.held["far", 0]]

    def total(self):
        parts = [None] if ("far", 0) in self.held else [0, 1]
        spans = [self.span(part, self.rows) for part in parts]
        sums = [
            self.sums(*span) + self.got("far", 0, *span, self.rows).astype(wide) for span in spans
        ]
        return jnp.concatenate(sums, axis=0)


class ReduceTensor:
    def __init__(self, links, partial):
        self.links, self.partial = links, partial
        self.held = {}

    def part(self, over_chips, over_cores):
        links = self.links
        rows = self.partial.shape[0] // links.group
        chip = lax.rem(links.chip_at + over_chips, links.chips)
        core = lax.rem(links.core_at + over_cores, links.cores)
        return lax.dynamic_slice_in_dim(self.partial, (core * links.chips + chip) * rows, rows, 0)

    def first(self):
        return [
            (self.part(j, 1), self.links.along(0, 1), self.held, ("half", j))
            for j in reversed(range(self.links.chips))
        ]

    def sums(self, j):
        return self.part(j, 0).astype(wide) + self.held["half", j].astype(wide)

    def second(self):
        return [
            (self.sums(j).astype(low_type), self.links.along(j, 0), self.held, j)
            for j in range(1, self.links.chips)
        ]

    def total(self):
        return self.sums(0) + sum(
            self.held[j].astype(wide) for j in range(1, self.links.chips)
        )


class GatherTensor:
    def __init__(self, links, own):
        self.links, self.own = links, own
        self.held = {}

    def first(self):
        chips = range(1, self.links.chips)
        return [(self.own, self.links.along(j, 0), self.held, (j, 0)) for j in chips] + [
            (self.own, self.links.along(0, 1), self.held, (0, 1))
        ]

    def second(self):
        chips = range(1, self.links.chips)
        return [
            (self.held[j, 0], self.links.along(0, 1), self.held, (j, 1)) for j in chips
        ]

    def now(self, moves):
        for value, send, store, key in moves:
            store[key] = send(value)

    def full(self):
        links = self.links
        rows = self.own.shape[0]
        full = jnp.zeros((links.group * rows,) + self.own.shape[1:], self.own.dtype)
        for (j, k), part in {(0, 0): self.own, **self.held}.items():
            chip = lax.rem(links.chip_at + links.chips - j, links.chips)
            core = lax.rem(links.core_at + k, links.cores)
            full = lax.dynamic_update_slice_in_dim(
                full, part, (core * links.chips + chip) * rows, 0
            )
        return full


class ReduceSmall:
    def __init__(self, links, partial):
        self.links = links
        self.split = partial.reshape(partial.shape[0], links.inner, links.outer, -1)
        self.held = {}

    def first(self):
        return [
            (self.split[:, j], self.links.across(0, j), self.held, j + 2)
            for j in range(1, self.links.inner)
        ]

    def outward(self):
        self.sums = self.split[:, 0] + sum(
            self.held[j + 2] for j in range(1, self.links.inner)
        )
        order = self.links.outer_order
        return [
            (self.sums[:, i], self.links.across(order[i], 0), self.held, -i)
            for i in range(1, len(order))
        ]

    def total(self):
        return self.sums[:, 0] + sum(self.held[-i] for i in range(1, self.links.outer))


def adam_update(master, moment, square, gradient, rate_value, decay_value):
    moment_new = beta_first * moment + (1.0 - beta_first) * gradient
    square_new = beta_second * square + (1.0 - beta_second) * gradient * gradient
    fix_first = 1.0 - beta_first**STEP
    fix_second = 1.0 - beta_second**STEP
    direction = moment_new / fix_first / (jnp.sqrt(square_new / fix_second) + adam_epsilon)
    master_new = master - rate_value * (direction + decay_value * master)
    return (master_new, moment_new, square_new)


def shards(
    links,
    hidden_in,
    out_cotangent,
    episode_lengths,
    self_generated,
    loss_numerator,
    attend_weights,
    attend_first,
    attend_second,
    attend_average,
    combine_weights,
    combine_first,
    combine_second,
    combine_average,
    expand_weights,
    expand_first,
    expand_second,
    expand_average,
    shrink_weights,
    shrink_first,
    shrink_second,
    shrink_average,
    layernorm_params,
    layernorm_first,
    layernorm_second,
    layernorm_average,
):
    links.place()
    local_tokens, width = hidden_in.shape
    row_count = episode_lengths.shape[0]
    row_length = local_tokens // row_count
    shard_rows, kinds_count, local_width = attend_weights.shape

    attend_low = attend_weights.astype(low_type).reshape(shard_rows, kinds_count * local_width)
    combine_low = combine_weights.astype(low_type).T
    expand_low = expand_weights.astype(low_type)
    shrink_low = shrink_weights.astype(low_type).T
    norm_rows, norm_columns = layernorm_params.shape
    norm_low = layernorm_params.astype(low_type).reshape(1, -1)
    spare = attend_low.shape[1] - norm_low.shape[1]
    norm_low = jnp.pad(norm_low, ((0, 15), (0, spare)))
    attend_move = Gather(links, jnp.concatenate([attend_low, norm_low], axis=0))
    combine_move, expand_move = Gather(links, combine_low), Gather(links, expand_low)
    half_rows = shard_rows // 2
    shrink_move = Gather(links, shrink_low, half_rows)
    later = (combine_move, shrink_move)
    links.round(lambda: attend_move.far() + attend_move.across("own"))
    hidden_low = reorder_columns(hidden_in, links.to_own)
    cotangent_low = reorder_columns(out_cotangent, links.to_own)
    factor = loss_numerator.astype(wide) / (4.0 * (1.0 + self_generated.astype(wide)))
    branch_grad_low = (factor[:, None] * cotangent_low.astype(wide)).astype(low_type)
    out_grad_own = links.own_rows(factor)[:, None] * links.own_rows(cotangent_low).astype(wide)
    segments = jnp.stack([segment_ids(lengths, row_length) for lengths in episode_lengths])
    scaled_one, _ = norm_parts(hidden_low.astype(wide))
    scaled_one, branch_grad_low, segments, *own = links.round(
        lambda: attend_move.near()
        + combine_move.far()
        + attend_move.across("far")
        + expand_move.across("own"),
        [scaled_one, branch_grad_low, segments, *(move.held["own"] for move in later)],
    )
    for move, shard in zip(later, own):
        move.held["own"] = shard
    links.round(
        lambda: combine_move.near()
        + expand_move.far()
        + attend_move.across("near")
        + combine_move.across("pair")
    )

    norm_values = jnp.concatenate(
        [
            part[first + shard_rows, : norm_rows * norm_columns].reshape(norm_rows, -1)
            for part, first in attend_move.parts()
        ],
        axis=1,
    ).astype(wide)
    normed_low = (scaled_one * norm_values[0] + norm_values[1]).astype(low_type)

    (normed_low,) = links.round(
        lambda: expand_move.near() + combine_move.across("near") + expand_move.across("far"),
        [normed_low],
    )
    attend_full = attend_move.full(shard_rows)
    projected = dot_low(normed_low, attend_full, "nn")
    mixed_low = attention(projected, segments)
    combine_full = combine_move.full(shard_rows)
    attended = ReduceTensor(links, dot_low(mixed_low, combine_full, "nt"))

    links.round(
        lambda: attended.first()
        + shrink_move.out("far0", shrink_move.half("own", 0), 2)
        + expand_move.across("near0", expand_move.half("near", 0)),
        [attended.partial],
    )
    hidden_own = links.own_rows(hidden_low).astype(wide)
    links.round(
        lambda: attended.second()
        + shrink_move.out("far1", shrink_move.half("own", 1), 2)
        + expand_move.across("near1", expand_move.half("near", 1))
    )
    residual = hidden_own + attended.total()
    scaled_two, inverse_two = norm_parts(residual)
    normed_two = GatherTensor(
        links, (scaled_two * norm_values[2] + norm_values[3]).astype(low_type)
    )
    (normed_two.own,) = links.round(
        lambda: normed_two.first()
        + shrink_move.out("near_own", shrink_move.held["own"], 1)
        + shrink_move.across("own"),
        [normed_two.own],
    )
    links.round(
        lambda: normed_two.second()
        + shrink_move.out("near_far", shrink_move.joined("far0", "far1"), 1)
        + shrink_move.across("far", shrink_move.joined("far0", "far1"))
    )
    links.round(lambda: shrink_move.across("near_own") + shrink_move.across("near_far"))
    normed_two_low = normed_two.full()
    expand_full = expand_move.full(shard_rows)
    expanded, activated_low = matmul(
        normed_two_low,
        expand_full,
        "nn",
        lambda made: (made, gelu_parts(made)[0]),
        [wide, low_type],
    )

    def gradient_rows(left, right):
        return lambda first, last: dot_low(left, right, "tn", first, last)

    shrink_back = Reduce(links, shard_rows, gradient_rows(branch_grad_low, activated_low))

    expanded, activated_low, *_ = links.round(
        shrink_back.first, [expanded, activated_low, *shrink_back.terms()]
    )
    shrink_full = shrink_move.full(half_rows)
    (expanded_grad_low,) = matmul(
        branch_grad_low,
        shrink_full,
        "nn",
        lambda made, before: (made * gelu_parts(before)[1],),
        [low_type],
        expanded,
    )
    normed_two_back = ReduceTensor(links, dot_low(expanded_grad_low, expand_full, "nt"))

    normed_two_back.partial, expanded_grad_low, activated_low = links.round(
        lambda: normed_two_back.first() + shrink_back.second(1) + shrink_back.near(1),
        [normed_two_back.partial, expanded_grad_low, activated_low],
    )
    expand_back = Reduce(links, shard_rows, gradient_rows(normed_two_low, expanded_grad_low))
    links.round(
        lambda: normed_two_back.second() + shrink_back.second(0) + shrink_back.near(0),
        expand_back.terms(),
    )
    residual_from_norm, gain_two_grad, shift_two_grad = norm_back(
        normed_two_back.total(), scaled_two, inverse_two, norm_values[2]
    )
    residual_grad = out_grad_own + residual_from_norm
    attended_grad = GatherTensor(links, residual_grad.astype(low_type))

    attended_grad.own, activated_low = links.round(
        lambda: attended_grad.first() + expand_back.first(1) + shrink_back.far(1),
        [attended_grad.own, activated_low],
    )
    branch = ReduceTensor(links, dot_low(activated_low, shrink_full, "nt"))
    links.round(
        lambda: attended_grad.second()
        + branch.first()
        + expand_back.first(0)
        + shrink_back.far(0),
        [branch.partial],
    )
    attended_grad_low = attended_grad.full()
    mixed_grad = dot_low(attended_grad_low, combine_full, "nn")
    projected_grad = attention(projected, segments, mixed_grad)
    (projected_grad,) = links.round(
        lambda: branch.second() + expand_back.second() + expand_back.near(), [projected_grad]
    )
    combine_back = Reduce(links, shard_rows, gradient_rows(attended_grad_low, mixed_low), True)
    attend_back = Reduce(links, shard_rows, gradient_rows(normed_low, projected_grad))
    normed_one_back = ReduceTensor(links, dot_low(projected_grad, attend_full, "nt"))

    shrink_back.mine, *_ = links.round(
        lambda: normed_one_back.first() + combine_back.both() + expand_back.far(1),
        [shrink_back.mine, normed_one_back.partial, *attend_back.terms(), *combine_back.terms()],
    )
    output = GatherTensor(
        links,
        reorder_columns((residual + branch.total()).astype(low_type), links.from_own),
    )
    combine_back.split_both()
    links.round(
        lambda: normed_one_back.second()
        + attend_back.first()
        + combine_back.near()
        + expand_back.far(0)
    )
    shrink_sum = turned(shrink_back.total())
    scaled_own, inverse_own = norm_parts(hidden_own)
    hidden_from_norm, gain_one_grad, shift_one_grad = norm_back(
        normed_one_back.total(), scaled_own, inverse_own, norm_values[0]
    )
    input_own = reorder_columns((residual_grad + hidden_from_norm).astype(low_type), links.from_own)
    input_back = GatherTensor(links, input_own)
    input_back.own, output.own = links.round(
        lambda: attend_back.second()
        + attend_back.near()
        + input_back.first()[:-1]
        + combine_back.far(),
        [input_own, output.own],
    )
    output.now(output.first()[:-1])
    norm_terms = jnp.stack([gain_one_grad, shift_one_grad, gain_two_grad, shift_two_grad])

    (expand_back.mine, norm_terms) = links.round(
        lambda: input_back.first()[-1:] + attend_back.far(), [expand_back.mine, norm_terms]
    )
    input_back.now(input_back.second())
    output.now(output.first()[-1:])
    output.now(output.second())
    norm_grads = ReduceSmall(links, links.sum_tensor(norm_terms))
    for value, send, store, key in norm_grads.first():
        store[key] = send(value)
    expand_sum = expand_back.total()
    combine_sum = turned(combine_back.total())
    layer_output = output.full()
    input_gradient = input_back.full().astype(wide)
    (input_gradient, layer_output, norm_grads.split) = links.round(
        norm_grads.outward, [input_gradient, layer_output, norm_grads.split]
    )
    norm_sum = norm_grads.total()
    attend_new = adam_planes(
        attend_back.last_terms(),
        (attend_weights, attend_first, attend_second, attend_average),
        matrix_rate,
        weight_decay,
    )
    kinds = (
        (
            combine_weights,
            combine_first,
            combine_second,
            combine_average,
            combine_sum,
            matrix_rate,
            weight_decay,
        ),
        (
            expand_weights,
            expand_first,
            expand_second,
            expand_average,
            expand_sum,
            matrix_rate,
            weight_decay,
        ),
        (
            shrink_weights,
            shrink_first,
            shrink_second,
            shrink_average,
            shrink_sum,
            matrix_rate,
            weight_decay,
        ),
        (
            layernorm_params,
            layernorm_first,
            layernorm_second,
            layernorm_average,
            norm_sum,
            norm_rate,
            0.0,
        ),
    )
    results = [layer_output, input_gradient, *attend_new, attend_new[0].astype(low_type)]
    for master, moment, square, average, gradient, rate_value, decay_value in kinds:
        master_new, moment_new, square_new = adam_update(
            master, moment, square, gradient, rate_value, decay_value
        )
        smooth_new = average_decay * average + (1.0 - average_decay) * master_new
        results.extend(
            [master_new, moment_new, square_new, smooth_new, master_new.astype(jnp.bfloat16)]
        )
    return tuple(results)


def solution(mesh):
    placed = (
        P("dp", None),
        P("dp", None),
        P("dp", None),
        P("dp"),
        P("dp"),
        P("dp", None, "tensor"),
        P("dp", None, "tensor"),
        P("dp", None, "tensor"),
        P("dp", None, "tensor"),
        P("tensor", "dp"),
        P("tensor", "dp"),
        P("tensor", "dp"),
        P("tensor", "dp"),
        P("dp", "tensor"),
        P("dp", "tensor"),
        P("dp", "tensor"),
        P("dp", "tensor"),
        P("tensor", "dp"),
        P("tensor", "dp"),
        P("tensor", "dp"),
        P("tensor", "dp"),
        P(None, "dp"),
        P(None, "dp"),
        P(None, "dp"),
        P(None, "dp"),
    )
    return jax.shard_map(
        functools.partial(shards, Links(mesh)),
        mesh=mesh,
        in_specs=placed,
        out_specs=(
            P("dp", None),
            P("dp", None),
            P("dp", None, "tensor"),
            P("dp", None, "tensor"),
            P("dp", None, "tensor"),
            P("dp", None, "tensor"),
            P("dp", None, "tensor"),
            P("tensor", "dp"),
            P("tensor", "dp"),
            P("tensor", "dp"),
            P("tensor", "dp"),
            P("tensor", "dp"),
            P("dp", "tensor"),
            P("dp", "tensor"),
            P("dp", "tensor"),
            P("dp", "tensor"),
            P("dp", "tensor"),
            P("tensor", "dp"),
            P("tensor", "dp"),
            P("tensor", "dp"),
            P("tensor", "dp"),
            P("tensor", "dp"),
            P(None, "dp"),
            P(None, "dp"),
            P(None, "dp"),
            P(None, "dp"),
            P(None, "dp"),
        ),
        check_vma=False,
    )
```

```python
import functools
import math

import jax
import jax.numpy as jnp
from jax import lax
from jax.experimental import pallas as pl
from jax.experimental.pallas import tpu as pltpu
from jax.sharding import PartitionSpec as P

HEAD_DIM = 128
STEP = 10


beta_first = 0.5
beta_second = 0.5
average_decay = 0.5
adam_epsilon = 1e-08
weight_decay = 0.1
matrix_rate = 0.02
norm_rate = 0.2
norm_epsilon = 1e-05
low_type = jnp.bfloat16
wide = jnp.float32
work_share = 0.1
kernel_memory = 23 * 1024 * 1024


def norm_parts(values):
    center = values - jnp.mean(values, axis=-1, keepdims=True)
    spread = jnp.mean(center * center, axis=-1, keepdims=True)
    inverse = lax.rsqrt(spread + norm_epsilon)
    return center * inverse, inverse


def norm_back(grad, scaled, inverse, gain_row):
    inner = grad * gain_row
    mean_inner = jnp.mean(inner, axis=-1, keepdims=True)
    mean_scaled = jnp.mean(inner * scaled, axis=-1, keepdims=True)
    result = inverse * (inner - mean_inner - scaled * mean_scaled)
    return result, jnp.sum(grad * scaled, axis=0), jnp.sum(grad, axis=0)


def gelu_parts(v):
    scale = math.sqrt(2.0 / math.pi)
    bend = jnp.tanh(scale * (v + 0.044715 * (v * v * v)))
    slope = 0.5 * (1.0 + bend) + 0.5 * v * (1.0 - bend * bend) * scale * (
        1.0 + 3.0 * 0.044715 * (v * v)
    )
    return 0.5 * v * (1.0 + bend), slope


def segment_ids(lengths_row, row_length):
    order = jnp.arange(lengths_row.shape[0], dtype=jnp.int32)
    earlier = order[None, :] <= order[:, None]
    bounds = jnp.sum(jnp.where(earlier, lengths_row[None, :], 0), axis=1)
    places = jnp.arange(row_length, dtype=jnp.int32)
    return jnp.sum((places[:, None] >= bounds[None, :]).astype(jnp.int32), axis=1)


def work(flops, size, exponents=0):
    return pl.CostEstimate(
        flops=int(flops * work_share), bytes_accessed=int(size * work_share), transcendentals=exponents
    )


def tile(size, most):
    return math.gcd(size, most)


product_dims = {
    "nn": (((1,), (0,)), ((), ())),
    "nt": (((1,), (1,)), ((), ())),
    "tn": (((0,), (0,)), ((), ())),
}


def product(left, right, kind):
    return lax.dot_general(left, right, product_dims[kind], preferred_element_type=wide)


class Pieces:
    def __init__(self, parts, rows):
        self.rows = rows
        self.arrays, self.places = [], []
        for array, first in parts:
            if not self.arrays or self.arrays[-1] is not array:
                self.arrays.append(array)
            self.places.append((len(self.arrays) - 1, first))
        self.shape = (rows * len(self.places), self.arrays[0].shape[1])

    def read(self, refs):
        start = 0
        while start < len(self.places):
            which, first = self.places[start]
            last = start + 1
            while (
                last < len(self.places)
                and self.places[last] == (which, first + (last - start) * self.rows)
            ):
                last += 1
            count = (last - start) * self.rows
            yield start * self.rows, count, refs[which][first : first + count, :]
            start = last


def matmul(left, right, kind, body, kinds_out, beside=None, first=0, last=None, most=(512, 512)):
    depth = left.shape[0 if kind == "tn" else 1]
    rows = (last or left.shape[1 if kind == "tn" else 0]) - first
    columns = right.shape[0 if kind == "nt" else 1]
    pieces = right if isinstance(right, Pieces) else None
    rights = pieces.arrays if pieces else [right]
    down, along = tile(math.gcd(rows, first), most[0]), tile(columns, most[1])
    if pieces and kind == "nt":
        down, along = tile(rows, 256), columns
    skip = first // down
    if kind == "tn":
        left_spec = pl.BlockSpec((depth, down), lambda j, i: (0, i + skip))
    else:
        left_spec = pl.BlockSpec((down, depth), lambda j, i: (i + skip, 0))
    if kind == "nt":
        height = [x.shape[0] if pieces else along for x in rights]
        right_specs = [pl.BlockSpec((x, depth), lambda j, i: (j, 0)) for x in height]
    else:
        right_specs = [pl.BlockSpec((x.shape[0], along), lambda j, i: (0, j)) for x in rights]
    out_spec = pl.BlockSpec((down, along), lambda j, i: (i, j))
    more = [] if beside is None else [beside]

    def kernel(left_ref, *refs):
        rights_in, refs = refs[: len(rights)], refs[len(rights) :]
        values = [ref[...] for ref in refs[: len(more)]]
        outs = refs[len(more) :]
        if pieces and kind == "nt":
            for start, count, piece in pieces.read(rights_in):
                made = body(product(left_ref[...], piece, kind), *values)
                for ref, value in zip(outs, made):
                    ref[:, start : start + count] = value.astype(ref.dtype)
            return
        if pieces:
            total = sum(
                product(left_ref[:, start : start + count], piece, kind)
                for start, count, piece in pieces.read(rights_in)
            )
        else:
            total = product(left_ref[...], rights_in[0][...], kind)
        for ref, value in zip(outs, body(total, *values)):
            ref[...] = value.astype(ref.dtype)

    shapes = [jax.ShapeDtypeStruct((rows, columns), kind_out) for kind_out in kinds_out]
    size = sum(x.size * x.dtype.itemsize for x in (left, *rights, *more, *shapes))
    return pl.pallas_call(
        kernel,
        out_shape=shapes,
        grid=(columns // along, rows // down),
        in_specs=[left_spec] + right_specs + [out_spec] * len(more),
        out_specs=[out_spec] * len(shapes),
        compiler_params=pltpu.CompilerParams(vmem_limit_bytes=kernel_memory),
        cost_estimate=work(2 * rows * columns * depth, size),
    )(left, *rights, *more)


def dot_low(left, right, kind, first=0, last=None):
    return matmul(left, right, kind, lambda made: (made,), [low_type], first=first, last=last)[0]


def block_softmax(queries, keys_seen, segment_down, segment_along, first_row):
    scores = product(queries, keys_seen, "nt") * HEAD_DIM ** (-0.5)
    places = lax.broadcasted_iota(jnp.int32, scores.shape, 0) + first_row
    key_places = lax.broadcasted_iota(jnp.int32, scores.shape, 1)
    allowed = (segment_down == segment_along) & (key_places <= places)
    masked = jnp.where(allowed, scores, -1e30)
    exponent = jnp.exp(masked - jnp.max(masked, axis=-1, keepdims=True))
    return exponent * (1.0 / jnp.sum(exponent, axis=-1, keepdims=True))


def attend_kernel(query_ref, key_ref, value_ref, down_ref, along_ref, out_ref):
    row_length = query_ref.shape[0]
    block = tile(row_length, 256)
    for first in range(0, row_length, block):
        last = first + block
        soft = block_softmax(
            query_ref[first:last, :],
            key_ref[:last, :],
            down_ref[first:last, :],
            along_ref[:, :last],
            first,
        )
        made = product(soft.astype(low_type), value_ref[:last, :], "nn")
        out_ref[first:last, :] = made.astype(low_type)


def attend_back_kernel(
    query_ref, key_ref, value_ref, grad_ref, down_ref, along_ref, out_ref, key_sum, value_sum
):
    row_length = query_ref.shape[0]
    block = tile(row_length, 256)
    scale = HEAD_DIM ** (-0.5)
    kind = pl.program_id(2)

    @pl.when(kind == 0)
    def _():
        key_sum[...] = jnp.zeros_like(key_sum)
        value_sum[...] = jnp.zeros_like(value_sum)
        for first in range(0, row_length, block):
            last = first + block
            queries, grads = query_ref[first:last, :], grad_ref[first:last, :]
            soft = block_softmax(
                queries, key_ref[:last, :], down_ref[first:last, :], along_ref[:, :last], first
            )
            value_sum[:last, :] += product(soft.astype(low_type), grads, "tn")
            prob_grad = product(grads, value_ref[:last, :], "nt")
            row_delta = jnp.sum(prob_grad * soft, axis=-1, keepdims=True)
            score_grad = (soft * (prob_grad - row_delta)).astype(low_type)
            made = product(score_grad, key_ref[:last, :], "nn") * scale
            out_ref[first:last, :] = made.astype(low_type)
            key_sum[:last, :] += product(score_grad, queries, "tn")

    @pl.when(kind == 1)
    def _():
        out_ref[...] = (key_sum[...] * scale).astype(low_type)

    @pl.when(kind == 2)
    def _():
        out_ref[...] = value_sum[...].astype(low_type)


def attention(projected, segments, grads=None):
    row_count, row_length = segments.shape
    tokens, columns = projected.shape
    head_count = columns // (3 * HEAD_DIM)
    shape = (row_length, HEAD_DIM)
    down = segments.reshape(tokens, 1)
    along = segments.reshape(row_count, 1, row_length)

    def spec(kind):
        return pl.BlockSpec(shape, lambda r, h, *_: (r, kind * head_count + h))

    in_specs = [spec(0), spec(1), spec(2)] + ([] if grads is None else [spec(0)])
    in_specs += [
        pl.BlockSpec((row_length, 1), lambda r, h, *_: (r, 0)),
        pl.BlockSpec((None, 1, row_length), lambda r, h, *_: (r, 0, 0)),
    ]
    square = 2 * row_count * head_count * row_length * row_length * HEAD_DIM
    params = pltpu.CompilerParams(vmem_limit_bytes=kernel_memory)
    if grads is None:
        return pl.pallas_call(
            attend_kernel,
            out_shape=jax.ShapeDtypeStruct((tokens, head_count * HEAD_DIM), low_type),
            grid=(row_count, head_count),
            in_specs=in_specs,
            out_specs=spec(0),
            compiler_params=params,
            cost_estimate=work(2 * square, projected.size * 4),
        )(projected, projected, projected, down, along)
    return pl.pallas_call(
        attend_back_kernel,
        out_shape=jax.ShapeDtypeStruct(projected.shape, low_type),
        grid=(row_count, head_count, 3),
        in_specs=in_specs,
        out_specs=pl.BlockSpec(shape, lambda r, h, kind: (r, kind * head_count + h)),
        scratch_shapes=[pltpu.VMEM(shape, wide), pltpu.VMEM(shape, wide)],
        compiler_params=params,
        cost_estimate=work(5 * square, projected.size * 6),
    )(projected, projected, projected, grads, down, along)


def after(value, *earlier):
    return lax.optimization_barrier((value, *earlier))[0] if earlier else value


def copy_block(order_ref, in_ref, out_ref):
    out_ref[...] = in_ref[...]


def reorder_columns(values, order):
    rows, width = values.shape
    count = order.shape[0]
    columns = width // count
    if columns % 128:
        blocks = [
            lax.dynamic_slice_in_dim(values, order[i] * columns, columns, 1) for i in range(count)
        ]
        return jnp.concatenate(blocks, axis=1)
    return pl.pallas_call(
        copy_block,
        out_shape=jax.ShapeDtypeStruct(values.shape, values.dtype),
        grid_spec=pltpu.PrefetchScalarGridSpec(
            num_scalar_prefetch=1,
            grid=(count,),
            in_specs=[pl.BlockSpec((rows, columns), lambda i, order_ref: (0, order_ref[i]))],
            out_specs=pl.BlockSpec((rows, columns), lambda i, order_ref: (0, i)),
        ),
        cost_estimate=pl.CostEstimate(
            flops=0, bytes_accessed=2 * values.size * values.dtype.itemsize, transcendentals=0
        ),
    )(order, values)


def turn_block(in_ref, out_ref):
    out_ref[...] = in_ref[...].T


def turned(values):
    rows, width = values.shape
    columns = min(512, width)
    return pl.pallas_call(
        turn_block,
        out_shape=jax.ShapeDtypeStruct((width, rows), values.dtype),
        grid=(width // columns,),
        in_specs=[pl.BlockSpec((rows, columns), lambda i: (0, i))],
        out_specs=pl.BlockSpec((columns, rows), lambda i: (i, 0)),
        cost_estimate=pl.CostEstimate(
            flops=0, bytes_accessed=2 * values.size * values.dtype.itemsize, transcendentals=0
        ),
    )(values)


def adam_kernel(rate_value, decay_value, terms, *refs):
    gradient = sum(ref[...].astype(wide) for ref in refs[:terms])
    states, outs = refs[terms : terms + 4], refs[terms + 4 :]
    master, moment, square, average = (ref[...] for ref in states)
    made = adam_update(master, moment, square, gradient, rate_value, decay_value)
    smooth = average_decay * average + (1.0 - average_decay) * made[0]
    for ref, value in zip(outs, (*made, smooth, made[0])):
        ref[...] = value.astype(ref.dtype)


def adam_planes(terms, states, rate_value, decay_value):
    planes, rows, width = states[0].shape
    block = tile(rows, 128)
    flat = pl.BlockSpec((block, width), lambda j, i: (i, j))
    deep = pl.BlockSpec((None, block, width), lambda j, i: (j, i, 0))
    size = sum(x.size * x.dtype.itemsize for x in terms) + 34 * states[0].size
    kinds = [wide] * 4 + [low_type]
    return pl.pallas_call(
        functools.partial(adam_kernel, rate_value, decay_value, len(terms)),
        out_shape=[jax.ShapeDtypeStruct(states[0].shape, kind) for kind in kinds],
        grid=(planes, rows // block),
        in_specs=[flat] * len(terms) + [deep] * 4,
        out_specs=[deep] * 5,
        compiler_params=pltpu.CompilerParams(vmem_limit_bytes=kernel_memory),
        cost_estimate=pl.CostEstimate(flops=0, bytes_accessed=size, transcendentals=0),
    )(*terms, *states)


class Links:
    outer_order = (0, 2, 1, 3)

    def __init__(self, mesh):
        self.count = mesh.shape["dp"]
        self.outer = len(self.outer_order)
        self.inner = self.count // self.outer
        self.group = mesh.shape["tensor"]
        self.cores = 2
        self.chips = self.group // self.cores

    def place(self):
        index = lax.axis_index("dp")
        out_at, in_at = lax.div(index, self.inner), lax.rem(index, self.inner)
        index = lax.axis_index("tensor")
        self.chip_at, self.core_at = lax.div(index, self.cores), lax.rem(index, self.cores)
        order = jnp.asarray(self.outer_order, jnp.int32)
        inner = jnp.arange(self.inner, dtype=jnp.int32)
        self.to_own = (
            (out_at ^ order)[None, :] * self.inner + (in_at ^ inner)[:, None]
        ).reshape(-1)
        outer = jnp.arange(self.outer, dtype=jnp.int32) ^ out_at
        placed = (outer & 1) * 2 + (outer >> 1)
        self.from_own = ((inner ^ in_at)[None, :] * self.outer + placed[:, None]).reshape(-1)
        self.running = []

    def flip(self, value, over_outer, over_inner):
        pairs = []
        for a in range(self.outer):
            for b in range(self.inner):
                to = (a ^ over_outer) * self.inner + (b ^ over_inner)
                pairs.append((a * self.inner + b, to))
        return lax.ppermute(value, "dp", pairs)

    def across(self, over_outer, over_inner):
        return lambda value: self.flip(value, over_outer, over_inner)

    def round(self, make_moves, carried=()):
        held = [store[key] for store, key in self.running]
        held = lax.optimization_barrier((*held, *carried))
        for (store, key), value in zip(self.running, held):
            store[key] = value
        moves = make_moves()
        for value, send, store, key in moves:
            store[key] = send(after(value, *held))
        count = len(self.running)
        self.running = [(store, key) for *_, store, key in moves]
        return held[count:]

    def turn(self, value, over_chips, over_cores):
        pairs = []
        for a in range(self.chips):
            for b in range(self.cores):
                to = (a + over_chips) % self.chips * self.cores + (b + over_cores) % self.cores
                pairs.append((a * self.cores + b, to))
        return lax.ppermute(value, "tensor", pairs)

    def sum_tensor(self, total):
        for parts, step in ((self.cores, (0, 1)), (self.chips, (1, 0))):
            moving = total
            for _ in range(parts - 1):
                moving = self.turn(moving, *step)
                total = total + moving
        return total

    def along(self, over_chips, over_cores):
        return lambda value: self.turn(value, over_chips, over_cores)

    def own_rows(self, value):
        rows = value.shape[0] // self.group
        return lax.dynamic_slice_in_dim(
            value, (self.core_at * self.chips + self.chip_at) * rows, rows, 0
        )


class Gather:
    here = ("own", "far", "far0", "far1", "near", "near_own", "near_far")
    there = ("pair", "own", "far", "near", "near0", "near1", "near_own", "near_far")

    def __init__(self, links, shard, step=None):
        self.links = links
        self.step = step or shard.shape[0]
        self.held = {"own": shard}

    def out(self, name, value, distance):
        return [(value, self.links.across(distance, 0), self.held, name)]

    def joined(self, *names):
        return jnp.concatenate([self.held[name] for name in names], axis=0)

    def far(self):
        return self.out("far", self.held["own"], 2)

    def near(self):
        return self.out("near", self.joined("own", "far"), 1)

    def across(self, name, value=None):
        if value is None:
            value = self.joined("own", "far") if name == "pair" else self.held[name]
        partners = range(1, self.links.inner)
        return [(value, self.links.across(0, j), self.held, (name, j)) for j in partners]

    def beside(self, name, result):
        send = self.links.across(1, 0)
        partners = range(1, self.links.inner)
        return [(self.held[name, j], send, self.held, (result, j)) for j in partners]

    def half(self, name, part):
        value = self.held[name]
        rows = value.shape[0] // 2
        return value[part * rows : (part + 1) * rows]

    def parts(self):
        names = [name for name in self.here if name in self.held]
        for j in range(1, self.links.inner):
            names += [(name, j) for name in self.there if (name, j) in self.held]
        for name in names:
            for first in range(0, self.held[name].shape[0], self.step):
                yield self.held[name], first

    def full(self, rows):
        return Pieces(self.parts(), rows)


class Reduce:
    def __init__(self, links, rows, make, joint=False):
        self.links, self.rows = links, rows
        size = 2 * rows
        starts = [j * 2 * size for j in range(links.inner)]
        self.whole = {}
        if joint:
            self.whole = {j: make(starts[j], starts[j] + 2 * size) for j in range(1, links.inner)}
            self.away = {j: made[size:] for j, made in self.whole.items()}
            self.close = {j: made[:size] for j, made in self.whole.items()}
        else:
            ends = [start + 2 * size for start in starts]
            self.away = {j: make(starts[j] + size, ends[j]) for j in range(1, links.inner)}
            self.close = {j: make(starts[j], starts[j] + size) for j in range(1, links.inner)}
        self.mine = make(0, 2 * size)
        self.size = size
        self.held = {}

    def terms(self):
        if self.whole:
            return [*self.whole.values(), self.mine]
        return [*self.away.values(), *self.close.values(), self.mine]

    def span(self, part, size):
        return (0, size) if part is None else (part * size // 2, (part + 1) * size // 2)

    def move(self, name, j, part, value, send):
        key = (name, j) if part is None else (name, j, part)
        return (value, send, self.held, key)

    def got(self, name, j, first, last, size):
        if (name, j) in self.held:
            return self.held[name, j][first:last]
        if last - first > size // 2:
            halves = [self.held[name, j, 0], self.held[name, j, 1]]
            return jnp.concatenate(halves, axis=0)[first:last]
        part = first // (size // 2)
        skip = part * (size // 2)
        return self.held[name, j, part][first - skip : last - skip]

    def inward(self, name, terms, part):
        first, last = self.span(part, self.size)
        return [
            self.move(name, j, part, term[first:last], self.links.across(0, j))
            for j, term in terms.items()
        ]

    def first(self, part=None):
        return self.inward("away", self.away, part)

    def second(self, part=None):
        return self.inward("close", self.close, part)

    def both(self):
        return [
            (made, self.links.across(0, j), self.held, ("both", j))
            for j, made in self.whole.items()
        ]

    def split_both(self):
        for j in self.away:
            self.held["close", j] = self.held["both", j][: self.size]
            self.held["away", j] = self.held["both", j][self.size :]

    def near(self, part=None):
        first, last = self.span(part, self.size)
        sums = self.mine[self.size + first : self.size + last].astype(wide)
        for j in self.away:
            sums = sums + self.got("away", j, first, last, self.size).astype(wide)
        return [self.move("near", 0, part, sums.astype(low_type), self.links.across(1, 0))]

    def sums(self, first, last):
        sums = self.mine[first:last].astype(wide)
        sums = sums + self.got("near", 0, first, last, self.size).astype(wide)
        for j in self.close:
            sums = sums + self.got("close", j, first, last, self.size).astype(wide)
        return sums

    def far(self, part=None):
        first, last = self.span(part, self.rows)
        sums = self.sums(self.rows + first, self.rows + last).astype(low_type)
        return [self.move("far", 0, part, sums, self.links.across(2, 0))]

    def last_terms(self):
        near = self.held["near", 0]
        return [self.mine, near, *(self.held["close", j] for j in self.close), self.held["far", 0]]

    def total(self):
        parts = [None] if ("far", 0) in self.held else [0, 1]
        spans = [self.span(part, self.rows) for part in parts]
        sums = [
            self.sums(*span) + self.got("far", 0, *span, self.rows).astype(wide) for span in spans
        ]
        return jnp.concatenate(sums, axis=0)


class ReduceTensor:
    def __init__(self, links, partial):
        self.links, self.partial = links, partial
        self.held = {}

    def part(self, over_chips, over_cores):
        links = self.links
        rows = self.partial.shape[0] // links.group
        chip = lax.rem(links.chip_at + over_chips, links.chips)
        core = lax.rem(links.core_at + over_cores, links.cores)
        return lax.dynamic_slice_in_dim(self.partial, (core * links.chips + chip) * rows, rows, 0)

    def first(self):
        return [
            (self.part(j, 1), self.links.along(0, 1), self.held, ("half", j))
            for j in reversed(range(self.links.chips))
        ]

    def sums(self, j):
        return self.part(j, 0).astype(wide) + self.held["half", j].astype(wide)

    def second(self):
        return [
            (self.sums(j).astype(low_type), self.links.along(j, 0), self.held, j)
            for j in range(1, self.links.chips)
        ]

    def total(self):
        return self.sums(0) + sum(
            self.held[j].astype(wide) for j in range(1, self.links.chips)
        )


class GatherTensor:
    def __init__(self, links, own):
        self.links, self.own = links, own
        self.held = {}

    def first(self):
        chips = range(1, self.links.chips)
        return [(self.own, self.links.along(j, 0), self.held, (j, 0)) for j in chips] + [
            (self.own, self.links.along(0, 1), self.held, (0, 1))
        ]

    def second(self):
        chips = range(1, self.links.chips)
        return [
            (self.held[j, 0], self.links.along(0, 1), self.held, (j, 1)) for j in chips
        ]

    def now(self, moves):
        for value, send, store, key in moves:
            store[key] = send(value)

    def full(self):
        links = self.links
        rows = self.own.shape[0]
        full = jnp.zeros((links.group * rows,) + self.own.shape[1:], self.own.dtype)
        for (j, k), part in {(0, 0): self.own, **self.held}.items():
            chip = lax.rem(links.chip_at + links.chips - j, links.chips)
            core = lax.rem(links.core_at + k, links.cores)
            full = lax.dynamic_update_slice_in_dim(
                full, part, (core * links.chips + chip) * rows, 0
            )
        return full


class ReduceSmall:
    def __init__(self, links, partial):
        self.links = links
        self.split = partial.reshape(partial.shape[0], links.inner, links.outer, -1)
        self.held = {}

    def first(self):
        return [
            (self.split[:, j], self.links.across(0, j), self.held, j + 2)
            for j in range(1, self.links.inner)
        ]

    def outward(self):
        self.sums = self.split[:, 0] + sum(
            self.held[j + 2] for j in range(1, self.links.inner)
        )
        order = self.links.outer_order
        return [
            (self.sums[:, i], self.links.across(order[i], 0), self.held, -i)
            for i in range(1, len(order))
        ]

    def total(self):
        return self.sums[:, 0] + sum(self.held[-i] for i in range(1, self.links.outer))


def adam_update(master, moment, square, gradient, rate_value, decay_value):
    moment_new = beta_first * moment + (1.0 - beta_first) * gradient
    square_new = beta_second * square + (1.0 - beta_second) * gradient * gradient
    fix_first = 1.0 - beta_first**STEP
    fix_second = 1.0 - beta_second**STEP
    direction = moment_new / fix_first / (jnp.sqrt(square_new / fix_second) + adam_epsilon)
    master_new = master - rate_value * (direction + decay_value * master)
    return (master_new, moment_new, square_new)


def shards(
    links,
    hidden_in,
    out_cotangent,
    episode_lengths,
    self_generated,
    loss_numerator,
    attend_weights,
    attend_first,
    attend_second,
    attend_average,
    combine_weights,
    combine_first,
    combine_second,
    combine_average,
    expand_weights,
    expand_first,
    expand_second,
    expand_average,
    shrink_weights,
    shrink_first,
    shrink_second,
    shrink_average,
    layernorm_params,
    layernorm_first,
    layernorm_second,
    layernorm_average,
):
    links.place()
    local_tokens, width = hidden_in.shape
    row_count = episode_lengths.shape[0]
    row_length = local_tokens // row_count
    shard_rows, kinds_count, local_width = attend_weights.shape

    attend_states = [
        state.transpose(1, 0, 2)
        for state in (attend_weights, attend_first, attend_second, attend_average)
    ]
    attend_low = attend_weights.astype(low_type).reshape(shard_rows, kinds_count * local_width)
    combine_low = combine_weights.astype(low_type).T
    expand_low = expand_weights.astype(low_type)
    shrink_low = shrink_weights.astype(low_type).T
    norm_rows, norm_columns = layernorm_params.shape
    norm_low = layernorm_params.astype(low_type).reshape(1, -1)
    spare = attend_low.shape[1] - norm_low.shape[1]
    norm_low = jnp.pad(norm_low, ((0, 15), (0, spare)))
    attend_move = Gather(links, jnp.concatenate([attend_low, norm_low], axis=0))
    combine_move, expand_move = Gather(links, combine_low), Gather(links, expand_low)
    half_rows = shard_rows // 2
    shrink_move = Gather(links, shrink_low, half_rows)
    later = (combine_move, shrink_move)
    links.round(lambda: attend_move.far() + attend_move.across("own"))
    hidden_low = reorder_columns(hidden_in, links.to_own)
    cotangent_low = reorder_columns(out_cotangent, links.to_own)
    factor = loss_numerator.astype(wide) / (4.0 * (1.0 + self_generated.astype(wide)))
    branch_grad_low = (factor[:, None] * cotangent_low.astype(wide)).astype(low_type)
    out_grad_own = links.own_rows(factor)[:, None] * links.own_rows(cotangent_low).astype(wide)
    segments = jnp.stack([segment_ids(lengths, row_length) for lengths in episode_lengths])
    scaled_one, _ = norm_parts(hidden_low.astype(wide))
    scaled_one, branch_grad_low, segments, *own = links.round(
        lambda: attend_move.near()
        + combine_move.far()
        + attend_move.across("far")
        + expand_move.across("own"),
        [scaled_one, branch_grad_low, segments, *(move.held["own"] for move in later)],
    )
    for move, shard in zip(later, own):
        move.held["own"] = shard
    attend_states = links.round(
        lambda: combine_move.near()
        + expand_move.far()
        + attend_move.across("near")
        + combine_move.across("pair"),
        attend_states,
    )

    norm_values = jnp.concatenate(
        [
            part[first + shard_rows, : norm_rows * norm_columns].reshape(norm_rows, -1)
            for part, first in attend_move.parts()
        ],
        axis=1,
    ).astype(wide)
    normed_low = (scaled_one * norm_values[0] + norm_values[1]).astype(low_type)

    (normed_low,) = links.round(
        lambda: expand_move.near() + combine_move.across("near") + expand_move.across("far"),
        [normed_low],
    )
    attend_full = attend_move.full(shard_rows)
    projected = dot_low(normed_low, attend_full, "nn")
    mixed_low = attention(projected, segments)
    combine_full = combine_move.full(shard_rows)
    attended = ReduceTensor(links, dot_low(mixed_low, combine_full, "nt"))

    links.round(
        lambda: attended.first()
        + shrink_move.out("far0", shrink_move.half("own", 0), 2)
        + expand_move.across("near0", expand_move.half("near", 0)),
        [attended.partial],
    )
    hidden_own = links.own_rows(hidden_low).astype(wide)
    links.round(
        lambda: attended.second()
        + shrink_move.out("far1", shrink_move.half("own", 1), 2)
        + expand_move.across("near1", expand_move.half("near", 1))
    )
    residual = hidden_own + attended.total()
    scaled_two, inverse_two = norm_parts(residual)
    normed_two = GatherTensor(
        links, (scaled_two * norm_values[2] + norm_values[3]).astype(low_type)
    )
    (normed_two.own,) = links.round(
        lambda: normed_two.first()
        + shrink_move.out("near_own", shrink_move.held["own"], 1)
        + shrink_move.across("own"),
        [normed_two.own],
    )
    links.round(
        lambda: normed_two.second()
        + shrink_move.out("near_far", shrink_move.joined("far0", "far1"), 1)
        + shrink_move.across("far", shrink_move.joined("far0", "far1"))
    )
    links.round(lambda: shrink_move.across("near_far") + shrink_move.beside("own", "near_own"))
    normed_two_low = normed_two.full()
    expand_full = expand_move.full(shard_rows)
    activated_low, slope = matmul(
        normed_two_low,
        expand_full,
        "nn",
        gelu_parts,
        [low_type, wide],
    )

    def gradient_rows(left, right):
        return lambda first, last: dot_low(left, right, "tn", first, last)

    shrink_back = Reduce(links, shard_rows, gradient_rows(branch_grad_low, activated_low))

    slope, activated_low, *_ = links.round(
        shrink_back.first, [slope, activated_low, *shrink_back.away.values()]
    )
    shrink_full = shrink_move.full(half_rows)
    (expanded_grad_low,) = matmul(
        branch_grad_low,
        shrink_full,
        "nn",
        lambda made, before: (made * before,),
        [low_type],
        slope,
    )
    normed_two_back = ReduceTensor(links, dot_low(expanded_grad_low, expand_full, "nt"))

    normed_two_back.partial, expanded_grad_low, activated_low = links.round(
        lambda: normed_two_back.first() + shrink_back.second(1) + shrink_back.near(1),
        [normed_two_back.partial, expanded_grad_low, activated_low],
    )
    expand_back = Reduce(links, shard_rows, gradient_rows(normed_two_low, expanded_grad_low))
    links.round(
        lambda: normed_two_back.second() + shrink_back.second(0) + shrink_back.near(0),
        expand_back.terms(),
    )
    residual_from_norm, gain_two_grad, shift_two_grad = norm_back(
        normed_two_back.total(), scaled_two, inverse_two, norm_values[2]
    )
    residual_grad = out_grad_own + residual_from_norm
    attended_grad = GatherTensor(links, residual_grad.astype(low_type))

    attended_grad.own, activated_low = links.round(
        lambda: attended_grad.first() + expand_back.first(1) + shrink_back.far(1),
        [attended_grad.own, activated_low],
    )
    branch = ReduceTensor(links, dot_low(activated_low, shrink_full, "nt"))
    links.round(
        lambda: attended_grad.second()
        + branch.first()
        + expand_back.first(0)
        + shrink_back.far(0),
        [branch.partial],
    )
    attended_grad_low = attended_grad.full()
    mixed_grad = dot_low(attended_grad_low, combine_full, "nn")
    projected_grad = attention(projected, segments, mixed_grad)
    (projected_grad,) = links.round(
        lambda: branch.second() + expand_back.second() + expand_back.near(), [projected_grad]
    )
    combine_back = Reduce(links, shard_rows, gradient_rows(attended_grad_low, mixed_low), True)
    attend_back = Reduce(links, shard_rows, gradient_rows(normed_low, projected_grad))
    normed_one_back = ReduceTensor(links, dot_low(projected_grad, attend_full, "nt"))

    shrink_back.mine, *_ = links.round(
        lambda: normed_one_back.first() + combine_back.both() + expand_back.far(1),
        [shrink_back.mine, normed_one_back.partial, *attend_back.terms(), *combine_back.terms()],
    )
    output = GatherTensor(
        links,
        reorder_columns((residual + branch.total()).astype(low_type), links.from_own),
    )
    combine_back.split_both()
    links.round(
        lambda: normed_one_back.second()
        + attend_back.first()
        + combine_back.near()
        + expand_back.far(0)
    )
    shrink_sum = turned(shrink_back.total())
    scaled_own, inverse_own = norm_parts(hidden_own)
    hidden_from_norm, gain_one_grad, shift_one_grad = norm_back(
        normed_one_back.total(), scaled_own, inverse_own, norm_values[0]
    )
    input_own = reorder_columns((residual_grad + hidden_from_norm).astype(low_type), links.from_own)
    input_back = GatherTensor(links, input_own)
    input_back.own, output.own = links.round(
        lambda: attend_back.second()
        + attend_back.near()
        + input_back.first()[:-1]
        + combine_back.far(),
        [input_own, output.own],
    )
    output.now(output.first()[:-1])
    norm_terms = jnp.stack([gain_one_grad, shift_one_grad, gain_two_grad, shift_two_grad])

    (expand_back.mine, norm_terms) = links.round(
        lambda: input_back.first()[-1:] + attend_back.far(), [expand_back.mine, norm_terms]
    )
    input_back.now(input_back.second())
    output.now(output.first()[-1:])
    output.now(output.second())
    norm_grads = ReduceSmall(links, links.sum_tensor(norm_terms))
    for value, send, store, key in norm_grads.first():
        store[key] = send(value)
    expand_sum = expand_back.total()
    combine_sum = turned(combine_back.total())
    layer_output = output.full()
    input_gradient = input_back.full().astype(wide)
    (input_gradient, layer_output, norm_grads.split) = links.round(
        norm_grads.outward, [input_gradient, layer_output, norm_grads.split]
    )
    norm_sum = norm_grads.total()
    attend_new = adam_planes(
        attend_back.last_terms(),
        attend_states,
        matrix_rate,
        weight_decay,
    )
    kinds = (
        (
            combine_weights,
            combine_first,
            combine_second,
            combine_average,
            combine_sum,
            matrix_rate,
            weight_decay,
        ),
        (
            expand_weights,
            expand_first,
            expand_second,
            expand_average,
            expand_sum,
            matrix_rate,
            weight_decay,
        ),
        (
            shrink_weights,
            shrink_first,
            shrink_second,
            shrink_average,
            shrink_sum,
            matrix_rate,
            weight_decay,
        ),
        (
            layernorm_params,
            layernorm_first,
            layernorm_second,
            layernorm_average,
            norm_sum,
            norm_rate,
            0.0,
        ),
    )
    results = [layer_output, input_gradient, *(made.transpose(1, 0, 2) for made in attend_new)]
    for master, moment, square, average, gradient, rate_value, decay_value in kinds:
        master_new, moment_new, square_new = adam_update(
            master, moment, square, gradient, rate_value, decay_value
        )
        smooth_new = average_decay * average + (1.0 - average_decay) * master_new
        results.extend(
            [master_new, moment_new, square_new, smooth_new, master_new.astype(jnp.bfloat16)]
        )
    return tuple(results)


def solution(mesh):
    placed = (
        P("dp", None),
        P("dp", None),
        P("dp", None),
        P("dp"),
        P("dp"),
        P("dp", None, "tensor"),
        P("dp", None, "tensor"),
        P("dp", None, "tensor"),
        P("dp", None, "tensor"),
        P("tensor", "dp"),
        P("tensor", "dp"),
        P("tensor", "dp"),
        P("tensor", "dp"),
        P("dp", "tensor"),
        P("dp", "tensor"),
        P("dp", "tensor"),
        P("dp", "tensor"),
        P("tensor", "dp"),
        P("tensor", "dp"),
        P("tensor", "dp"),
        P("tensor", "dp"),
        P(None, "dp"),
        P(None, "dp"),
        P(None, "dp"),
        P(None, "dp"),
    )
    return jax.shard_map(
        functools.partial(shards, Links(mesh)),
        mesh=mesh,
        in_specs=placed,
        out_specs=(
            P("dp", None),
            P("dp", None),
            P("dp", None, "tensor"),
            P("dp", None, "tensor"),
            P("dp", None, "tensor"),
            P("dp", None, "tensor"),
            P("dp", None, "tensor"),
            P("tensor", "dp"),
            P("tensor", "dp"),
            P("tensor", "dp"),
            P("tensor", "dp"),
            P("tensor", "dp"),
            P("dp", "tensor"),
            P("dp", "tensor"),
            P("dp", "tensor"),
            P("dp", "tensor"),
            P("dp", "tensor"),
            P("tensor", "dp"),
            P("tensor", "dp"),
            P("tensor", "dp"),
            P("tensor", "dp"),
            P("tensor", "dp"),
            P(None, "dp"),
            P(None, "dp"),
            P(None, "dp"),
            P(None, "dp"),
            P(None, "dp"),
        ),
        check_vma=False,
    )
```

```python
import functools
import math

import jax
import jax.numpy as jnp
from jax import lax
from jax.experimental import pallas as pl
from jax.experimental.pallas import tpu as pltpu
from jax.sharding import PartitionSpec as P

HEAD_DIM = 128
STEP = 10


beta_first = 0.5
beta_second = 0.5
average_decay = 0.5
adam_epsilon = 1e-08
weight_decay = 0.1
matrix_rate = 0.02
norm_rate = 0.2
norm_epsilon = 1e-05
low_type = jnp.bfloat16
wide = jnp.float32
work_share = 0.1
kernel_memory = 25 * 1024 * 1024


def norm_parts(values):
    center = values - jnp.mean(values, axis=-1, keepdims=True)
    spread = jnp.mean(center * center, axis=-1, keepdims=True)
    inverse = lax.rsqrt(spread + norm_epsilon)
    return center * inverse, inverse


def norm_back(grad, scaled, inverse, gain_row):
    inner = grad * gain_row
    mean_inner = jnp.mean(inner, axis=-1, keepdims=True)
    mean_scaled = jnp.mean(inner * scaled, axis=-1, keepdims=True)
    result = inverse * (inner - mean_inner - scaled * mean_scaled)
    return result, jnp.sum(grad * scaled, axis=0), jnp.sum(grad, axis=0)


def gelu_parts(v):
    scale = math.sqrt(2.0 / math.pi)
    bend = jnp.tanh(scale * (v + 0.044715 * (v * v * v)))
    slope = 0.5 * (1.0 + bend) + 0.5 * v * (1.0 - bend * bend) * scale * (
        1.0 + 3.0 * 0.044715 * (v * v)
    )
    return 0.5 * v * (1.0 + bend), slope


def segment_ids(lengths_row, row_length):
    order = jnp.arange(lengths_row.shape[0], dtype=jnp.int32)
    earlier = order[None, :] <= order[:, None]
    bounds = jnp.sum(jnp.where(earlier, lengths_row[None, :], 0), axis=1)
    places = jnp.arange(row_length, dtype=jnp.int32)
    return jnp.sum((places[:, None] >= bounds[None, :]).astype(jnp.int32), axis=1)


def work(flops, size, exponents=0):
    return pl.CostEstimate(
        flops=int(flops * work_share), bytes_accessed=int(size * work_share), transcendentals=exponents
    )


def tile(size, most):
    return math.gcd(size, most)


product_dims = {
    "nn": (((1,), (0,)), ((), ())),
    "nt": (((1,), (1,)), ((), ())),
    "tn": (((0,), (0,)), ((), ())),
}


def product(left, right, kind):
    return lax.dot_general(left, right, product_dims[kind], preferred_element_type=wide)


class Pieces:
    def __init__(self, parts, rows):
        self.rows = rows
        self.arrays, self.places = [], []
        for array, first in parts:
            if not self.arrays or self.arrays[-1] is not array:
                self.arrays.append(array)
            self.places.append((len(self.arrays) - 1, first))
        self.shape = (rows * len(self.places), self.arrays[0].shape[1])

    def read(self, refs):
        start = 0
        while start < len(self.places):
            which, first = self.places[start]
            last = start + 1
            while (
                last < len(self.places)
                and self.places[last] == (which, first + (last - start) * self.rows)
            ):
                last += 1
            count = (last - start) * self.rows
            yield start * self.rows, count, refs[which][first : first + count, :]
            start = last


def matmul(left, right, kind, body, kinds_out, beside=None, first=0, last=None, most=(512, 1024)):
    depth = left.shape[0 if kind == "tn" else 1]
    rows = (last or left.shape[1 if kind == "tn" else 0]) - first
    columns = right.shape[0 if kind == "nt" else 1]
    pieces = right if isinstance(right, Pieces) else None
    rights = pieces.arrays if pieces else [right]
    down, along = tile(math.gcd(rows, first), most[0]), tile(columns, most[1])
    if pieces and kind == "nt":
        down, along = tile(rows, 256), columns
    skip = first // down
    if kind == "tn":
        left_spec = pl.BlockSpec((depth, down), lambda j, i: (0, i + skip))
    else:
        left_spec = pl.BlockSpec((down, depth), lambda j, i: (i + skip, 0))
    if kind == "nt":
        height = [x.shape[0] if pieces else along for x in rights]
        right_specs = [pl.BlockSpec((x, depth), lambda j, i: (j, 0)) for x in height]
    else:
        right_specs = [pl.BlockSpec((x.shape[0], along), lambda j, i: (0, j)) for x in rights]
    out_spec = pl.BlockSpec((down, along), lambda j, i: (i, j))
    more = [] if beside is None else [beside]

    def kernel(left_ref, *refs):
        rights_in, refs = refs[: len(rights)], refs[len(rights) :]
        values = [ref[...] for ref in refs[: len(more)]]
        outs = refs[len(more) :]
        if pieces and kind == "nt":
            for start, count, piece in pieces.read(rights_in):
                made = body(product(left_ref[...], piece, kind), *values)
                for ref, value in zip(outs, made):
                    ref[:, start : start + count] = value.astype(ref.dtype)
            return
        if pieces:
            total = sum(
                product(left_ref[:, start : start + count], piece, kind)
                for start, count, piece in pieces.read(rights_in)
            )
        else:
            total = product(left_ref[...], rights_in[0][...], kind)
        for ref, value in zip(outs, body(total, *values)):
            ref[...] = value.astype(ref.dtype)

    shapes = [jax.ShapeDtypeStruct((rows, columns), kind_out) for kind_out in kinds_out]
    size = sum(x.size * x.dtype.itemsize for x in (left, *rights, *more, *shapes))
    return pl.pallas_call(
        kernel,
        out_shape=shapes,
        grid=(columns // along, rows // down),
        in_specs=[left_spec] + right_specs + [out_spec] * len(more),
        out_specs=[out_spec] * len(shapes),
        compiler_params=pltpu.CompilerParams(vmem_limit_bytes=kernel_memory),
        cost_estimate=work(2 * rows * columns * depth, size),
    )(left, *rights, *more)


def dot_low(left, right, kind, first=0, last=None):
    return matmul(left, right, kind, lambda made: (made,), [low_type], first=first, last=last)[0]


def block_softmax(queries, keys_seen, segment_down, segment_along, first_row):
    scores = product(queries, keys_seen, "nt") * HEAD_DIM ** (-0.5)
    places = lax.broadcasted_iota(jnp.int32, scores.shape, 0) + first_row
    key_places = lax.broadcasted_iota(jnp.int32, scores.shape, 1)
    allowed = (segment_down == segment_along) & (key_places <= places)
    masked = jnp.where(allowed, scores, -1e30)
    exponent = jnp.exp(masked - jnp.max(masked, axis=-1, keepdims=True))
    return exponent * (1.0 / jnp.sum(exponent, axis=-1, keepdims=True))


def attend_kernel(query_ref, key_ref, value_ref, down_ref, along_ref, out_ref):
    row_length = query_ref.shape[0]
    block = tile(row_length, 256)
    for first in range(0, row_length, block):
        last = first + block
        soft = block_softmax(
            query_ref[first:last, :],
            key_ref[:last, :],
            down_ref[first:last, :],
            along_ref[:, :last],
            first,
        )
        made = product(soft.astype(low_type), value_ref[:last, :], "nn")
        out_ref[first:last, :] = made.astype(low_type)


def attend_back_kernel(
    query_ref, key_ref, value_ref, grad_ref, down_ref, along_ref, out_ref, key_sum, value_sum
):
    row_length = query_ref.shape[0]
    block = tile(row_length, 256)
    scale = HEAD_DIM ** (-0.5)
    kind = pl.program_id(2)

    @pl.when(kind == 0)
    def _():
        key_sum[...] = jnp.zeros_like(key_sum)
        value_sum[...] = jnp.zeros_like(value_sum)
        for first in range(0, row_length, block):
            last = first + block
            queries, grads = query_ref[first:last, :], grad_ref[first:last, :]
            soft = block_softmax(
                queries, key_ref[:last, :], down_ref[first:last, :], along_ref[:, :last], first
            )
            value_sum[:last, :] += product(soft.astype(low_type), grads, "tn")
            prob_grad = product(grads, value_ref[:last, :], "nt")
            row_delta = jnp.sum(prob_grad * soft, axis=-1, keepdims=True)
            score_grad = (soft * (prob_grad - row_delta)).astype(low_type)
            made = product(score_grad, key_ref[:last, :], "nn") * scale
            out_ref[first:last, :] = made.astype(low_type)
            key_sum[:last, :] += product(score_grad, queries, "tn")

    @pl.when(kind == 1)
    def _():
        out_ref[...] = (key_sum[...] * scale).astype(low_type)

    @pl.when(kind == 2)
    def _():
        out_ref[...] = value_sum[...].astype(low_type)


def attention(projected, segments, grads=None):
    row_count, row_length = segments.shape
    tokens, columns = projected.shape
    head_count = columns // (3 * HEAD_DIM)
    shape = (row_length, HEAD_DIM)
    down = segments.reshape(tokens, 1)
    along = segments.reshape(row_count, 1, row_length)

    def spec(kind):
        return pl.BlockSpec(shape, lambda r, h, *_: (r, kind * head_count + h))

    in_specs = [spec(0), spec(1), spec(2)] + ([] if grads is None else [spec(0)])
    in_specs += [
        pl.BlockSpec((row_length, 1), lambda r, h, *_: (r, 0)),
        pl.BlockSpec((None, 1, row_length), lambda r, h, *_: (r, 0, 0)),
    ]
    square = 2 * row_count * head_count * row_length * row_length * HEAD_DIM
    params = pltpu.CompilerParams(vmem_limit_bytes=kernel_memory)
    if grads is None:
        return pl.pallas_call(
            attend_kernel,
            out_shape=jax.ShapeDtypeStruct((tokens, head_count * HEAD_DIM), low_type),
            grid=(row_count, head_count),
            in_specs=in_specs,
            out_specs=spec(0),
            compiler_params=params,
            cost_estimate=work(2 * square, projected.size * 4),
        )(projected, projected, projected, down, along)
    return pl.pallas_call(
        attend_back_kernel,
        out_shape=jax.ShapeDtypeStruct(projected.shape, low_type),
        grid=(row_count, head_count, 3),
        in_specs=in_specs,
        out_specs=pl.BlockSpec(shape, lambda r, h, kind: (r, kind * head_count + h)),
        scratch_shapes=[pltpu.VMEM(shape, wide), pltpu.VMEM(shape, wide)],
        compiler_params=params,
        cost_estimate=work(5 * square, projected.size * 6),
    )(projected, projected, projected, grads, down, along)


def after(value, *earlier):
    return lax.optimization_barrier((value, *earlier))[0] if earlier else value


def copy_block(order_ref, in_ref, out_ref):
    out_ref[...] = in_ref[...]


def reorder_columns(values, order):
    rows, width = values.shape
    count = order.shape[0]
    columns = width // count
    if columns % 128:
        blocks = [
            lax.dynamic_slice_in_dim(values, order[i] * columns, columns, 1) for i in range(count)
        ]
        return jnp.concatenate(blocks, axis=1)
    return pl.pallas_call(
        copy_block,
        out_shape=jax.ShapeDtypeStruct(values.shape, values.dtype),
        grid_spec=pltpu.PrefetchScalarGridSpec(
            num_scalar_prefetch=1,
            grid=(count,),
            in_specs=[pl.BlockSpec((rows, columns), lambda i, order_ref: (0, order_ref[i]))],
            out_specs=pl.BlockSpec((rows, columns), lambda i, order_ref: (0, i)),
        ),
        cost_estimate=pl.CostEstimate(
            flops=0, bytes_accessed=2 * values.size * values.dtype.itemsize, transcendentals=0
        ),
    )(order, values)


def turn_block(in_ref, out_ref):
    out_ref[...] = in_ref[...].T


def turned(values):
    rows, width = values.shape
    columns = min(512, width)
    return pl.pallas_call(
        turn_block,
        out_shape=jax.ShapeDtypeStruct((width, rows), values.dtype),
        grid=(width // columns,),
        in_specs=[pl.BlockSpec((rows, columns), lambda i: (0, i))],
        out_specs=pl.BlockSpec((columns, rows), lambda i: (i, 0)),
        cost_estimate=pl.CostEstimate(
            flops=0, bytes_accessed=2 * values.size * values.dtype.itemsize, transcendentals=0
        ),
    )(values)


def adam_kernel(rate_value, decay_value, terms, *refs):
    gradient = sum(ref[...].astype(wide) for ref in refs[:terms])
    states, outs = refs[terms : terms + 4], refs[terms + 4 :]
    master, moment, square, average = (ref[...] for ref in states)
    made = adam_update(master, moment, square, gradient, rate_value, decay_value)
    smooth = average_decay * average + (1.0 - average_decay) * made[0]
    for ref, value in zip(outs, (*made, smooth, made[0])):
        ref[...] = value.astype(ref.dtype)


def adam_planes(terms, states, rate_value, decay_value):
    planes, rows, width = states[0].shape
    block = tile(rows, 128)
    flat = pl.BlockSpec((block, width), lambda j, i: (i, j))
    deep = pl.BlockSpec((None, block, width), lambda j, i: (j, i, 0))
    size = sum(x.size * x.dtype.itemsize for x in terms) + 34 * states[0].size
    kinds = [wide] * 4 + [low_type]
    return pl.pallas_call(
        functools.partial(adam_kernel, rate_value, decay_value, len(terms)),
        out_shape=[jax.ShapeDtypeStruct(states[0].shape, kind) for kind in kinds],
        grid=(planes, rows // block),
        in_specs=[flat] * len(terms) + [deep] * 4,
        out_specs=[deep] * 5,
        compiler_params=pltpu.CompilerParams(vmem_limit_bytes=kernel_memory),
        cost_estimate=pl.CostEstimate(flops=0, bytes_accessed=size, transcendentals=0),
    )(*terms, *states)


class Links:
    outer_order = (0, 2, 1, 3)

    def __init__(self, mesh):
        self.count = mesh.shape["dp"]
        self.outer = len(self.outer_order)
        self.inner = self.count // self.outer
        self.group = mesh.shape["tensor"]
        self.cores = 2
        self.chips = self.group // self.cores

    def place(self):
        index = lax.axis_index("dp")
        out_at, in_at = lax.div(index, self.inner), lax.rem(index, self.inner)
        index = lax.axis_index("tensor")
        self.chip_at, self.core_at = lax.div(index, self.cores), lax.rem(index, self.cores)
        order = jnp.asarray(self.outer_order, jnp.int32)
        inner = jnp.arange(self.inner, dtype=jnp.int32)
        self.to_own = (
            (out_at ^ order)[None, :] * self.inner + (in_at ^ inner)[:, None]
        ).reshape(-1)
        outer = jnp.arange(self.outer, dtype=jnp.int32) ^ out_at
        placed = (outer & 1) * 2 + (outer >> 1)
        self.from_own = ((inner ^ in_at)[None, :] * self.outer + placed[:, None]).reshape(-1)
        self.running = []

    def flip(self, value, over_outer, over_inner):
        pairs = []
        for a in range(self.outer):
            for b in range(self.inner):
                to = (a ^ over_outer) * self.inner + (b ^ over_inner)
                pairs.append((a * self.inner + b, to))
        return lax.ppermute(value, "dp", pairs)

    def across(self, over_outer, over_inner):
        return lambda value: self.flip(value, over_outer, over_inner)

    def round(self, make_moves, carried=()):
        held = [store[key] for store, key in self.running]
        held = lax.optimization_barrier((*held, *carried))
        for (store, key), value in zip(self.running, held):
            store[key] = value
        moves = make_moves()
        for value, send, store, key in moves:
            store[key] = send(after(value, *held))
        count = len(self.running)
        self.running = [(store, key) for *_, store, key in moves]
        return held[count:]

    def turn(self, value, over_chips, over_cores):
        pairs = []
        for a in range(self.chips):
            for b in range(self.cores):
                to = (a + over_chips) % self.chips * self.cores + (b + over_cores) % self.cores
                pairs.append((a * self.cores + b, to))
        return lax.ppermute(value, "tensor", pairs)

    def sum_tensor(self, total):
        for parts, step in ((self.cores, (0, 1)), (self.chips, (1, 0))):
            moving = total
            for _ in range(parts - 1):
                moving = self.turn(moving, *step)
                total = total + moving
        return total

    def along(self, over_chips, over_cores):
        return lambda value: self.turn(value, over_chips, over_cores)

    def own_rows(self, value):
        rows = value.shape[0] // self.group
        return lax.dynamic_slice_in_dim(
            value, (self.core_at * self.chips + self.chip_at) * rows, rows, 0
        )


class Gather:
    here = ("own", "far", "far0", "far1", "near", "near_own", "near_far")
    there = ("pair", "own", "far", "near", "near0", "near1", "near_own", "near_far")

    def __init__(self, links, shard, step=None):
        self.links = links
        self.step = step or shard.shape[0]
        self.held = {"own": shard}

    def out(self, name, value, distance):
        return [(value, self.links.across(distance, 0), self.held, name)]

    def joined(self, *names):
        return jnp.concatenate([self.held[name] for name in names], axis=0)

    def far(self):
        return self.out("far", self.held["own"], 2)

    def near(self):
        return self.out("near", self.joined("own", "far"), 1)

    def across(self, name, value=None):
        if value is None:
            value = self.joined("own", "far") if name == "pair" else self.held[name]
        partners = range(1, self.links.inner)
        return [(value, self.links.across(0, j), self.held, (name, j)) for j in partners]

    def beside(self, name, result):
        send = self.links.across(1, 0)
        partners = range(1, self.links.inner)
        return [(self.held[name, j], send, self.held, (result, j)) for j in partners]

    def half(self, name, part):
        value = self.held[name]
        rows = value.shape[0] // 2
        return value[part * rows : (part + 1) * rows]

    def parts(self):
        names = [name for name in self.here if name in self.held]
        for j in range(1, self.links.inner):
            names += [(name, j) for name in self.there if (name, j) in self.held]
        for name in names:
            for first in range(0, self.held[name].shape[0], self.step):
                yield self.held[name], first

    def full(self, rows):
        return Pieces(self.parts(), rows)


class Reduce:
    def __init__(self, links, rows, make, joint=False):
        self.links, self.rows = links, rows
        size = 2 * rows
        starts = [j * 2 * size for j in range(links.inner)]
        self.whole = {}
        if joint:
            self.whole = {j: make(starts[j], starts[j] + 2 * size) for j in range(1, links.inner)}
            self.away = {j: made[size:] for j, made in self.whole.items()}
            self.close = {j: made[:size] for j, made in self.whole.items()}
        else:
            ends = [start + 2 * size for start in starts]
            self.away = {j: make(starts[j] + size, ends[j]) for j in range(1, links.inner)}
            self.close = {j: make(starts[j], starts[j] + size) for j in range(1, links.inner)}
        self.mine = make(0, 2 * size)
        self.size = size
        self.held = {}

    def terms(self):
        if self.whole:
            return [*self.whole.values(), self.mine]
        return [*self.away.values(), *self.close.values(), self.mine]

    def span(self, part, size):
        return (0, size) if part is None else (part * size // 2, (part + 1) * size // 2)

    def move(self, name, j, part, value, send):
        key = (name, j) if part is None else (name, j, part)
        return (value, send, self.held, key)

    def got(self, name, j, first, last, size):
        if (name, j) in self.held:
            return self.held[name, j][first:last]
        if last - first > size // 2:
            halves = [self.held[name, j, 0], self.held[name, j, 1]]
            return jnp.concatenate(halves, axis=0)[first:last]
        part = first // (size // 2)
        skip = part * (size // 2)
        return self.held[name, j, part][first - skip : last - skip]

    def inward(self, name, terms, part):
        first, last = self.span(part, self.size)
        return [
            self.move(name, j, part, term[first:last], self.links.across(0, j))
            for j, term in terms.items()
        ]

    def first(self, part=None):
        return self.inward("away", self.away, part)

    def second(self, part=None):
        return self.inward("close", self.close, part)

    def both(self):
        return [
            (made, self.links.across(0, j), self.held, ("both", j))
            for j, made in self.whole.items()
        ]

    def split_both(self):
        for j in self.away:
            self.held["close", j] = self.held["both", j][: self.size]
            self.held["away", j] = self.held["both", j][self.size :]

    def near(self, part=None):
        first, last = self.span(part, self.size)
        sums = self.mine[self.size + first : self.size + last].astype(wide)
        for j in self.away:
            sums = sums + self.got("away", j, first, last, self.size).astype(wide)
        return [self.move("near", 0, part, sums.astype(low_type), self.links.across(1, 0))]

    def sums(self, first, last):
        sums = self.mine[first:last].astype(wide)
        sums = sums + self.got("near", 0, first, last, self.size).astype(wide)
        for j in self.close:
            sums = sums + self.got("close", j, first, last, self.size).astype(wide)
        return sums

    def far(self, part=None):
        first, last = self.span(part, self.rows)
        sums = self.sums(self.rows + first, self.rows + last).astype(low_type)
        return [self.move("far", 0, part, sums, self.links.across(2, 0))]

    def last_terms(self):
        near = self.held["near", 0]
        return [self.mine, near, *(self.held["close", j] for j in self.close), self.held["far", 0]]

    def total(self):
        parts = [None] if ("far", 0) in self.held else [0, 1]
        spans = [self.span(part, self.rows) for part in parts]
        sums = [
            self.sums(*span) + self.got("far", 0, *span, self.rows).astype(wide) for span in spans
        ]
        return jnp.concatenate(sums, axis=0)


class ReduceTensor:
    def __init__(self, links, partial):
        self.links, self.partial = links, partial
        self.held = {}

    def part(self, over_chips, over_cores):
        links = self.links
        rows = self.partial.shape[0] // links.group
        chip = lax.rem(links.chip_at + over_chips, links.chips)
        core = lax.rem(links.core_at + over_cores, links.cores)
        return lax.dynamic_slice_in_dim(self.partial, (core * links.chips + chip) * rows, rows, 0)

    def first(self):
        return [
            (self.part(j, 1), self.links.along(0, 1), self.held, ("half", j))
            for j in reversed(range(self.links.chips))
        ]

    def sums(self, j):
        return self.part(j, 0).astype(wide) + self.held["half", j].astype(wide)

    def second(self):
        return [
            (self.sums(j).astype(low_type), self.links.along(j, 0), self.held, j)
            for j in range(1, self.links.chips)
        ]

    def total(self):
        return self.sums(0) + sum(
            self.held[j].astype(wide) for j in range(1, self.links.chips)
        )


class GatherTensor:
    def __init__(self, links, own):
        self.links, self.own = links, own
        self.held = {}

    def first(self):
        chips = range(1, self.links.chips)
        return [(self.own, self.links.along(j, 0), self.held, (j, 0)) for j in chips] + [
            (self.own, self.links.along(0, 1), self.held, (0, 1))
        ]

    def second(self):
        chips = range(1, self.links.chips)
        return [
            (self.held[j, 0], self.links.along(0, 1), self.held, (j, 1)) for j in chips
        ]

    def now(self, moves):
        for value, send, store, key in moves:
            store[key] = send(value)

    def full(self):
        links = self.links
        rows = self.own.shape[0]
        full = jnp.zeros((links.group * rows,) + self.own.shape[1:], self.own.dtype)
        for (j, k), part in {(0, 0): self.own, **self.held}.items():
            chip = lax.rem(links.chip_at + links.chips - j, links.chips)
            core = lax.rem(links.core_at + k, links.cores)
            full = lax.dynamic_update_slice_in_dim(
                full, part, (core * links.chips + chip) * rows, 0
            )
        return full


class ReduceSmall:
    def __init__(self, links, partial):
        self.links = links
        self.split = partial.reshape(partial.shape[0], links.inner, links.outer, -1)
        self.held = {}

    def first(self):
        return [
            (self.split[:, j], self.links.across(0, j), self.held, j + 2)
            for j in range(1, self.links.inner)
        ]

    def outward(self):
        self.sums = self.split[:, 0] + sum(
            self.held[j + 2] for j in range(1, self.links.inner)
        )
        order = self.links.outer_order
        return [
            (self.sums[:, i], self.links.across(order[i], 0), self.held, -i)
            for i in range(1, len(order))
        ]

    def total(self):
        return self.sums[:, 0] + sum(self.held[-i] for i in range(1, self.links.outer))


def adam_update(master, moment, square, gradient, rate_value, decay_value):
    moment_new = beta_first * moment + (1.0 - beta_first) * gradient
    square_new = beta_second * square + (1.0 - beta_second) * gradient * gradient
    fix_first = 1.0 - beta_first**STEP
    fix_second = 1.0 - beta_second**STEP
    direction = moment_new / fix_first / (jnp.sqrt(square_new / fix_second) + adam_epsilon)
    master_new = master - rate_value * (direction + decay_value * master)
    return (master_new, moment_new, square_new)


def shards(
    links,
    hidden_in,
    out_cotangent,
    episode_lengths,
    self_generated,
    loss_numerator,
    attend_weights,
    attend_first,
    attend_second,
    attend_average,
    combine_weights,
    combine_first,
    combine_second,
    combine_average,
    expand_weights,
    expand_first,
    expand_second,
    expand_average,
    shrink_weights,
    shrink_first,
    shrink_second,
    shrink_average,
    layernorm_params,
    layernorm_first,
    layernorm_second,
    layernorm_average,
):
    links.place()
    local_tokens, width = hidden_in.shape
    row_count = episode_lengths.shape[0]
    row_length = local_tokens // row_count
    shard_rows, kinds_count, local_width = attend_weights.shape

    attend_states = [
        state.transpose(1, 0, 2)
        for state in (attend_weights, attend_first, attend_second, attend_average)
    ]
    attend_low = attend_weights.astype(low_type).reshape(shard_rows, kinds_count * local_width)
    combine_low = combine_weights.astype(low_type).T
    expand_low = expand_weights.astype(low_type)
    shrink_low = shrink_weights.astype(low_type).T
    norm_rows, norm_columns = layernorm_params.shape
    norm_low = layernorm_params.astype(low_type).reshape(1, -1)
    spare = attend_low.shape[1] - norm_low.shape[1]
    norm_low = jnp.pad(norm_low, ((0, 15), (0, spare)))
    attend_move = Gather(links, jnp.concatenate([attend_low, norm_low], axis=0))
    combine_move, expand_move = Gather(links, combine_low), Gather(links, expand_low)
    half_rows = shard_rows // 2
    shrink_move = Gather(links, shrink_low, half_rows)
    later = (combine_move, shrink_move)
    links.round(lambda: attend_move.far() + attend_move.across("own"))
    hidden_low = reorder_columns(hidden_in, links.to_own)
    cotangent_low = reorder_columns(out_cotangent, links.to_own)
    factor = loss_numerator.astype(wide) / (4.0 * (1.0 + self_generated.astype(wide)))
    branch_grad_low = (factor[:, None] * cotangent_low.astype(wide)).astype(low_type)
    out_grad_own = links.own_rows(factor)[:, None] * links.own_rows(cotangent_low).astype(wide)
    segments = jnp.stack([segment_ids(lengths, row_length) for lengths in episode_lengths])
    scaled_one, _ = norm_parts(hidden_low.astype(wide))
    scaled_one, branch_grad_low, segments, *own = links.round(
        lambda: attend_move.near()
        + combine_move.far()
        + attend_move.across("far")
        + expand_move.across("own"),
        [scaled_one, branch_grad_low, segments, *(move.held["own"] for move in later)],
    )
    for move, shard in zip(later, own):
        move.held["own"] = shard
    attend_states = links.round(
        lambda: combine_move.near()
        + expand_move.far()
        + attend_move.across("near")
        + combine_move.across("pair"),
        attend_states,
    )

    norm_values = jnp.concatenate(
        [
            part[first + shard_rows, : norm_rows * norm_columns].reshape(norm_rows, -1)
            for part, first in attend_move.parts()
        ],
        axis=1,
    ).astype(wide)
    normed_low = (scaled_one * norm_values[0] + norm_values[1]).astype(low_type)

    (normed_low,) = links.round(
        lambda: expand_move.near() + combine_move.across("near") + expand_move.across("far"),
        [normed_low],
    )
    attend_full = attend_move.full(shard_rows)
    projected = dot_low(normed_low, attend_full, "nn")
    mixed_low = attention(projected, segments)
    combine_full = combine_move.full(shard_rows)
    attended = ReduceTensor(links, dot_low(mixed_low, combine_full, "nt"))

    links.round(
        lambda: attended.first()
        + shrink_move.out("far0", shrink_move.half("own", 0), 2)
        + expand_move.across("near0", expand_move.half("near", 0)),
        [attended.partial],
    )
    hidden_own = links.own_rows(hidden_low).astype(wide)
    links.round(
        lambda: attended.second()
        + shrink_move.out("far1", shrink_move.half("own", 1), 2)
        + expand_move.across("near1", expand_move.half("near", 1))
    )
    residual = hidden_own + attended.total()
    scaled_two, inverse_two = norm_parts(residual)
    normed_two = GatherTensor(
        links, (scaled_two * norm_values[2] + norm_values[3]).astype(low_type)
    )
    (normed_two.own,) = links.round(
        lambda: normed_two.first()
        + shrink_move.out("near_own", shrink_move.held["own"], 1)
        + shrink_move.across("own"),
        [normed_two.own],
    )
    links.round(
        lambda: normed_two.second()
        + shrink_move.out("near_far", shrink_move.joined("far0", "far1"), 1)
        + shrink_move.across("far", shrink_move.joined("far0", "far1"))
    )
    links.round(lambda: shrink_move.across("near_far") + shrink_move.beside("own", "near_own"))
    normed_two_low = normed_two.full()
    expand_full = expand_move.full(shard_rows)
    activated_low, slope = matmul(
        normed_two_low,
        expand_full,
        "nn",
        gelu_parts,
        [low_type, wide],
    )

    def gradient_rows(left, right):
        return lambda first, last: dot_low(left, right, "tn", first, last)

    shrink_back = Reduce(links, shard_rows, gradient_rows(branch_grad_low, activated_low))

    slope, activated_low, *_ = links.round(
        shrink_back.first, [slope, activated_low, *shrink_back.away.values()]
    )
    shrink_full = shrink_move.full(half_rows)
    (expanded_grad_low,) = matmul(
        branch_grad_low,
        shrink_full,
        "nn",
        lambda made, before: (made * before,),
        [low_type],
        slope,
    )
    normed_two_back = ReduceTensor(links, dot_low(expanded_grad_low, expand_full, "nt"))

    normed_two_back.partial, expanded_grad_low, activated_low = links.round(
        lambda: normed_two_back.first() + shrink_back.second(1) + shrink_back.near(1),
        [normed_two_back.partial, expanded_grad_low, activated_low],
    )
    expand_back = Reduce(links, shard_rows, gradient_rows(normed_two_low, expanded_grad_low))
    links.round(
        lambda: normed_two_back.second() + shrink_back.second(0) + shrink_back.near(0),
        expand_back.terms(),
    )
    residual_from_norm, gain_two_grad, shift_two_grad = norm_back(
        normed_two_back.total(), scaled_two, inverse_two, norm_values[2]
    )
    residual_grad = out_grad_own + residual_from_norm
    attended_grad = GatherTensor(links, residual_grad.astype(low_type))

    attended_grad.own, activated_low = links.round(
        lambda: attended_grad.first() + expand_back.first(1) + shrink_back.far(1),
        [attended_grad.own, activated_low],
    )
    branch = ReduceTensor(links, dot_low(activated_low, shrink_full, "nt"))
    links.round(
        lambda: attended_grad.second()
        + branch.first()
        + expand_back.first(0)
        + shrink_back.far(0),
        [branch.partial],
    )
    attended_grad_low = attended_grad.full()
    mixed_grad = dot_low(attended_grad_low, combine_full, "nn")
    projected_grad = attention(projected, segments, mixed_grad)
    (projected_grad,) = links.round(
        lambda: branch.second() + expand_back.second() + expand_back.near(), [projected_grad]
    )
    combine_back = Reduce(links, shard_rows, gradient_rows(attended_grad_low, mixed_low), True)
    attend_back = Reduce(links, shard_rows, gradient_rows(normed_low, projected_grad))
    normed_one_back = ReduceTensor(links, dot_low(projected_grad, attend_full, "nt"))

    shrink_back.mine, *_ = links.round(
        lambda: normed_one_back.first() + combine_back.both() + expand_back.far(1),
        [shrink_back.mine, normed_one_back.partial, *attend_back.terms(), *combine_back.terms()],
    )
    output = GatherTensor(
        links,
        reorder_columns((residual + branch.total()).astype(low_type), links.from_own),
    )
    combine_back.split_both()
    (shrink_back.mine,) = links.round(
        lambda: normed_one_back.second()
        + attend_back.first()
        + combine_back.near()
        + expand_back.far(0),
        [shrink_back.mine],
    )
    shrink_sum = turned(shrink_back.total())
    scaled_own, inverse_own = norm_parts(hidden_own)
    hidden_from_norm, gain_one_grad, shift_one_grad = norm_back(
        normed_one_back.total(), scaled_own, inverse_own, norm_values[0]
    )
    input_own = reorder_columns((residual_grad + hidden_from_norm).astype(low_type), links.from_own)
    input_back = GatherTensor(links, input_own)
    input_back.own, output.own = links.round(
        lambda: attend_back.second()
        + attend_back.near()
        + input_back.first()[:-1]
        + combine_back.far(),
        [input_own, output.own],
    )
    output.now(output.first()[:-1])
    norm_terms = jnp.stack([gain_one_grad, shift_one_grad, gain_two_grad, shift_two_grad])

    (expand_back.mine, norm_terms) = links.round(
        lambda: input_back.first()[-1:] + attend_back.far(), [expand_back.mine, norm_terms]
    )
    input_back.now(input_back.second())
    output.now(output.first()[-1:])
    output.now(output.second())
    norm_grads = ReduceSmall(links, links.sum_tensor(norm_terms))
    for value, send, store, key in norm_grads.first():
        store[key] = send(value)
    expand_sum = expand_back.total()
    combine_sum = turned(combine_back.total())
    layer_output = output.full()
    input_gradient = input_back.full().astype(wide)
    (input_gradient, layer_output, norm_grads.split) = links.round(
        norm_grads.outward, [input_gradient, layer_output, norm_grads.split]
    )
    norm_sum = norm_grads.total()
    attend_new = adam_planes(
        attend_back.last_terms(),
        attend_states,
        matrix_rate,
        weight_decay,
    )
    kinds = (
        (
            combine_weights,
            combine_first,
            combine_second,
            combine_average,
            combine_sum,
            matrix_rate,
            weight_decay,
        ),
        (
            expand_weights,
            expand_first,
            expand_second,
            expand_average,
            expand_sum,
            matrix_rate,
            weight_decay,
        ),
        (
            shrink_weights,
            shrink_first,
            shrink_second,
            shrink_average,
            shrink_sum,
            matrix_rate,
            weight_decay,
        ),
        (
            layernorm_params,
            layernorm_first,
            layernorm_second,
            layernorm_average,
            norm_sum,
            norm_rate,
            0.0,
        ),
    )
    results = [layer_output, input_gradient, *(made.transpose(1, 0, 2) for made in attend_new)]
    for master, moment, square, average, gradient, rate_value, decay_value in kinds:
        master_new, moment_new, square_new = adam_update(
            master, moment, square, gradient, rate_value, decay_value
        )
        smooth_new = average_decay * average + (1.0 - average_decay) * master_new
        results.extend(
            [master_new, moment_new, square_new, smooth_new, master_new.astype(jnp.bfloat16)]
        )
    return tuple(results)


def solution(mesh):
    placed = (
        P("dp", None),
        P("dp", None),
        P("dp", None),
        P("dp"),
        P("dp"),
        P("dp", None, "tensor"),
        P("dp", None, "tensor"),
        P("dp", None, "tensor"),
        P("dp", None, "tensor"),
        P("tensor", "dp"),
        P("tensor", "dp"),
        P("tensor", "dp"),
        P("tensor", "dp"),
        P("dp", "tensor"),
        P("dp", "tensor"),
        P("dp", "tensor"),
        P("dp", "tensor"),
        P("tensor", "dp"),
        P("tensor", "dp"),
        P("tensor", "dp"),
        P("tensor", "dp"),
        P(None, "dp"),
        P(None, "dp"),
        P(None, "dp"),
        P(None, "dp"),
    )
    return jax.shard_map(
        functools.partial(shards, Links(mesh)),
        mesh=mesh,
        in_specs=placed,
        out_specs=(
            P("dp", None),
            P("dp", None),
            P("dp", None, "tensor"),
            P("dp", None, "tensor"),
            P("dp", None, "tensor"),
            P("dp", None, "tensor"),
            P("dp", None, "tensor"),
            P("tensor", "dp"),
            P("tensor", "dp"),
            P("tensor", "dp"),
            P("tensor", "dp"),
            P("tensor", "dp"),
            P("dp", "tensor"),
            P("dp", "tensor"),
            P("dp", "tensor"),
            P("dp", "tensor"),
            P("dp", "tensor"),
            P("tensor", "dp"),
            P("tensor", "dp"),
            P("tensor", "dp"),
            P("tensor", "dp"),
            P("tensor", "dp"),
            P(None, "dp"),
            P(None, "dp"),
            P(None, "dp"),
            P(None, "dp"),
            P(None, "dp"),
        ),
        check_vma=False,
    )
```

```python
import functools
import math

import jax
import jax.numpy as jnp
from jax import lax
from jax.experimental import pallas as pl
from jax.experimental.pallas import tpu as pltpu
from jax.sharding import PartitionSpec as P

HEAD_DIM = 128
STEP = 10


beta_first = 0.5
beta_second = 0.5
average_decay = 0.5
adam_epsilon = 1e-08
weight_decay = 0.1
matrix_rate = 0.02
norm_rate = 0.2
norm_epsilon = 1e-05
low_type = jnp.bfloat16
wide = jnp.float32
work_share = 0.1
kernel_memory = 21 * 1024 * 1024


def norm_parts(values):
    center = values - jnp.mean(values, axis=-1, keepdims=True)
    spread = jnp.mean(center * center, axis=-1, keepdims=True)
    inverse = lax.rsqrt(spread + norm_epsilon)
    return center * inverse, inverse


def norm_back(grad, scaled, inverse, gain_row):
    inner = grad * gain_row
    mean_inner = jnp.mean(inner, axis=-1, keepdims=True)
    mean_scaled = jnp.mean(inner * scaled, axis=-1, keepdims=True)
    result = inverse * (inner - mean_inner - scaled * mean_scaled)
    return result, jnp.sum(grad * scaled, axis=0), jnp.sum(grad, axis=0)


def gelu_parts(v):
    scale = math.sqrt(2.0 / math.pi)
    bend = jnp.tanh(scale * (v + 0.044715 * (v * v * v)))
    slope = 0.5 * (1.0 + bend) + 0.5 * v * (1.0 - bend * bend) * scale * (
        1.0 + 3.0 * 0.044715 * (v * v)
    )
    return 0.5 * v * (1.0 + bend), slope


def segment_ids(lengths_row, row_length):
    order = jnp.arange(lengths_row.shape[0], dtype=jnp.int32)
    earlier = order[None, :] <= order[:, None]
    bounds = jnp.sum(jnp.where(earlier, lengths_row[None, :], 0), axis=1)
    places = jnp.arange(row_length, dtype=jnp.int32)
    return jnp.sum((places[:, None] >= bounds[None, :]).astype(jnp.int32), axis=1)


def work(flops, size, exponents=0):
    return pl.CostEstimate(
        flops=int(flops * work_share), bytes_accessed=int(size * work_share), transcendentals=exponents
    )


def tile(size, most):
    return math.gcd(size, most)


product_dims = {
    "nn": (((1,), (0,)), ((), ())),
    "nt": (((1,), (1,)), ((), ())),
    "tn": (((0,), (0,)), ((), ())),
}


def product(left, right, kind):
    return lax.dot_general(left, right, product_dims[kind], preferred_element_type=wide)


class Pieces:
    def __init__(self, parts, rows):
        self.rows = rows
        self.arrays, self.places = [], []
        for array, first in parts:
            if not self.arrays or self.arrays[-1] is not array:
                self.arrays.append(array)
            self.places.append((len(self.arrays) - 1, first))
        self.shape = (rows * len(self.places), self.arrays[0].shape[1])

    def read(self, refs):
        start = 0
        while start < len(self.places):
            which, first = self.places[start]
            last = start + 1
            while (
                last < len(self.places)
                and self.places[last] == (which, first + (last - start) * self.rows)
            ):
                last += 1
            count = (last - start) * self.rows
            yield start * self.rows, count, refs[which][first : first + count, :]
            start = last


def matmul(left, right, kind, body, kinds_out, beside=None, first=0, last=None, most=(512, 1024)):
    depth = left.shape[0 if kind == "tn" else 1]
    rows = (last or left.shape[1 if kind == "tn" else 0]) - first
    columns = right.shape[0 if kind == "nt" else 1]
    pieces = right if isinstance(right, Pieces) else None
    rights = pieces.arrays if pieces else [right]
    down, along = tile(math.gcd(rows, first), most[0]), tile(columns, most[1])
    if pieces and kind == "nt":
        down, along = tile(rows, 256), columns
    skip = first // down
    if kind == "tn":
        left_spec = pl.BlockSpec((depth, down), lambda j, i: (0, i + skip))
    else:
        left_spec = pl.BlockSpec((down, depth), lambda j, i: (i + skip, 0))
    if kind == "nt":
        height = [x.shape[0] if pieces else along for x in rights]
        held = pl.Buffered(1) if pieces else None
        right_specs = [
            pl.BlockSpec((x, depth), lambda j, i: (j, 0), pipeline_mode=held) for x in height
        ]
    else:
        right_specs = [pl.BlockSpec((x.shape[0], along), lambda j, i: (0, j)) for x in rights]
    out_spec = pl.BlockSpec((down, along), lambda j, i: (i, j))
    more = [] if beside is None else [beside]

    def kernel(left_ref, *refs):
        rights_in, refs = refs[: len(rights)], refs[len(rights) :]
        values = [ref[...] for ref in refs[: len(more)]]
        outs = refs[len(more) :]
        if pieces and kind == "nt":
            for start, count, piece in pieces.read(rights_in):
                made = body(product(left_ref[...], piece, kind), *values)
                for ref, value in zip(outs, made):
                    ref[:, start : start + count] = value.astype(ref.dtype)
            return
        if pieces:
            total = sum(
                product(left_ref[:, start : start + count], piece, kind)
                for start, count, piece in pieces.read(rights_in)
            )
        else:
            total = product(left_ref[...], rights_in[0][...], kind)
        for ref, value in zip(outs, body(total, *values)):
            ref[...] = value.astype(ref.dtype)

    shapes = [jax.ShapeDtypeStruct((rows, columns), kind_out) for kind_out in kinds_out]
    size = sum(x.size * x.dtype.itemsize for x in (left, *rights, *more, *shapes))
    return pl.pallas_call(
        kernel,
        out_shape=shapes,
        grid=(columns // along, rows // down),
        in_specs=[left_spec] + right_specs + [out_spec] * len(more),
        out_specs=[out_spec] * len(shapes),
        compiler_params=pltpu.CompilerParams(vmem_limit_bytes=kernel_memory),
        cost_estimate=work(2 * rows * columns * depth, size),
    )(left, *rights, *more)


def dot_low(left, right, kind, first=0, last=None):
    return matmul(left, right, kind, lambda made: (made,), [low_type], first=first, last=last)[0]


def block_softmax(queries, keys_seen, segment_down, segment_along, first_row):
    scores = product(queries, keys_seen, "nt") * HEAD_DIM ** (-0.5)
    places = lax.broadcasted_iota(jnp.int32, scores.shape, 0) + first_row
    key_places = lax.broadcasted_iota(jnp.int32, scores.shape, 1)
    allowed = (segment_down == segment_along) & (key_places <= places)
    masked = jnp.where(allowed, scores, -1e30)
    exponent = jnp.exp(masked - jnp.max(masked, axis=-1, keepdims=True))
    return exponent * (1.0 / jnp.sum(exponent, axis=-1, keepdims=True))


def attend_kernel(query_ref, key_ref, value_ref, down_ref, along_ref, out_ref):
    row_length = query_ref.shape[0]
    block = tile(row_length, 256)
    for first in range(0, row_length, block):
        last = first + block
        soft = block_softmax(
            query_ref[first:last, :],
            key_ref[:last, :],
            down_ref[first:last, :],
            along_ref[:, :last],
            first,
        )
        made = product(soft.astype(low_type), value_ref[:last, :], "nn")
        out_ref[first:last, :] = made.astype(low_type)


def attend_back_kernel(
    query_ref, key_ref, value_ref, grad_ref, down_ref, along_ref, out_ref, key_sum, value_sum
):
    row_length = query_ref.shape[0]
    block = tile(row_length, 256)
    scale = HEAD_DIM ** (-0.5)
    kind = pl.program_id(2)

    @pl.when(kind == 0)
    def _():
        key_sum[...] = jnp.zeros_like(key_sum)
        value_sum[...] = jnp.zeros_like(value_sum)
        for first in range(0, row_length, block):
            last = first + block
            queries, grads = query_ref[first:last, :], grad_ref[first:last, :]
            soft = block_softmax(
                queries, key_ref[:last, :], down_ref[first:last, :], along_ref[:, :last], first
            )
            value_sum[:last, :] += product(soft.astype(low_type), grads, "tn")
            prob_grad = product(grads, value_ref[:last, :], "nt")
            row_delta = jnp.sum(prob_grad * soft, axis=-1, keepdims=True)
            score_grad = (soft * (prob_grad - row_delta)).astype(low_type)
            made = product(score_grad, key_ref[:last, :], "nn") * scale
            out_ref[first:last, :] = made.astype(low_type)
            key_sum[:last, :] += product(score_grad, queries, "tn")

    @pl.when(kind == 1)
    def _():
        out_ref[...] = (key_sum[...] * scale).astype(low_type)

    @pl.when(kind == 2)
    def _():
        out_ref[...] = value_sum[...].astype(low_type)


def attention(projected, segments, grads=None):
    row_count, row_length = segments.shape
    tokens, columns = projected.shape
    head_count = columns // (3 * HEAD_DIM)
    shape = (row_length, HEAD_DIM)
    down = segments.reshape(tokens, 1)
    along = segments.reshape(row_count, 1, row_length)

    def spec(kind):
        return pl.BlockSpec(shape, lambda r, h, *_: (r, kind * head_count + h))

    in_specs = [spec(0), spec(1), spec(2)] + ([] if grads is None else [spec(0)])
    in_specs += [
        pl.BlockSpec((row_length, 1), lambda r, h, *_: (r, 0)),
        pl.BlockSpec((None, 1, row_length), lambda r, h, *_: (r, 0, 0)),
    ]
    square = 2 * row_count * head_count * row_length * row_length * HEAD_DIM
    params = pltpu.CompilerParams(vmem_limit_bytes=kernel_memory)
    if grads is None:
        return pl.pallas_call(
            attend_kernel,
            out_shape=jax.ShapeDtypeStruct((tokens, head_count * HEAD_DIM), low_type),
            grid=(row_count, head_count),
            in_specs=in_specs,
            out_specs=spec(0),
            compiler_params=params,
            cost_estimate=work(2 * square, projected.size * 4),
        )(projected, projected, projected, down, along)
    return pl.pallas_call(
        attend_back_kernel,
        out_shape=jax.ShapeDtypeStruct(projected.shape, low_type),
        grid=(row_count, head_count, 3),
        in_specs=in_specs,
        out_specs=pl.BlockSpec(shape, lambda r, h, kind: (r, kind * head_count + h)),
        scratch_shapes=[pltpu.VMEM(shape, wide), pltpu.VMEM(shape, wide)],
        compiler_params=params,
        cost_estimate=work(5 * square, projected.size * 6),
    )(projected, projected, projected, grads, down, along)


def after(value, *earlier):
    return lax.optimization_barrier((value, *earlier))[0] if earlier else value


def copy_block(order_ref, in_ref, out_ref):
    out_ref[...] = in_ref[...]


def reorder_columns(values, order):
    rows, width = values.shape
    count = order.shape[0]
    columns = width // count
    if columns % 128:
        blocks = [
            lax.dynamic_slice_in_dim(values, order[i] * columns, columns, 1) for i in range(count)
        ]
        return jnp.concatenate(blocks, axis=1)
    return pl.pallas_call(
        copy_block,
        out_shape=jax.ShapeDtypeStruct(values.shape, values.dtype),
        grid_spec=pltpu.PrefetchScalarGridSpec(
            num_scalar_prefetch=1,
            grid=(count,),
            in_specs=[pl.BlockSpec((rows, columns), lambda i, order_ref: (0, order_ref[i]))],
            out_specs=pl.BlockSpec((rows, columns), lambda i, order_ref: (0, i)),
        ),
        cost_estimate=pl.CostEstimate(
            flops=0, bytes_accessed=2 * values.size * values.dtype.itemsize, transcendentals=0
        ),
    )(order, values)


def turn_block(in_ref, out_ref):
    out_ref[...] = in_ref[...].T


def turned(values):
    rows, width = values.shape
    columns = min(512, width)
    return pl.pallas_call(
        turn_block,
        out_shape=jax.ShapeDtypeStruct((width, rows), values.dtype),
        grid=(width // columns,),
        in_specs=[pl.BlockSpec((rows, columns), lambda i: (0, i))],
        out_specs=pl.BlockSpec((columns, rows), lambda i: (i, 0)),
        cost_estimate=pl.CostEstimate(
            flops=0, bytes_accessed=2 * values.size * values.dtype.itemsize, transcendentals=0
        ),
    )(values)


def adam_kernel(rate_value, decay_value, terms, *refs):
    gradient = sum(ref[...].astype(wide) for ref in refs[:terms])
    states, outs = refs[terms : terms + 4], refs[terms + 4 :]
    master, moment, square, average = (ref[...] for ref in states)
    made = adam_update(master, moment, square, gradient, rate_value, decay_value)
    smooth = average_decay * average + (1.0 - average_decay) * made[0]
    for ref, value in zip(outs, (*made, smooth, made[0])):
        ref[...] = value.astype(ref.dtype)


def adam_planes(terms, states, rate_value, decay_value):
    planes, rows, width = states[0].shape
    block = tile(rows, 128)
    flat = pl.BlockSpec((block, width), lambda j, i: (i, j))
    deep = pl.BlockSpec((None, block, width), lambda j, i: (j, i, 0))
    size = sum(x.size * x.dtype.itemsize for x in terms) + 34 * states[0].size
    kinds = [wide] * 4 + [low_type]
    return pl.pallas_call(
        functools.partial(adam_kernel, rate_value, decay_value, len(terms)),
        out_shape=[jax.ShapeDtypeStruct(states[0].shape, kind) for kind in kinds],
        grid=(planes, rows // block),
        in_specs=[flat] * len(terms) + [deep] * 4,
        out_specs=[deep] * 5,
        compiler_params=pltpu.CompilerParams(vmem_limit_bytes=kernel_memory),
        cost_estimate=pl.CostEstimate(flops=0, bytes_accessed=size, transcendentals=0),
    )(*terms, *states)


class Links:
    outer_order = (0, 2, 1, 3)

    def __init__(self, mesh):
        self.count = mesh.shape["dp"]
        self.outer = len(self.outer_order)
        self.inner = self.count // self.outer
        self.group = mesh.shape["tensor"]
        self.cores = 2
        self.chips = self.group // self.cores

    def place(self):
        index = lax.axis_index("dp")
        out_at, in_at = lax.div(index, self.inner), lax.rem(index, self.inner)
        index = lax.axis_index("tensor")
        self.chip_at, self.core_at = lax.div(index, self.cores), lax.rem(index, self.cores)
        order = jnp.asarray(self.outer_order, jnp.int32)
        inner = jnp.arange(self.inner, dtype=jnp.int32)
        self.to_own = (
            (out_at ^ order)[None, :] * self.inner + (in_at ^ inner)[:, None]
        ).reshape(-1)
        outer = jnp.arange(self.outer, dtype=jnp.int32) ^ out_at
        placed = (outer & 1) * 2 + (outer >> 1)
        self.from_own = ((inner ^ in_at)[None, :] * self.outer + placed[:, None]).reshape(-1)
        self.running = []

    def flip(self, value, over_outer, over_inner):
        pairs = []
        for a in range(self.outer):
            for b in range(self.inner):
                to = (a ^ over_outer) * self.inner + (b ^ over_inner)
                pairs.append((a * self.inner + b, to))
        return lax.ppermute(value, "dp", pairs)

    def across(self, over_outer, over_inner):
        return lambda value: self.flip(value, over_outer, over_inner)

    def round(self, make_moves, carried=()):
        held = [store[key] for store, key in self.running]
        held = lax.optimization_barrier((*held, *carried))
        for (store, key), value in zip(self.running, held):
            store[key] = value
        moves = make_moves()
        for value, send, store, key in moves:
            store[key] = send(after(value, *held))
        count = len(self.running)
        self.running = [(store, key) for *_, store, key in moves]
        return held[count:]

    def turn(self, value, over_chips, over_cores):
        pairs = []
        for a in range(self.chips):
            for b in range(self.cores):
                to = (a + over_chips) % self.chips * self.cores + (b + over_cores) % self.cores
                pairs.append((a * self.cores + b, to))
        return lax.ppermute(value, "tensor", pairs)

    def sum_tensor(self, total):
        for parts, step in ((self.cores, (0, 1)), (self.chips, (1, 0))):
            moving = total
            for _ in range(parts - 1):
                moving = self.turn(moving, *step)
                total = total + moving
        return total

    def along(self, over_chips, over_cores):
        return lambda value: self.turn(value, over_chips, over_cores)

    def own_rows(self, value):
        rows = value.shape[0] // self.group
        return lax.dynamic_slice_in_dim(
            value, (self.core_at * self.chips + self.chip_at) * rows, rows, 0
        )


class Gather:
    here = ("own", "far", "far0", "far1", "near", "near_own", "near_far")
    there = ("pair", "own", "far", "near", "near0", "near1", "near_own", "near_far")

    def __init__(self, links, shard, step=None):
        self.links = links
        self.step = step or shard.shape[0]
        self.held = {"own": shard}

    def out(self, name, value, distance):
        return [(value, self.links.across(distance, 0), self.held, name)]

    def joined(self, *names):
        return jnp.concatenate([self.held[name] for name in names], axis=0)

    def far(self):
        return self.out("far", self.held["own"], 2)

    def near(self):
        return self.out("near", self.joined("own", "far"), 1)

    def across(self, name, value=None):
        if value is None:
            value = self.joined("own", "far") if name == "pair" else self.held[name]
        partners = range(1, self.links.inner)
        return [(value, self.links.across(0, j), self.held, (name, j)) for j in partners]

    def beside(self, name, result):
        send = self.links.across(1, 0)
        partners = range(1, self.links.inner)
        return [(self.held[name, j], send, self.held, (result, j)) for j in partners]

    def half(self, name, part):
        value = self.held[name]
        rows = value.shape[0] // 2
        return value[part * rows : (part + 1) * rows]

    def parts(self):
        names = [name for name in self.here if name in self.held]
        for j in range(1, self.links.inner):
            names += [(name, j) for name in self.there if (name, j) in self.held]
        for name in names:
            for first in range(0, self.held[name].shape[0], self.step):
                yield self.held[name], first

    def full(self, rows):
        return Pieces(self.parts(), rows)


class Reduce:
    def __init__(self, links, rows, make, joint=False):
        self.links, self.rows = links, rows
        size = 2 * rows
        starts = [j * 2 * size for j in range(links.inner)]
        self.whole = {}
        if joint:
            self.whole = {j: make(starts[j], starts[j] + 2 * size) for j in range(1, links.inner)}
            self.away = {j: made[size:] for j, made in self.whole.items()}
            self.close = {j: made[:size] for j, made in self.whole.items()}
        else:
            ends = [start + 2 * size for start in starts]
            self.away = {j: make(starts[j] + size, ends[j]) for j in range(1, links.inner)}
            self.close = {j: make(starts[j], starts[j] + size) for j in range(1, links.inner)}
        self.mine = make(0, 2 * size)
        self.size = size
        self.held = {}

    def terms(self):
        if self.whole:
            return [*self.whole.values(), self.mine]
        return [*self.away.values(), *self.close.values(), self.mine]

    def span(self, part, size):
        return (0, size) if part is None else (part * size // 2, (part + 1) * size // 2)

    def move(self, name, j, part, value, send):
        key = (name, j) if part is None else (name, j, part)
        return (value, send, self.held, key)

    def got(self, name, j, first, last, size):
        if (name, j) in self.held:
            return self.held[name, j][first:last]
        if last - first > size // 2:
            halves = [self.held[name, j, 0], self.held[name, j, 1]]
            return jnp.concatenate(halves, axis=0)[first:last]
        part = first // (size // 2)
        skip = part * (size // 2)
        return self.held[name, j, part][first - skip : last - skip]

    def inward(self, name, terms, part):
        first, last = self.span(part, self.size)
        return [
            self.move(name, j, part, term[first:last], self.links.across(0, j))
            for j, term in terms.items()
        ]

    def first(self, part=None):
        return self.inward("away", self.away, part)

    def second(self, part=None):
        return self.inward("close", self.close, part)

    def both(self):
        return [
            (made, self.links.across(0, j), self.held, ("both", j))
            for j, made in self.whole.items()
        ]

    def split_both(self):
        for j in self.away:
            self.held["close", j] = self.held["both", j][: self.size]
            self.held["away", j] = self.held["both", j][self.size :]

    def near(self, part=None):
        first, last = self.span(part, self.size)
        sums = self.mine[self.size + first : self.size + last].astype(wide)
        for j in self.away:
            sums = sums + self.got("away", j, first, last, self.size).astype(wide)
        return [self.move("near", 0, part, sums.astype(low_type), self.links.across(1, 0))]

    def sums(self, first, last):
        sums = self.mine[first:last].astype(wide)
        sums = sums + self.got("near", 0, first, last, self.size).astype(wide)
        for j in self.close:
            sums = sums + self.got("close", j, first, last, self.size).astype(wide)
        return sums

    def far(self, part=None):
        first, last = self.span(part, self.rows)
        sums = self.sums(self.rows + first, self.rows + last).astype(low_type)
        return [self.move("far", 0, part, sums, self.links.across(2, 0))]

    def last_terms(self):
        near = self.held["near", 0]
        return [self.mine, near, *(self.held["close", j] for j in self.close), self.held["far", 0]]

    def total(self):
        parts = [None] if ("far", 0) in self.held else [0, 1]
        spans = [self.span(part, self.rows) for part in parts]
        sums = [
            self.sums(*span) + self.got("far", 0, *span, self.rows).astype(wide) for span in spans
        ]
        return jnp.concatenate(sums, axis=0)


class ReduceTensor:
    def __init__(self, links, partial):
        self.links, self.partial = links, partial
        self.held = {}

    def part(self, over_chips, over_cores):
        links = self.links
        rows = self.partial.shape[0] // links.group
        chip = lax.rem(links.chip_at + over_chips, links.chips)
        core = lax.rem(links.core_at + over_cores, links.cores)
        return lax.dynamic_slice_in_dim(self.partial, (core * links.chips + chip) * rows, rows, 0)

    def first(self):
        return [
            (self.part(j, 1), self.links.along(0, 1), self.held, ("half", j))
            for j in reversed(range(self.links.chips))
        ]

    def sums(self, j):
        return self.part(j, 0).astype(wide) + self.held["half", j].astype(wide)

    def second(self):
        return [
            (self.sums(j).astype(low_type), self.links.along(j, 0), self.held, j)
            for j in range(1, self.links.chips)
        ]

    def total(self):
        return self.sums(0) + sum(
            self.held[j].astype(wide) for j in range(1, self.links.chips)
        )


class GatherTensor:
    def __init__(self, links, own):
        self.links, self.own = links, own
        self.held = {}

    def first(self):
        chips = range(1, self.links.chips)
        return [(self.own, self.links.along(j, 0), self.held, (j, 0)) for j in chips] + [
            (self.own, self.links.along(0, 1), self.held, (0, 1))
        ]

    def second(self):
        chips = range(1, self.links.chips)
        return [
            (self.held[j, 0], self.links.along(0, 1), self.held, (j, 1)) for j in chips
        ]

    def now(self, moves):
        for value, send, store, key in moves:
            store[key] = send(value)

    def full(self):
        links = self.links
        rows = self.own.shape[0]
        full = jnp.zeros((links.group * rows,) + self.own.shape[1:], self.own.dtype)
        for (j, k), part in {(0, 0): self.own, **self.held}.items():
            chip = lax.rem(links.chip_at + links.chips - j, links.chips)
            core = lax.rem(links.core_at + k, links.cores)
            full = lax.dynamic_update_slice_in_dim(
                full, part, (core * links.chips + chip) * rows, 0
            )
        return full


class ReduceSmall:
    def __init__(self, links, partial):
        self.links = links
        self.split = partial.reshape(partial.shape[0], links.inner, links.outer, -1)
        self.held = {}

    def first(self):
        return [
            (self.split[:, j], self.links.across(0, j), self.held, j + 2)
            for j in range(1, self.links.inner)
        ]

    def outward(self):
        self.sums = self.split[:, 0] + sum(
            self.held[j + 2] for j in range(1, self.links.inner)
        )
        order = self.links.outer_order
        return [
            (self.sums[:, i], self.links.across(order[i], 0), self.held, -i)
            for i in range(1, len(order))
        ]

    def total(self):
        return self.sums[:, 0] + sum(self.held[-i] for i in range(1, self.links.outer))


def adam_update(master, moment, square, gradient, rate_value, decay_value):
    moment_new = beta_first * moment + (1.0 - beta_first) * gradient
    square_new = beta_second * square + (1.0 - beta_second) * gradient * gradient
    fix_first = 1.0 - beta_first**STEP
    fix_second = 1.0 - beta_second**STEP
    direction = moment_new / fix_first / (jnp.sqrt(square_new / fix_second) + adam_epsilon)
    master_new = master - rate_value * (direction + decay_value * master)
    return (master_new, moment_new, square_new)


def shards(
    links,
    hidden_in,
    out_cotangent,
    episode_lengths,
    self_generated,
    loss_numerator,
    attend_weights,
    attend_first,
    attend_second,
    attend_average,
    combine_weights,
    combine_first,
    combine_second,
    combine_average,
    expand_weights,
    expand_first,
    expand_second,
    expand_average,
    shrink_weights,
    shrink_first,
    shrink_second,
    shrink_average,
    layernorm_params,
    layernorm_first,
    layernorm_second,
    layernorm_average,
):
    links.place()
    local_tokens, width = hidden_in.shape
    row_count = episode_lengths.shape[0]
    row_length = local_tokens // row_count
    shard_rows, kinds_count, local_width = attend_weights.shape

    attend_states = [
        state.transpose(1, 0, 2)
        for state in (attend_weights, attend_first, attend_second, attend_average)
    ]
    attend_low = attend_weights.astype(low_type).reshape(shard_rows, kinds_count * local_width)
    combine_low = combine_weights.astype(low_type).T
    expand_low = expand_weights.astype(low_type)
    shrink_low = shrink_weights.astype(low_type).T
    norm_rows, norm_columns = layernorm_params.shape
    norm_low = layernorm_params.astype(low_type).reshape(1, -1)
    spare = attend_low.shape[1] - norm_low.shape[1]
    norm_low = jnp.pad(norm_low, ((0, 15), (0, spare)))
    attend_move = Gather(links, jnp.concatenate([attend_low, norm_low], axis=0))
    combine_move, expand_move = Gather(links, combine_low), Gather(links, expand_low)
    half_rows = shard_rows // 2
    shrink_move = Gather(links, shrink_low, half_rows)
    later = (combine_move, shrink_move)
    links.round(lambda: attend_move.far() + attend_move.across("own"))
    hidden_low = reorder_columns(hidden_in, links.to_own)
    cotangent_low = reorder_columns(out_cotangent, links.to_own)
    factor = loss_numerator.astype(wide) / (4.0 * (1.0 + self_generated.astype(wide)))
    branch_grad_low = (factor[:, None] * cotangent_low.astype(wide)).astype(low_type)
    out_grad_own = links.own_rows(factor)[:, None] * links.own_rows(cotangent_low).astype(wide)
    segments = jnp.stack([segment_ids(lengths, row_length) for lengths in episode_lengths])
    scaled_one, _ = norm_parts(hidden_low.astype(wide))
    scaled_one, branch_grad_low, segments, *own = links.round(
        lambda: attend_move.near()
        + combine_move.far()
        + attend_move.across("far")
        + expand_move.across("own"),
        [scaled_one, branch_grad_low, segments, *(move.held["own"] for move in later)],
    )
    for move, shard in zip(later, own):
        move.held["own"] = shard
    attend_states = links.round(
        lambda: combine_move.near()
        + expand_move.far()
        + attend_move.across("near")
        + combine_move.across("pair"),
        attend_states,
    )

    norm_values = jnp.concatenate(
        [
            part[first + shard_rows, : norm_rows * norm_columns].reshape(norm_rows, -1)
            for part, first in attend_move.parts()
        ],
        axis=1,
    ).astype(wide)
    normed_low = (scaled_one * norm_values[0] + norm_values[1]).astype(low_type)

    (normed_low,) = links.round(
        lambda: expand_move.near() + combine_move.across("near") + expand_move.across("far"),
        [normed_low],
    )
    attend_full = attend_move.full(shard_rows)
    projected = dot_low(normed_low, attend_full, "nn")
    mixed_low = attention(projected, segments)
    combine_full = combine_move.full(shard_rows)
    attended = ReduceTensor(links, dot_low(mixed_low, combine_full, "nt"))

    links.round(
        lambda: attended.first()
        + shrink_move.out("far0", shrink_move.half("own", 0), 2)
        + expand_move.across("near0", expand_move.half("near", 0)),
        [attended.partial],
    )
    hidden_own = links.own_rows(hidden_low).astype(wide)
    links.round(
        lambda: attended.second()
        + shrink_move.out("far1", shrink_move.half("own", 1), 2)
        + expand_move.across("near1", expand_move.half("near", 1))
    )
    residual = hidden_own + attended.total()
    scaled_two, inverse_two = norm_parts(residual)
    normed_two = GatherTensor(
        links, (scaled_two * norm_values[2] + norm_values[3]).astype(low_type)
    )
    (normed_two.own,) = links.round(
        lambda: normed_two.first()
        + shrink_move.out("near_own", shrink_move.held["own"], 1)
        + shrink_move.across("own"),
        [normed_two.own],
    )
    links.round(
        lambda: normed_two.second()
        + shrink_move.out("near_far", shrink_move.joined("far0", "far1"), 1)
        + shrink_move.across("far", shrink_move.joined("far0", "far1"))
    )
    links.round(lambda: shrink_move.across("near_far") + shrink_move.beside("own", "near_own"))
    normed_two_low = normed_two.full()
    expand_full = expand_move.full(shard_rows)
    activated_low, slope = matmul(
        normed_two_low,
        expand_full,
        "nn",
        gelu_parts,
        [low_type, wide],
    )

    def gradient_rows(left, right):
        return lambda first, last: dot_low(left, right, "tn", first, last)

    shrink_back = Reduce(links, shard_rows, gradient_rows(branch_grad_low, activated_low))

    slope, activated_low, *_ = links.round(
        shrink_back.first, [slope, activated_low, *shrink_back.away.values()]
    )
    shrink_full = shrink_move.full(half_rows)
    (expanded_grad_low,) = matmul(
        branch_grad_low,
        shrink_full,
        "nn",
        lambda made, before: (made * before,),
        [low_type],
        slope,
    )
    normed_two_back = ReduceTensor(links, dot_low(expanded_grad_low, expand_full, "nt"))

    normed_two_back.partial, expanded_grad_low, activated_low = links.round(
        lambda: normed_two_back.first() + shrink_back.second(1) + shrink_back.near(1),
        [normed_two_back.partial, expanded_grad_low, activated_low],
    )
    expand_back = Reduce(links, shard_rows, gradient_rows(normed_two_low, expanded_grad_low))
    links.round(
        lambda: normed_two_back.second() + shrink_back.second(0) + shrink_back.near(0),
        expand_back.terms(),
    )
    residual_from_norm, gain_two_grad, shift_two_grad = norm_back(
        normed_two_back.total(), scaled_two, inverse_two, norm_values[2]
    )
    residual_grad = out_grad_own + residual_from_norm
    attended_grad = GatherTensor(links, residual_grad.astype(low_type))

    attended_grad.own, activated_low = links.round(
        lambda: attended_grad.first() + expand_back.first(1) + shrink_back.far(1),
        [attended_grad.own, activated_low],
    )
    branch = ReduceTensor(links, dot_low(activated_low, shrink_full, "nt"))
    links.round(
        lambda: attended_grad.second()
        + branch.first()
        + expand_back.first(0)
        + shrink_back.far(0),
        [branch.partial],
    )
    attended_grad_low = attended_grad.full()
    mixed_grad = dot_low(attended_grad_low, combine_full, "nn")
    projected_grad = attention(projected, segments, mixed_grad)
    (projected_grad,) = links.round(
        lambda: branch.second() + expand_back.second() + expand_back.near(), [projected_grad]
    )
    combine_back = Reduce(links, shard_rows, gradient_rows(attended_grad_low, mixed_low), True)
    attend_back = Reduce(links, shard_rows, gradient_rows(normed_low, projected_grad))
    normed_one_back = ReduceTensor(links, dot_low(projected_grad, attend_full, "nt"))

    shrink_back.mine, *_ = links.round(
        lambda: normed_one_back.first() + combine_back.both() + expand_back.far(1),
        [shrink_back.mine, normed_one_back.partial, *attend_back.terms(), *combine_back.terms()],
    )
    output = GatherTensor(
        links,
        reorder_columns((residual + branch.total()).astype(low_type), links.from_own),
    )
    combine_back.split_both()
    (shrink_back.mine,) = links.round(
        lambda: normed_one_back.second()
        + attend_back.first()
        + combine_back.near()
        + expand_back.far(0),
        [shrink_back.mine],
    )
    shrink_sum = turned(shrink_back.total())
    scaled_own, inverse_own = norm_parts(hidden_own)
    hidden_from_norm, gain_one_grad, shift_one_grad = norm_back(
        normed_one_back.total(), scaled_own, inverse_own, norm_values[0]
    )
    input_own = reorder_columns((residual_grad + hidden_from_norm).astype(low_type), links.from_own)
    input_back = GatherTensor(links, input_own)
    input_back.own, output.own = links.round(
        lambda: attend_back.second()
        + attend_back.near()
        + input_back.first()[:-1]
        + combine_back.far(),
        [input_own, output.own],
    )
    output.now(output.first()[:-1])
    norm_terms = jnp.stack([gain_one_grad, shift_one_grad, gain_two_grad, shift_two_grad])

    (expand_back.mine, norm_terms) = links.round(
        lambda: input_back.first()[-1:] + attend_back.far(), [expand_back.mine, norm_terms]
    )
    input_back.now(input_back.second())
    output.now(output.first()[-1:])
    output.now(output.second())
    norm_grads = ReduceSmall(links, links.sum_tensor(norm_terms))
    for value, send, store, key in norm_grads.first():
        store[key] = send(value)
    expand_sum = expand_back.total()
    combine_sum = turned(combine_back.total())
    layer_output = output.full()
    input_gradient = input_back.full().astype(wide)
    (input_gradient, layer_output, norm_grads.split) = links.round(
        norm_grads.outward, [input_gradient, layer_output, norm_grads.split]
    )
    norm_sum = norm_grads.total()
    attend_new = adam_planes(
        attend_back.last_terms(),
        attend_states,
        matrix_rate,
        weight_decay,
    )
    kinds = (
        (
            combine_weights,
            combine_first,
            combine_second,
            combine_average,
            combine_sum,
            matrix_rate,
            weight_decay,
        ),
        (
            expand_weights,
            expand_first,
            expand_second,
            expand_average,
            expand_sum,
            matrix_rate,
            weight_decay,
        ),
        (
            shrink_weights,
            shrink_first,
            shrink_second,
            shrink_average,
            shrink_sum,
            matrix_rate,
            weight_decay,
        ),
        (
            layernorm_params,
            layernorm_first,
            layernorm_second,
            layernorm_average,
            norm_sum,
            norm_rate,
            0.0,
        ),
    )
    results = [layer_output, input_gradient, *(made.transpose(1, 0, 2) for made in attend_new)]
    for master, moment, square, average, gradient, rate_value, decay_value in kinds:
        master_new, moment_new, square_new = adam_update(
            master, moment, square, gradient, rate_value, decay_value
        )
        smooth_new = average_decay * average + (1.0 - average_decay) * master_new
        results.extend(
            [master_new, moment_new, square_new, smooth_new, master_new.astype(jnp.bfloat16)]
        )
    return tuple(results)


def solution(mesh):
    placed = (
        P("dp", None),
        P("dp", None),
        P("dp", None),
        P("dp"),
        P("dp"),
        P("dp", None, "tensor"),
        P("dp", None, "tensor"),
        P("dp", None, "tensor"),
        P("dp", None, "tensor"),
        P("tensor", "dp"),
        P("tensor", "dp"),
        P("tensor", "dp"),
        P("tensor", "dp"),
        P("dp", "tensor"),
        P("dp", "tensor"),
        P("dp", "tensor"),
        P("dp", "tensor"),
        P("tensor", "dp"),
        P("tensor", "dp"),
        P("tensor", "dp"),
        P("tensor", "dp"),
        P(None, "dp"),
        P(None, "dp"),
        P(None, "dp"),
        P(None, "dp"),
    )
    return jax.shard_map(
        functools.partial(shards, Links(mesh)),
        mesh=mesh,
        in_specs=placed,
        out_specs=(
            P("dp", None),
            P("dp", None),
            P("dp", None, "tensor"),
            P("dp", None, "tensor"),
            P("dp", None, "tensor"),
            P("dp", None, "tensor"),
            P("dp", None, "tensor"),
            P("tensor", "dp"),
            P("tensor", "dp"),
            P("tensor", "dp"),
            P("tensor", "dp"),
            P("tensor", "dp"),
            P("dp", "tensor"),
            P("dp", "tensor"),
            P("dp", "tensor"),
            P("dp", "tensor"),
            P("dp", "tensor"),
            P("tensor", "dp"),
            P("tensor", "dp"),
            P("tensor", "dp"),
            P("tensor", "dp"),
            P("tensor", "dp"),
            P(None, "dp"),
            P(None, "dp"),
            P(None, "dp"),
            P(None, "dp"),
            P(None, "dp"),
        ),
        check_vma=False,
    )
```
